256 devices in a mesh: mesh: 2 (over core), vocab: 32 (over y, z), dp: 4 (over x).
Axes of the slice: x: 4, y: 4, z: 8, core: 2. Of those that a mesh axis runs over, the one named last changes fastest.
Arguments:
- teacher_hidden: bfloat16 [512, 5120], P(('vocab', 'dp')), may hold values from -1024 to 1024
- teacher_head: bfloat16 [5120, 81920], P(None, ('vocab', 'dp')), may hold values from -2 to 2
- student_hidden: bfloat16 [512, 3584], P(('vocab', 'dp')), may hold values from -1024 to 1024
- student_head: bfloat16 [3584, 640, 128], P(None, None, ('vocab', 'dp')), may hold values from -2 to 2
- tiles: int32 [512, 128], replicated, may hold values from 0 to 639, as said below
Outputs:
- hidden_grad: bfloat16 [512, 3584], P(('mesh', 'vocab', 'dp'))
The draws below stay inside these ranges and needn't reach their ends.
Inputs may be any that keep to these rules, and one draw needn't show every extreme that they name: Each row names 128 distinct tiles, at most 2 of them among tiles k * 5 to (k + 1) * 5 - 1 for any k; in every draw some such block holds 2 tiles of every row, so that it holds 1024 named (row, tile) pairs.
All inputs are finite; a program needn't handle non-finite values.
Results may differ from the reference program's by a relative error of at most 0.0048.
Values may be sent and summed in bfloat16 or wider, within the bound.
No kernel may reach another device: no remote copies, remote signals or barrier semaphores. Data moves between devices by JAX's collectives and lax.ppermute only.
A program may use at most 128 MiB of HBM per device.

```python
import math
import jax
import jax.numpy as jnp
from jax import lax

DT = 5120
DS = 3584
TILE = 128
TILES_DEV = 5
SHARDS = 128
ROWS = 512
TILES = 640
VOCAB = 81920
PICK = 128


def tile_lists(key):
    key = jax.random.fold_in(key, 7)
    key_list = jax.random.split(key, 5)
    hot_shard = jax.random.randint(key_list[0], (), 0, SHARDS)
    doubled = jax.random.randint(key_list[1], (ROWS, 1), 1, SHARDS // 4 + 1)
    shuffled = jax.vmap(lambda single: jax.random.permutation(single, SHARDS))(jax.random.split(key_list[2], ROWS))
    position = jnp.argsort(shuffled, axis=1).astype(jnp.int32)
    rank_hot = (position - position[:, hot_shard][:, None]) % SHARDS
    pick_count = jnp.where(rank_hot < doubled, 2, jnp.where(rank_hot >= SHARDS - doubled, 0, 1))
    scores = jax.random.randint(key_list[3], (ROWS, SHARDS, TILES_DEV), 0, 1 << 20) * TILES_DEV + jnp.arange(TILES_DEV, dtype=jnp.int32)
    within = jnp.argsort(scores, axis=2)[:, :, :2].astype(jnp.int32)
    candidate = jnp.arange(SHARDS, dtype=jnp.int32)[None, :, None] * TILES_DEV + within
    is_valid = (jnp.arange(2, dtype=jnp.int32)[None, None, :] < pick_count[:, :, None]).astype(jnp.int32)
    flat_valid = is_valid.reshape(ROWS, 2 * SHARDS)
    slot_index = jnp.where(flat_valid > 0, jnp.cumsum(flat_valid, axis=1) - 1, PICK)
    listed = jnp.zeros((ROWS, PICK), jnp.int32).at[jnp.arange(ROWS)[:, None], slot_index].set(candidate.reshape(ROWS, 2 * SHARDS), mode='drop')
    mixing = jax.vmap(lambda single: jax.random.permutation(single, PICK))(jax.random.split(key_list[4], ROWS))
    return jnp.take_along_axis(listed, mixing, axis=1)


def head_matrix(key, salt, depth):
    key = jax.random.fold_in(key, salt)
    first_key, second_key = jax.random.split(key)
    base = jnp.clip(jax.random.normal(first_key, (depth, VOCAB), jnp.float32), -5.0, 5.0)
    column_scale = jnp.exp(jax.random.uniform(second_key, (1, VOCAB), jnp.float32, math.log(0.6), math.log(1.8)))
    return base * column_scale / math.sqrt(depth)


def draw_tiles(key, part):
    listed = tile_lists(key)
    return listed


def draw_teacher_head(key, part):
    weights = head_matrix(key, 11, DT)
    return weights.astype(jnp.bfloat16)


def draw_student_head(key, part):
    weights = head_matrix(key, 12, DS)
    return weights.reshape(DS, TILES, TILE).astype(jnp.bfloat16)


def draw_teacher_hidden(key, part):
    key = jax.random.fold_in(key, 17)
    scale_key, base_key = jax.random.split(key, 2)
    row_scale = jnp.exp(jax.random.uniform(scale_key, (ROWS, 1), jnp.float32, math.log(0.4), math.log(4.0)))
    base = jnp.clip(jax.random.normal(base_key, (ROWS, DT), jnp.float32), -4.0, 4.0) * row_scale
    return base.astype(jnp.bfloat16)


def draw_student_hidden(key, part):
    key = jax.random.fold_in(key, 19)
    scale_key, base_key = jax.random.split(key, 2)
    row_scale = jnp.exp(jax.random.uniform(scale_key, (ROWS, 1), jnp.float32, math.log(0.4), math.log(4.0)))
    base = jnp.clip(jax.random.normal(base_key, (ROWS, DS), jnp.float32), -4.0, 4.0) * row_scale
    return base.astype(jnp.bfloat16)


def setup_inputs(seed: int = 0) -> dict:
    keys = jax.random.split(jax.random.key(seed), 6)
    teacher_hidden = draw_teacher_hidden(jax.random.fold_in(keys[5], 71), 0)
    teacher_head = draw_teacher_head(jax.random.fold_in(keys[5], 71), 0)
    student_hidden = draw_student_hidden(jax.random.fold_in(keys[5], 71), 0)
    student_head = draw_student_head(jax.random.fold_in(keys[5], 71), 0)
    tiles = draw_tiles(jax.random.fold_in(keys[5], 71), 0)
    return {"teacher_hidden": teacher_hidden, "teacher_head": teacher_head, "student_hidden": student_hidden, "student_head": student_head, "tiles": tiles}


loss_scale = 1024.0


def softmax_parts(logits, unnamed):
    row_top = jnp.max(logits, axis=1, keepdims=True)
    exponent = jnp.exp(logits - row_top)
    row_total = jnp.sum(exponent, axis=1)
    row_rest = jnp.sum(exponent * unnamed, axis=1)
    return exponent / row_total[:, None], row_rest / row_total


def reference(teacher_hidden, teacher_head, student_hidden, student_head, tiles):
    named = jnp.zeros((ROWS, TILES), jnp.float32).at[jnp.arange(ROWS)[:, None], tiles].set(1.0)
    named_cols = jnp.repeat(named, TILE, axis=1)
    unnamed = 1.0 - named_cols
    teacher_logits = jnp.dot(teacher_hidden, teacher_head, preferred_element_type=jnp.float32)
    teacher_prob, teacher_mass = softmax_parts(teacher_logits, unnamed)
    teacher_prob = teacher_prob.astype(jnp.bfloat16)
    student_cols = student_head.reshape(DS, VOCAB)
    student_logits = jnp.dot(student_hidden, student_cols, preferred_element_type=jnp.float32)
    student_prob, student_mass = softmax_parts(student_logits, unnamed)
    kl_grad = jnp.where(named_cols > 0,
                        student_prob - teacher_prob.astype(jnp.float32),
                        student_prob * (1.0 - teacher_mass[:, None] / student_mass[:, None])) * loss_scale
    kl_half = kl_grad.astype(jnp.bfloat16)
    hidden_grad = lax.dot_general(kl_half, student_cols, (((1,), (1,)), ((), ())),
                                  preferred_element_type=jnp.float32)
    return hidden_grad.astype(jnp.bfloat16)
```

```python
import functools

import jax
import jax.numpy as jnp
import numpy as np
from jax import lax
from jax.experimental import pallas as pl
from jax.experimental.pallas import tpu as pltpu
from jax.sharding import PartitionSpec as P

loss_scale = 1024.0
NX, NY, NZ = 4, 4, 8
LINE = ("vocab", "dp")
WHOLE = ("mesh", "vocab", "dp")
HALF = NX * NY * NZ


def device(m, x, y, z):
    return m * HALF + (y * NZ + z) * NX + x


LINES_Z = [
    [device(m, x, y, z) for z in range(NZ)]
    for m in range(2)
    for x in range(NX)
    for y in range(NY)
]
LINES_X = [
    [[device(m, x, y, z) for x in range(NX)] for y in range(NY) for z in range(NZ)]
    for m in range(2)
]
LINES_Y = [
    [[device(m, x, y, z) for y in range(NY)] for x in range(NX) for z in range(NZ)]
    for m in range(2)
]
PLANES_YZ = [
    [device(0, x, y, z) for y in range(NY) for z in range(NZ)] for x in range(NX)
]
PLANES_XZ = [
    [device(1, x, y, z) for x in range(NX) for z in range(NZ)] for y in range(NY)
]


def exchange(value, groups):
    return lax.all_to_all(value, WHOLE, 0, 0, tiled=True, axis_index_groups=groups)


def spread(value, groups):
    count = len(groups[0])
    rows, width = value.shape
    copies = jnp.broadcast_to(value[None], (count, rows, width)).reshape(count * rows, width)
    return exchange(copies, groups)


def home(x, y, z):
    x1, x0 = x // 2, x % 2
    y1, y0 = y // 2, y % 2
    z2, z1, z0 = z // 4, (z // 2) % 2, z % 2
    return 2 * x0 + y1, 2 * y0 + z2, 4 * z1 + 2 * z0 + x1


def row_orders():
    orders = np.zeros((2, 2 * HALF, 2 * HALF), np.float32)
    for x in range(NX):
        for y in range(NY):
            for z in range(NZ):
                hx, hy, hz = home(x, y, z)
                for b in range(2):
                    orders[0, ((hx * NY + hy) * NZ + hz) * 2 + b, ((x * NY + y) * NZ + z) * 2 + b] = 1
                    orders[1, ((hy * NX + hx) * NZ + hz) * 2 + b, ((y * NX + x) * NZ + z) * 2 + b] = 1
    return orders


def last_hop():
    pairs = []
    for m in range(2):
        for x in range(NX):
            for y in range(NY):
                for z in range(NZ):
                    pairs.append(
                        (device(m, x, y, z), device(x % 2, 2 * (x // 2) + m, y, z))
                    )
    return pairs


def tile_words(tiles_t):
    count, rows = tiles_t.shape

    def kernel(tiles_ref, word_ref):
        block = lax.broadcasted_iota(jnp.int32, (count, rows), 0)

        def step(k, word):
            tile = tiles_ref[pl.ds(k, 1), :]
            own = (tile * 205) >> 10
            bit = 1 << (tile - 5 * own)
            return word + jnp.where(block == own, bit, 0)

        word_ref[...] = lax.fori_loop(0, count, step, jnp.zeros((count, rows), jnp.int32))

    return pl.pallas_call(
        kernel,
        out_shape=jax.ShapeDtypeStruct((count, rows), jnp.int32),
    )(tiles_t)


def logits_and_message(hidden, teacher_head, student_cols, own_word, per_shard):
    rows = hidden.shape[0]
    dt, cols = teacher_head.shape
    ds = student_cols.shape[0]
    depth = 512
    t_steps, s_steps = dt // depth, ds // depth
    lanes = cols // per_shard

    def kernel(word_ref, h_ref, t_ref, s_ref, msg_ref, logit_ref, t_acc, s_acc):
        k = pl.program_id(0)

        @pl.when(k == 0)
        def _():
            t_acc[...] = jnp.zeros_like(t_acc)
            s_acc[...] = jnp.zeros_like(s_acc)

        @pl.when(k < t_steps)
        def _():
            t_acc[...] += jnp.dot(h_ref[...], t_ref[...], preferred_element_type=jnp.float32)

        @pl.when(k >= t_steps)
        def _():
            s_acc[...] += jnp.dot(h_ref[...], s_ref[...], preferred_element_type=jnp.float32)

        @pl.when(k == t_steps + s_steps - 1)
        def _():
            word = word_ref[...]
            t_log = t_acc[...].T
            s_log = s_acc[...].T
            logit_ref[...] = s_log
            t_top = jnp.max(t_log, axis=0, keepdims=True)
            named_before = jnp.zeros((1, rows), jnp.int32)
            t_total = jnp.zeros((1, rows), jnp.float32)
            t_rest = jnp.zeros((1, rows), jnp.float32)
            first = jnp.zeros((lanes, rows), jnp.float32)
            second = jnp.zeros((lanes, rows), jnp.float32)
            for t in range(per_shard):
                e = jnp.exp(t_log[t * lanes : (t + 1) * lanes] - t_top)
                part = jnp.sum(e, axis=0, keepdims=True)
                named = (word >> t) & 1
                t_total += part
                t_rest += jnp.where(named == 0, part, 0.0)
                first = jnp.where((named == 1) & (named_before == 0), e, first)
                second = jnp.where((named == 1) & (named_before == 1), e, second)
                named_before += named
            s_top = jnp.max(s_log, axis=0, keepdims=True)
            place = lax.broadcasted_iota(jnp.int32, (8, rows), 0)
            stats = jnp.where(place == 2, t_top, 0.0)
            stats = jnp.where(place == 3, t_total, stats)
            stats = jnp.where(place == 4, t_rest, stats)
            stats = jnp.where(place == 5, s_top, stats)
            msg_ref[...] = jnp.where(
                (place == 0)[None],
                first[:, None, :],
                jnp.where((place == 1)[None], second[:, None, :], stats[None]),
            )

    return pl.pallas_call(
        kernel,
        grid=(t_steps + s_steps,),
        in_specs=[
            pl.BlockSpec((1, rows), lambda k: (0, 0)),
            pl.BlockSpec((rows, depth), lambda k: (0, k)),
            pl.BlockSpec((depth, cols), lambda k: (jnp.minimum(k, t_steps - 1), 0)),
            pl.BlockSpec((depth, cols), lambda k: (jnp.maximum(k - t_steps, 0), 0)),
        ],
        out_specs=[
            pl.BlockSpec((lanes, 8, rows), lambda k: (0, 0, 0)),
            pl.BlockSpec((cols, rows), lambda k: (0, 0)),
        ],
        out_shape=[
            jax.ShapeDtypeStruct((lanes, 8, rows), jnp.float32),
            jax.ShapeDtypeStruct((cols, rows), jnp.float32),
        ],
        scratch_shapes=[
            pltpu.VMEM((rows, cols), jnp.float32),
            pltpu.VMEM((rows, cols), jnp.float32),
        ],
        compiler_params=pltpu.CompilerParams(vmem_limit_bytes=40 * 1024 * 1024),
    )(own_word, hidden, teacher_head, student_cols)


def expand_words(words, per_shard):
    shards = words.shape[0]
    tile = lax.broadcasted_iota(jnp.int32, (shards * per_shard, 1), 0)
    within = tile - per_shard * ((tile * 205) >> 10)
    wide = spread_blocks(words.astype(jnp.bfloat16), per_shard).astype(jnp.int32)
    named = (wide >> within) & 1
    before = wide & ((1 << within) - 1)
    return named == 1, before == 0


def spread_blocks(value, per_shard):
    shards = value.shape[0]
    tile = lax.broadcasted_iota(jnp.int32, (shards * per_shard, shards), 0)
    start = per_shard * lax.broadcasted_iota(jnp.int32, (shards * per_shard, shards), 1)
    chosen = ((tile >= start) & (tile < start + per_shard)).astype(jnp.float32).astype(jnp.bfloat16)
    return jnp.dot(chosen, value, preferred_element_type=jnp.float32)


def student_sums(words, logit, message, per_shard):
    cols, rows = logit.shape

    def kernel(word_ref, logit_ref, msg_ref, out_ref):
        named, _ = expand_words(word_ref[...], per_shard)
        top = jnp.max(logit_ref[...], axis=0, keepdims=True)
        e = jnp.exp(logit_ref[...] - top)
        total = jnp.sum(e, axis=0, keepdims=True)
        rest = jnp.sum(jnp.where(named, 0.0, e), axis=0, keepdims=True)
        place = lax.broadcasted_iota(jnp.int32, (8, rows), 0)
        stats = jnp.where(place == 6, total, jnp.where(place == 7, rest, 0.0))
        out_ref[...] = jnp.where((place >= 6)[None], stats[None], msg_ref[...])

    return pl.pallas_call(
        kernel,
        out_shape=jax.ShapeDtypeStruct(message.shape, jnp.float32),
        compiler_params=pltpu.CompilerParams(vmem_limit_bytes=40 * 1024 * 1024),
    )(words, logit, message)


def gradient(words, logit, arrived, order, student_cols, per_shard):
    cols, rows = logit.shape
    ds = student_cols.shape[0]
    width = 512

    def kernel(word_ref, logit_ref, msg_ref, order_ref, w_ref, out_ref, kl_ref):
        @pl.when(pl.program_id(0) == 0)
        def _():
            def sums(at):
                top_each = msg_ref[:, at, :]
                top = jnp.max(top_each, axis=0, keepdims=True)
                weight = jnp.exp(top_each - top)
                total = jnp.sum(weight * msg_ref[:, at + 1, :], axis=0, keepdims=True)
                rest = jnp.sum(weight * msg_ref[:, at + 2, :], axis=0, keepdims=True)
                return top, weight, total, rest / total

            _, t_weight, t_total, t_mass = sums(2)
            s_top, _, s_total, s_mass = sums(5)
            scale = t_weight / t_total
            first = (msg_ref[:, 0, :] * scale).astype(jnp.bfloat16)
            second = (msg_ref[:, 1, :] * scale).astype(jnp.bfloat16)
            named, is_first = expand_words(word_ref[...], per_shard)
            teacher = jnp.where(
                is_first, spread_blocks(first, per_shard), spread_blocks(second, per_shard)
            )
            prob = jnp.exp(logit_ref[...] - s_top) / s_total
            kl = (
                jnp.where(named, prob - teacher, prob * (1.0 - t_mass / s_mass)) * loss_scale
            ).astype(jnp.bfloat16)
            kl_ref[...] = lax.dot_general(
                order_ref[...], kl, (((1,), (1,)), ((), ())), preferred_element_type=jnp.float32
            ).astype(jnp.bfloat16)

        out_ref[...] = lax.dot_general(
            kl_ref[...], w_ref[...], (((1,), (1,)), ((), ())), preferred_element_type=jnp.float32
        ).astype(jnp.bfloat16)

    return pl.pallas_call(
        kernel,
        grid=(ds // width,),
        in_specs=[
            pl.BlockSpec(words.shape, lambda k: (0, 0)),
            pl.BlockSpec((cols, rows), lambda k: (0, 0)),
            pl.BlockSpec(arrived.shape, lambda k: (0, 0, 0)),
            pl.BlockSpec((rows, rows), lambda k: (0, 0)),
            pl.BlockSpec((width, cols), lambda k: (k, 0)),
        ],
        out_specs=pl.BlockSpec((rows, width), lambda k: (0, k)),
        out_shape=jax.ShapeDtypeStruct((rows, ds), jnp.bfloat16),
        scratch_shapes=[pltpu.VMEM((rows, cols), jnp.bfloat16)],
        compiler_params=pltpu.CompilerParams(vmem_limit_bytes=40 * 1024 * 1024),
    )(words, logit, arrived, order, student_cols)


def per_device(teacher_hidden, teacher_head, student_hidden, student_head, tiles):
    shards = lax.axis_size(LINE)
    shard_index = lax.axis_index(LINE)
    core = lax.axis_index("mesh")
    ds, tiles_all, lane_count = student_head.shape
    student_cols = student_head.reshape(ds, tiles_all * lane_count)
    per_shard = tiles_all // shards
    picks = tiles.shape[1]

    both = jnp.concatenate((teacher_hidden, student_hidden), axis=1)
    mine = lax.dynamic_slice_in_dim(both, 2 * core, 2, 0)
    gathered = spread(mine, LINES_Z)
    gathered = spread(gathered, LINES_Y[0] + LINES_X[1])
    gathered = spread(gathered, LINES_X[0] + LINES_Y[1])

    by_chip = tiles.reshape(NY, NZ, NX, 2, 2, picks)
    by_chip = lax.dynamic_index_in_dim(by_chip, core, 3, keepdims=False)
    tiles_t = jnp.where(
        core == 0, by_chip.transpose(4, 2, 0, 1, 3), by_chip.transpose(4, 0, 2, 1, 3)
    ).reshape(picks, 2 * shards)
    words = tile_words(tiles_t)
    own_word = lax.dynamic_slice_in_dim(words, shard_index, 1, 0)

    message, logit = logits_and_message(
        gathered, teacher_head, student_cols, own_word, per_shard
    )
    message = student_sums(words, logit, message, per_shard)
    arrived = lax.all_to_all(message, LINE, 0, 0, tiled=True)

    order = lax.dynamic_index_in_dim(
        jnp.asarray(row_orders(), jnp.bfloat16), core, 0, keepdims=False
    )
    partial = gradient(words, logit, arrived, order, student_cols, per_shard)

    rows = partial.shape[0]
    near = exchange(partial, LINES_X[0] + LINES_Y[1])
    near = jnp.sum(near.reshape(NX, rows // NX, ds).astype(jnp.float32), axis=0)
    far = exchange(near.astype(jnp.bfloat16), PLANES_YZ + PLANES_XZ)
    summed = jnp.sum(far.reshape(NY * NZ, 2, ds).astype(jnp.float32), axis=0)
    return lax.ppermute(summed.astype(jnp.bfloat16), WHOLE, last_hop())


def solution(mesh):
    return jax.shard_map(
        per_device,
        mesh=mesh,
        in_specs=(
            P(("vocab", "dp"), None),
            P(None, ("vocab", "dp")),
            P(("vocab", "dp"), None),
            P(None, None, ("vocab", "dp")),
            P(),
        ),
        out_specs=P(("mesh", "vocab", "dp"), None),
        check_vma=False,
    )
```

```python
import functools

import jax
import jax.numpy as jnp
import numpy as np
from jax import lax
from jax.experimental import pallas as pl
from jax.experimental.pallas import tpu as pltpu
from jax.sharding import PartitionSpec as P

loss_scale = 1024.0
NX, NY, NZ = 4, 4, 8
LINE = ("vocab", "dp")
WHOLE = ("mesh", "vocab", "dp")
HALF = NX * NY * NZ


def device(m, x, y, z):
    return m * HALF + (y * NZ + z) * NX + x


LINES_Z = [
    [device(m, x, y, z) for z in range(NZ)]
    for m in range(2)
    for x in range(NX)
    for y in range(NY)
]
LINES_X = [
    [[device(m, x, y, z) for x in range(NX)] for y in range(NY) for z in range(NZ)]
    for m in range(2)
]
LINES_Y = [
    [[device(m, x, y, z) for y in range(NY)] for x in range(NX) for z in range(NZ)]
    for m in range(2)
]
PLANES_YZ = [
    [device(0, x, y, z) for y in range(NY) for z in range(NZ)] for x in range(NX)
]
PLANES_XZ = [
    [device(1, x, y, z) for x in range(NX) for z in range(NZ)] for y in range(NY)
]


def exchange(value, groups):
    return lax.all_to_all(value, WHOLE, 0, 0, tiled=True, axis_index_groups=groups)


def spread(value, groups):
    count = len(groups[0])
    rows, width = value.shape
    copies = jnp.broadcast_to(value[None], (count, rows, width)).reshape(count * rows, width)
    return exchange(copies, groups)


def along(value, by):
    pairs = []
    for x in range(NX):
        for y in range(NY):
            for z in range(NZ):
                pairs.append((device(0, x, y, z), device(0, (x + by) % NX, y, z)))
                pairs.append((device(1, x, y, z), device(1, x, (y + by) % NY, z)))
    return lax.ppermute(value, WHOLE, pairs)


def home(x, y, z):
    x1, x0 = x // 2, x % 2
    y1, y0 = y // 2, y % 2
    z2, z1, z0 = z // 4, (z // 2) % 2, z % 2
    return 2 * x0 + y1, 2 * y0 + z2, 4 * z1 + 2 * z0 + x1


def row_orders():
    orders = np.zeros((2, 2 * HALF, 2 * HALF), np.float32)
    for x in range(NX):
        for y in range(NY):
            for z in range(NZ):
                hx, hy, hz = home(x, y, z)
                for b in range(2):
                    orders[0, ((hx * NY + hy) * NZ + hz) * 2 + b, ((x * NY + y) * NZ + z) * 2 + b] = 1
                    orders[1, ((hy * NX + hx) * NZ + hz) * 2 + b, ((y * NX + x) * NZ + z) * 2 + b] = 1
    return orders


def last_hop():
    pairs = []
    for m in range(2):
        for x in range(NX):
            for y in range(NY):
                for z in range(NZ):
                    pairs.append(
                        (device(m, x, y, z), device(x % 2, 2 * (x // 2) + m, y, z))
                    )
    return pairs


def tile_words(tiles_t):
    count, rows = tiles_t.shape

    def kernel(tiles_ref, word_ref):
        block = lax.broadcasted_iota(jnp.int32, (count, rows), 0)

        def step(k, word):
            tile = tiles_ref[pl.ds(k, 1), :]
            own = (tile * 205) >> 10
            bit = 1 << (tile - 5 * own)
            return word + jnp.where(block == own, bit, 0)

        word_ref[...] = lax.fori_loop(0, count, step, jnp.zeros((count, rows), jnp.int32), unroll=8)

    return pl.pallas_call(
        kernel,
        out_shape=jax.ShapeDtypeStruct((count, rows), jnp.int32),
        cost_estimate=pl.CostEstimate(
            flops=16 * count * count * rows, bytes_accessed=8 * count * rows, transcendentals=0
        ),
    )(tiles_t)


def fetch(source, chunk, buffer, semaphores):
    copies = []
    for k in range(source.shape[0] // chunk):
        rows = pl.ds(k * chunk, chunk)
        copies.append(pltpu.make_async_copy(source.at[rows], buffer.at[rows], semaphores.at[k]))
        copies[-1].start()
    return copies


def logits_and_message(
    slot, own, below, above, left_half, right_half, teacher_head, student_cols, words, own_word,
    per_shard,
):
    piece = own.shape[0]
    rows = 4 * piece
    cols = teacher_head.shape[1]
    lanes = cols // per_shard
    half = left_half.shape[1]
    depth = 512
    t_steps, s_steps = teacher_head.shape[0] // depth, student_cols.shape[0] // depth

    def kernel(
        slot_ref, own_ref, below_ref, above_ref, lh_ref, rh_ref, word_ref, own_word_ref,
        t_hbm, s_hbm, msg_ref, logit_ref, t_ref, s_ref, part_ref, all_ref, t_sem, s_sem,
    ):
        copies = fetch(t_hbm, depth, t_ref, t_sem) + fetch(s_hbm, depth, s_ref, s_sem)

        def across(start, stop):
            if stop <= half:
                return lh_ref[:, start:stop]
            if start >= half:
                return rh_ref[:, start - half : stop - half]
            return jnp.concatenate((lh_ref[:, start:], rh_ref[:, : stop - half]), axis=1)

        for k in range(t_steps + s_steps):
            at = k * depth
            span = slice(at, at + depth)
            left = jnp.concatenate(
                (own_ref[:, span], above_ref[:, span], across(at, at + depth), below_ref[:, span]),
                axis=0,
            )
            copies[k].wait()
            if k < t_steps:
                right, col = t_ref[span, :], slice(0, cols)
            else:
                right, col = s_ref[at - t_steps * depth : at - t_steps * depth + depth, :], slice(cols, 2 * cols)
            term = jnp.dot(left, right, preferred_element_type=jnp.float32)
            if k in (0, t_steps):
                part_ref[:, col] = term
            else:
                part_ref[:, col] += term

        for offset in range(4):
            at = lax.rem(slot_ref[0] + offset, 4)
            all_ref[pl.ds(pl.multiple_of(at * piece, piece), piece), :] = part_ref[
                offset * piece : (offset + 1) * piece, :
            ]

        word = own_word_ref[...]
        t_log = all_ref[:, :cols].T
        s_log = all_ref[:, cols:].T
        logit_ref[...] = s_log
        t_top = jnp.max(t_log, axis=0, keepdims=True)
        named_before = jnp.zeros((1, rows), jnp.int32)
        t_total = jnp.zeros((1, rows), jnp.float32)
        t_rest = jnp.zeros((1, rows), jnp.float32)
        first = jnp.zeros((lanes, rows), jnp.float32)
        second = jnp.zeros((lanes, rows), jnp.float32)
        for t in range(per_shard):
            e = jnp.exp(t_log[t * lanes : (t + 1) * lanes] - t_top)
            part = jnp.sum(e, axis=0, keepdims=True)
            named = (word >> t) & 1
            t_total += part
            t_rest += jnp.where(named == 0, part, 0.0)
            first = jnp.where((named == 1) & (named_before == 0), e, first)
            second = jnp.where((named == 1) & (named_before == 1), e, second)
            named_before += named
        named_s, _ = expand_words(word_ref[...], per_shard)
        s_top = jnp.max(s_log, axis=0, keepdims=True)
        e = jnp.exp(s_log - s_top)
        s_total = jnp.sum(e, axis=0, keepdims=True)
        s_rest = jnp.sum(jnp.where(named_s, 0.0, e), axis=0, keepdims=True)
        line = lax.broadcasted_iota(jnp.int32, (8, rows), 0)
        stats = jnp.zeros((8, rows), jnp.float32)
        for at, value in enumerate((t_top, t_total, t_rest, s_top, s_total, s_rest)):
            stats = jnp.where(line == at + 2, value, stats)
        msg_ref[...] = jnp.where(
            (line == 0)[None],
            first[:, None, :],
            jnp.where((line == 1)[None], second[:, None, :], stats[None]),
        )

    whole = pl.BlockSpec(memory_space=pltpu.VMEM)
    remote = pl.BlockSpec(memory_space=pltpu.HBM)
    return pl.pallas_call(
        kernel,
        in_specs=[pl.BlockSpec(memory_space=pltpu.SMEM)] + [whole] * 7 + [remote] * 2,
        out_specs=[whole, whole],
        out_shape=[
            jax.ShapeDtypeStruct((lanes, 8, rows), jnp.float32),
            jax.ShapeDtypeStruct((cols, rows), jnp.float32),
        ],
        scratch_shapes=[
            pltpu.VMEM(teacher_head.shape, jnp.bfloat16),
            pltpu.VMEM(student_cols.shape, jnp.bfloat16),
            pltpu.VMEM((rows, 2 * cols), jnp.float32),
            pltpu.VMEM((rows, 2 * cols), jnp.float32),
            pltpu.SemaphoreType.DMA((t_steps,)),
            pltpu.SemaphoreType.DMA((s_steps,)),
        ],
        compiler_params=pltpu.CompilerParams(vmem_limit_bytes=48 * 1024 * 1024),
    )(slot, own, below, above, left_half, right_half, words, own_word, teacher_head, student_cols)


def expand_words(words, per_shard):
    shards = words.shape[0]
    tile = lax.broadcasted_iota(jnp.int32, (shards * per_shard, 1), 0)
    within = tile - per_shard * ((tile * 205) >> 10)
    wide = spread_blocks(words.astype(jnp.bfloat16), per_shard).astype(jnp.int32)
    named = (wide >> within) & 1
    before = wide & ((1 << within) - 1)
    return named == 1, before == 0


def spread_blocks(value, per_shard):
    shards = value.shape[0]
    tile = lax.broadcasted_iota(jnp.int32, (shards * per_shard, shards), 0)
    start = per_shard * lax.broadcasted_iota(jnp.int32, (shards * per_shard, shards), 1)
    chosen = ((tile >= start) & (tile < start + per_shard)).astype(jnp.float32).astype(jnp.bfloat16)
    return jnp.dot(chosen, value, preferred_element_type=jnp.float32)


def gradient(words, logit, arrived, order, student_cols, per_shard):
    cols, rows = logit.shape
    ds = student_cols.shape[0]
    width = 512

    def kernel(word_ref, logit_ref, msg_ref, order_ref, w_hbm, out_ref, w_ref, w_sem):
        copies = fetch(w_hbm, width, w_ref, w_sem)

        def sums(at):
            top_each = msg_ref[:, at, :]
            top = jnp.max(top_each, axis=0, keepdims=True)
            weight = jnp.exp(top_each - top)
            total = jnp.sum(weight * msg_ref[:, at + 1, :], axis=0, keepdims=True)
            rest = jnp.sum(weight * msg_ref[:, at + 2, :], axis=0, keepdims=True)
            return top, weight, total, rest / total

        _, t_weight, t_total, t_mass = sums(2)
        s_top, _, s_total, s_mass = sums(5)
        scale = t_weight / t_total
        first = (msg_ref[:, 0, :] * scale).astype(jnp.bfloat16)
        second = (msg_ref[:, 1, :] * scale).astype(jnp.bfloat16)
        named, is_first = expand_words(word_ref[...], per_shard)
        teacher = jnp.where(
            is_first, spread_blocks(first, per_shard), spread_blocks(second, per_shard)
        )
        prob = jnp.exp(logit_ref[...] - s_top) / s_total
        kl = (
            jnp.where(named, prob - teacher, prob * (1.0 - t_mass / s_mass)) * loss_scale
        ).astype(jnp.bfloat16)
        kl = lax.dot_general(
            order_ref[...], kl, (((1,), (1,)), ((), ())), preferred_element_type=jnp.float32
        ).astype(jnp.bfloat16)
        for k in range(ds // width):
            span = slice(k * width, (k + 1) * width)
            copies[k].wait()
            out_ref[:, span] = lax.dot_general(
                kl, w_ref[span, :], (((1,), (1,)), ((), ())), preferred_element_type=jnp.float32
            ).astype(jnp.bfloat16)

    whole = pl.BlockSpec(memory_space=pltpu.VMEM)
    return pl.pallas_call(
        kernel,
        in_specs=[whole] * 4 + [pl.BlockSpec(memory_space=pltpu.HBM)],
        out_specs=whole,
        out_shape=jax.ShapeDtypeStruct((rows, ds), jnp.bfloat16),
        scratch_shapes=[
            pltpu.VMEM(student_cols.shape, jnp.bfloat16),
            pltpu.SemaphoreType.DMA((ds // width,)),
        ],
        compiler_params=pltpu.CompilerParams(vmem_limit_bytes=48 * 1024 * 1024),
    )(words, logit, arrived, order, student_cols)


def per_device(teacher_hidden, teacher_head, student_hidden, student_head, tiles):
    shards = lax.axis_size(LINE)
    shard_index = lax.axis_index(LINE)
    core = lax.axis_index("mesh")
    ds, tiles_all, lane_count = student_head.shape
    student_cols = student_head.reshape(ds, tiles_all * lane_count)
    per_shard = tiles_all // shards
    picks = tiles.shape[1]

    both = jnp.concatenate((teacher_hidden, student_hidden), axis=1)
    mine = lax.dynamic_slice_in_dim(both, 2 * core, 2, 0)
    gathered = spread(mine, LINES_Z)
    gathered = spread(gathered, LINES_Y[0] + LINES_X[1])
    by_chip = tiles.reshape(NY, NZ, NX, 2, 2, picks)
    by_chip = lax.dynamic_index_in_dim(by_chip, core, 3, keepdims=False)
    tiles_t = jnp.where(
        core == 0, by_chip.transpose(4, 2, 0, 1, 3), by_chip.transpose(4, 0, 2, 1, 3)
    ).reshape(picks, 2 * shards)
    words = tile_words(tiles_t)
    below, above = along(gathered, 1), along(gathered, -1)
    below, above, words = lax.optimization_barrier((below, above, words))
    half = gathered.shape[1] // 2
    left_half = along(below[:, :half], 1)
    right_half = along(above[:, half:], -1)
    own_word = lax.dynamic_slice_in_dim(words, shard_index, 1, 0)

    slot = jnp.where(core == 0, lax.axis_index("dp"), lax.axis_index("vocab") // NZ)
    message, logit = logits_and_message(
        slot.reshape(1), gathered, below, above, left_half, right_half, teacher_head,
        student_cols, words, own_word, per_shard,
    )
    arrived = lax.all_to_all(message, LINE, 0, 0, tiled=True)

    order = lax.dynamic_index_in_dim(
        jnp.asarray(row_orders(), jnp.bfloat16), core, 0, keepdims=False
    )
    partial = gradient(words, logit, arrived, order, student_cols, per_shard)

    rows = partial.shape[0]
    near = exchange(partial, LINES_X[0] + LINES_Y[1])
    near = jnp.sum(near.reshape(NX, rows // NX, ds).astype(jnp.float32), axis=0)
    far = exchange(near.astype(jnp.bfloat16), PLANES_YZ + PLANES_XZ)
    summed = jnp.sum(far.reshape(NY * NZ, 2, ds).astype(jnp.float32), axis=0)
    return lax.ppermute(summed.astype(jnp.bfloat16), WHOLE, last_hop())


def solution(mesh):
    return jax.shard_map(
        per_device,
        mesh=mesh,
        in_specs=(
            P(("vocab", "dp"), None),
            P(None, ("vocab", "dp")),
            P(("vocab", "dp"), None),
            P(None, None, ("vocab", "dp")),
            P(),
        ),
        out_specs=P(("mesh", "vocab", "dp"), None),
        check_vma=False,
    )
```

```python
import functools

import jax
import jax.numpy as jnp
import numpy as np
from jax import lax
from jax.experimental import pallas as pl
from jax.experimental.pallas import tpu as pltpu
from jax.sharding import PartitionSpec as P

loss_scale = 1024.0
NX, NY, NZ = 4, 4, 8
LINE = ("vocab", "dp")
WHOLE = ("mesh", "vocab", "dp")
HALF = NX * NY * NZ


def device(m, x, y, z):
    return m * HALF + (y * NZ + z) * NX + x


LINES_Z = [
    [device(m, x, y, z) for z in range(NZ)]
    for m in range(2)
    for x in range(NX)
    for y in range(NY)
]
LINES_X = [
    [[device(m, x, y, z) for x in range(NX)] for y in range(NY) for z in range(NZ)]
    for m in range(2)
]
LINES_Y = [
    [[device(m, x, y, z) for y in range(NY)] for x in range(NX) for z in range(NZ)]
    for m in range(2)
]
PLANES_YZ = [
    [device(0, x, y, z) for y in range(NY) for z in range(NZ)] for x in range(NX)
]
PLANES_XZ = [
    [device(1, x, y, z) for x in range(NX) for z in range(NZ)] for y in range(NY)
]


def exchange(value, groups):
    return lax.all_to_all(value, WHOLE, 0, 0, tiled=True, axis_index_groups=groups)


def spread(value, groups):
    count = len(groups[0])
    rows, width = value.shape
    copies = jnp.broadcast_to(value[None], (count, rows, width)).reshape(count * rows, width)
    return exchange(copies, groups)


def step(value, axes, by):
    sizes = {"x": NX, "y": NY}
    pairs = []
    for m in range(2):
        for x in range(NX):
            for y in range(NY):
                for z in range(NZ):
                    to = {"x": x, "y": y}
                    to[axes[m]] = (to[axes[m]] + by) % sizes[axes[m]]
                    pairs.append((device(m, x, y, z), device(m, to["x"], to["y"], z)))
    return lax.ppermute(value, WHOLE, pairs)


def across(value, by):
    return step(value, ("y", "x"), by)


def along(value, by):
    return step(value, ("x", "y"), by)


def home(x, y, z):
    x1, x0 = x // 2, x % 2
    y1, y0 = y // 2, y % 2
    z2, z1, z0 = z // 4, (z // 2) % 2, z % 2
    return 2 * x0 + y1, 2 * y0 + z2, 4 * z1 + 2 * z0 + x1


def row_orders():
    orders = np.zeros((2, 2 * HALF, 2 * HALF), np.float32)
    for x in range(NX):
        for y in range(NY):
            for z in range(NZ):
                hx, hy, hz = home(x, y, z)
                for b in range(2):
                    orders[0, ((hx * NY + hy) * NZ + hz) * 2 + b, ((x * NY + y) * NZ + z) * 2 + b] = 1
                    orders[1, ((hy * NX + hx) * NZ + hz) * 2 + b, ((y * NX + x) * NZ + z) * 2 + b] = 1
    return orders


def last_hop():
    pairs = []
    for m in range(2):
        for x in range(NX):
            for y in range(NY):
                for z in range(NZ):
                    pairs.append(
                        (device(m, x, y, z), device(x % 2, 2 * (x // 2) + m, y, z))
                    )
    return pairs


def tile_words(tiles_t):
    count, rows = tiles_t.shape

    def kernel(tiles_ref, word_ref):
        block = lax.broadcasted_iota(jnp.int32, (count, rows), 0)

        def step(k, word):
            tile = tiles_ref[pl.ds(k, 1), :]
            own = (tile * 205) >> 10
            bit = 1 << (tile - 5 * own)
            return word + jnp.where(block == own, bit, 0)

        word_ref[...] = lax.fori_loop(0, count, step, jnp.zeros((count, rows), jnp.int32), unroll=8)

    return pl.pallas_call(
        kernel,
        out_shape=jax.ShapeDtypeStruct((count, rows), jnp.int32),
        cost_estimate=pl.CostEstimate(
            flops=16 * count * count * rows, bytes_accessed=8 * count * rows, transcendentals=0
        ),
    )(tiles_t)


def fetch(source, chunk, buffer, semaphores):
    copies = []
    for k in range(source.shape[0] // chunk):
        rows = pl.ds(k * chunk, chunk)
        copies.append(pltpu.make_async_copy(source.at[rows], buffer.at[rows], semaphores.at[k]))
        copies[-1].start()
    return copies


def logits_and_message(slots, halves, teacher_head, student_cols, words, own_word, per_shard):
    count = len(halves)
    half = halves[0].shape[0]
    rows = count * half
    block = half // 2
    cols = teacher_head.shape[1]
    lanes = cols // per_shard
    depth = 512
    t_steps, s_steps = teacher_head.shape[0] // depth, student_cols.shape[0] // depth

    def kernel(slot_ref, *refs):
        half_refs = refs[:count]
        (
            word_ref, own_word_ref, t_hbm, s_hbm, msg_ref, logit_ref,
            t_ref, s_ref, part_ref, all_ref, t_sem, s_sem,
        ) = refs[count:]
        copies = fetch(t_hbm, depth, t_ref, t_sem) + fetch(s_hbm, depth, s_ref, s_sem)

        for k in range(t_steps + s_steps):
            left = jnp.concatenate(
                [ref[:, k * depth : (k + 1) * depth] for ref in half_refs], axis=0
            )
            copies[k].wait()
            if k < t_steps:
                right, col = t_ref[k * depth : (k + 1) * depth, :], slice(0, cols)
            else:
                n = k - t_steps
                right, col = s_ref[n * depth : (n + 1) * depth, :], slice(cols, 2 * cols)
            term = jnp.dot(left, right, preferred_element_type=jnp.float32)
            if k in (0, t_steps):
                part_ref[:, col] = term
            else:
                part_ref[:, col] += term

        for n in range(16):
            third = lax.rem(slot_ref[0] + n // 4, 4)
            second = lax.rem(slot_ref[1] + (0, 3, 1, 2)[n % 4], 4)
            at = pl.multiple_of((third * 4 + second) * block, block)
            all_ref[pl.ds(at, block), :] = part_ref[n * block : (n + 1) * block, :]

        word = own_word_ref[...]
        t_log = all_ref[:, :cols].T
        s_log = all_ref[:, cols:].T
        logit_ref[...] = s_log
        t_top = jnp.max(t_log, axis=0, keepdims=True)
        named_before = jnp.zeros((1, rows), jnp.int32)
        t_total = jnp.zeros((1, rows), jnp.float32)
        t_rest = jnp.zeros((1, rows), jnp.float32)
        first = jnp.zeros((lanes, rows), jnp.float32)
        second = jnp.zeros((lanes, rows), jnp.float32)
        for t in range(per_shard):
            e = jnp.exp(t_log[t * lanes : (t + 1) * lanes] - t_top)
            part = jnp.sum(e, axis=0, keepdims=True)
            named = (word >> t) & 1
            t_total += part
            t_rest += jnp.where(named == 0, part, 0.0)
            first = jnp.where((named == 1) & (named_before == 0), e, first)
            second = jnp.where((named == 1) & (named_before == 1), e, second)
            named_before += named
        named_s, _ = expand_words(word_ref[...], per_shard)
        s_top = jnp.max(s_log, axis=0, keepdims=True)
        e = jnp.exp(s_log - s_top)
        s_total = jnp.sum(e, axis=0, keepdims=True)
        s_rest = jnp.sum(jnp.where(named_s, 0.0, e), axis=0, keepdims=True)
        line = lax.broadcasted_iota(jnp.int32, (8, rows), 0)
        stats = jnp.zeros((8, rows), jnp.float32)
        for at, value in enumerate((t_top, t_total, t_rest, s_top, s_total, s_rest)):
            stats = jnp.where(line == at + 2, value, stats)
        msg_ref[...] = jnp.where(
            (line == 0)[None],
            first[:, None, :],
            jnp.where((line == 1)[None], second[:, None, :], stats[None]),
        )

    whole = pl.BlockSpec(memory_space=pltpu.VMEM)
    remote = pl.BlockSpec(memory_space=pltpu.HBM)
    return pl.pallas_call(
        kernel,
        in_specs=[pl.BlockSpec(memory_space=pltpu.SMEM)] + [whole] * (count + 2) + [remote] * 2,
        out_specs=[whole, whole],
        out_shape=[
            jax.ShapeDtypeStruct((lanes, 8, rows), jnp.float32),
            jax.ShapeDtypeStruct((cols, rows), jnp.float32),
        ],
        scratch_shapes=[
            pltpu.VMEM(teacher_head.shape, jnp.bfloat16),
            pltpu.VMEM(student_cols.shape, jnp.bfloat16),
            pltpu.VMEM((rows, 2 * cols), jnp.float32),
            pltpu.VMEM((rows, 2 * cols), jnp.float32),
            pltpu.SemaphoreType.DMA((t_steps,)),
            pltpu.SemaphoreType.DMA((s_steps,)),
        ],
        compiler_params=pltpu.CompilerParams(vmem_limit_bytes=48 * 1024 * 1024),
    )(slots, *halves, words, own_word, teacher_head, student_cols)


def expand_words(words, per_shard):
    shards = words.shape[0]
    tile = lax.broadcasted_iota(jnp.int32, (shards * per_shard, 1), 0)
    within = tile - per_shard * ((tile * 205) >> 10)
    wide = spread_blocks(words.astype(jnp.bfloat16), per_shard).astype(jnp.int32)
    named = (wide >> within) & 1
    before = wide & ((1 << within) - 1)
    return named == 1, before == 0


def spread_blocks(value, per_shard):
    shards = value.shape[0]
    tile = lax.broadcasted_iota(jnp.int32, (shards * per_shard, shards), 0)
    start = per_shard * lax.broadcasted_iota(jnp.int32, (shards * per_shard, shards), 1)
    chosen = ((tile >= start) & (tile < start + per_shard)).astype(jnp.float32).astype(jnp.bfloat16)
    return jnp.dot(chosen, value, preferred_element_type=jnp.float32)


def gradient(words, logit, arrived, order, student_cols, per_shard):
    cols, rows = logit.shape
    ds = student_cols.shape[0]
    width = 512

    def kernel(word_ref, logit_ref, msg_ref, order_ref, w_hbm, out_ref, w_ref, w_sem):
        copies = fetch(w_hbm, width, w_ref, w_sem)

        def sums(at):
            top_each = msg_ref[:, at, :]
            top = jnp.max(top_each, axis=0, keepdims=True)
            weight = jnp.exp(top_each - top)
            total = jnp.sum(weight * msg_ref[:, at + 1, :], axis=0, keepdims=True)
            rest = jnp.sum(weight * msg_ref[:, at + 2, :], axis=0, keepdims=True)
            return top, weight, total, rest / total

        _, t_weight, t_total, t_mass = sums(2)
        s_top, _, s_total, s_mass = sums(5)
        scale = t_weight / t_total
        first = (msg_ref[:, 0, :] * scale).astype(jnp.bfloat16)
        second = (msg_ref[:, 1, :] * scale).astype(jnp.bfloat16)
        named, is_first = expand_words(word_ref[...], per_shard)
        teacher = jnp.where(
            is_first, spread_blocks(first, per_shard), spread_blocks(second, per_shard)
        )
        prob = jnp.exp(logit_ref[...] - s_top) / s_total
        kl = (
            jnp.where(named, prob - teacher, prob * (1.0 - t_mass / s_mass)) * loss_scale
        ).astype(jnp.bfloat16)
        kl = lax.dot_general(
            order_ref[...], kl, (((1,), (1,)), ((), ())), preferred_element_type=jnp.float32
        ).astype(jnp.bfloat16)
        for k in range(ds // width):
            span = slice(k * width, (k + 1) * width)
            copies[k].wait()
            out_ref[:, span] = lax.dot_general(
                kl, w_ref[span, :], (((1,), (1,)), ((), ())), preferred_element_type=jnp.float32
            ).astype(jnp.bfloat16)

    whole = pl.BlockSpec(memory_space=pltpu.VMEM)
    return pl.pallas_call(
        kernel,
        in_specs=[whole] * 4 + [pl.BlockSpec(memory_space=pltpu.HBM)],
        out_specs=whole,
        out_shape=jax.ShapeDtypeStruct((rows, ds), jnp.bfloat16),
        scratch_shapes=[
            pltpu.VMEM(student_cols.shape, jnp.bfloat16),
            pltpu.SemaphoreType.DMA((ds // width,)),
        ],
        compiler_params=pltpu.CompilerParams(vmem_limit_bytes=48 * 1024 * 1024),
    )(words, logit, arrived, order, student_cols)


def per_device(teacher_hidden, teacher_head, student_hidden, student_head, tiles):
    shards = lax.axis_size(LINE)
    shard_index = lax.axis_index(LINE)
    core = lax.axis_index("mesh")
    ds, tiles_all, lane_count = student_head.shape
    student_cols = student_head.reshape(ds, tiles_all * lane_count)
    per_shard = tiles_all // shards
    picks = tiles.shape[1]

    both = jnp.concatenate((teacher_hidden, student_hidden), axis=1)
    mine = lax.dynamic_slice_in_dim(both, 2 * core, 2, 0)
    gathered = spread(mine, LINES_Z)
    by_chip = tiles.reshape(NY, NZ, NX, 2, 2, picks)
    by_chip = lax.dynamic_index_in_dim(by_chip, core, 3, keepdims=False)
    tiles_t = jnp.where(
        core == 0, by_chip.transpose(4, 2, 0, 1, 3), by_chip.transpose(4, 0, 2, 1, 3)
    ).reshape(picks, 2 * shards)
    words = tile_words(tiles_t)
    last, after, opposite = across(gathered, 1), across(gathered, -1), across(gathered, 2)
    own = (
        jnp.concatenate((gathered, last), axis=0),
        jnp.concatenate((after, opposite), axis=0),
    )
    below_first = along(own[0], 1)
    above_first = along(own[1], -1)
    below_second = along(own[1], 1)
    above_second = along(own[0], -1)
    below_first, above_first, words = lax.optimization_barrier((below_first, above_first, words))
    far = (along(below_first, 1), along(above_first, -1))
    halves = own + (above_second, above_first) + far + (below_first, below_second)
    own_word = lax.dynamic_slice_in_dim(words, shard_index, 1, 0)

    x, y = lax.axis_index("dp"), lax.axis_index("vocab") // NZ
    slots = jnp.stack((jnp.where(core == 0, x, y), jnp.where(core == 0, y, x)))
    message, logit = logits_and_message(
        slots, halves, teacher_head, student_cols, words, own_word, per_shard
    )
    arrived = lax.all_to_all(message, LINE, 0, 0, tiled=True)

    order = lax.dynamic_index_in_dim(
        jnp.asarray(row_orders(), jnp.bfloat16), core, 0, keepdims=False
    )
    partial = gradient(words, logit, arrived, order, student_cols, per_shard)

    rows = partial.shape[0]
    near = exchange(partial, LINES_X[0] + LINES_Y[1])
    near = jnp.sum(near.reshape(NX, rows // NX, ds).astype(jnp.float32), axis=0)
    far = exchange(near.astype(jnp.bfloat16), PLANES_YZ + PLANES_XZ)
    summed = jnp.sum(far.reshape(NY * NZ, 2, ds).astype(jnp.float32), axis=0)
    return lax.ppermute(summed.astype(jnp.bfloat16), WHOLE, last_hop())


def solution(mesh):
    return jax.shard_map(
        per_device,
        mesh=mesh,
        in_specs=(
            P(("vocab", "dp"), None),
            P(None, ("vocab", "dp")),
            P(("vocab", "dp"), None),
            P(None, None, ("vocab", "dp")),
            P(),
        ),
        out_specs=P(("mesh", "vocab", "dp"), None),
        check_vma=False,
    )
```

```python
import functools

import jax
import jax.numpy as jnp
import numpy as np
from jax import lax
from jax.experimental import pallas as pl
from jax.experimental.pallas import tpu as pltpu
from jax.sharding import PartitionSpec as P

loss_scale = 1024.0
NX, NY, NZ = 4, 4, 8
LINE = ("vocab", "dp")
WHOLE = ("mesh", "vocab", "dp")
HALF = NX * NY * NZ


def device(m, x, y, z):
    return m * HALF + (y * NZ + z) * NX + x


LINES_Z = [
    [device(m, x, y, z) for z in range(NZ)]
    for m in range(2)
    for x in range(NX)
    for y in range(NY)
]
LINES_X = [
    [[device(m, x, y, z) for x in range(NX)] for y in range(NY) for z in range(NZ)]
    for m in range(2)
]
LINES_Y = [
    [[device(m, x, y, z) for y in range(NY)] for x in range(NX) for z in range(NZ)]
    for m in range(2)
]
PLANES_YZ = [
    [device(0, x, y, z) for y in range(NY) for z in range(NZ)] for x in range(NX)
]
PLANES_XZ = [
    [device(1, x, y, z) for x in range(NX) for z in range(NZ)] for y in range(NY)
]


def exchange(value, groups):
    return lax.all_to_all(value, WHOLE, 0, 0, tiled=True, axis_index_groups=groups)


def spread(value, groups):
    count = len(groups[0])
    rows, width = value.shape
    copies = jnp.broadcast_to(value[None], (count, rows, width)).reshape(count * rows, width)
    return exchange(copies, groups)


def step(value, axes, by):
    sizes = {"x": NX, "y": NY}
    pairs = []
    for m in range(2):
        for x in range(NX):
            for y in range(NY):
                for z in range(NZ):
                    to = {"x": x, "y": y}
                    to[axes[m]] = (to[axes[m]] + by) % sizes[axes[m]]
                    pairs.append((device(m, x, y, z), device(m, to["x"], to["y"], z)))
    return lax.ppermute(value, WHOLE, pairs)


def across(value, by):
    return step(value, ("y", "x"), by)


def along(value, by):
    return step(value, ("x", "y"), by)


def home(x, y, z):
    x1, x0 = x // 2, x % 2
    y1, y0 = y // 2, y % 2
    z2, z1, z0 = z // 4, (z // 2) % 2, z % 2
    return 2 * x0 + y1, 2 * y0 + z2, 4 * z1 + 2 * z0 + x1


def row_orders():
    orders = np.zeros((2, 2 * HALF, 2 * HALF), np.float32)
    for x in range(NX):
        for y in range(NY):
            for z in range(NZ):
                hx, hy, hz = home(x, y, z)
                for b in range(2):
                    orders[0, ((hx * NY + hy) * NZ + hz) * 2 + b, ((x * NY + y) * NZ + z) * 2 + b] = 1
                    orders[1, ((hy * NX + hx) * NZ + hz) * 2 + b, ((y * NX + x) * NZ + z) * 2 + b] = 1
    return orders


def last_hop():
    pairs = []
    for m in range(2):
        for x in range(NX):
            for y in range(NY):
                for z in range(NZ):
                    pairs.append(
                        (device(m, x, y, z), device(x % 2, 2 * (x // 2) + m, y, z))
                    )
    return pairs


def tile_words(tiles_t):
    count, rows = tiles_t.shape

    def kernel(tiles_ref, word_ref):
        block = lax.broadcasted_iota(jnp.int32, (count, rows), 0)

        def step(k, word):
            tile = tiles_ref[pl.ds(k, 1), :]
            own = (tile * 205) >> 10
            bit = 1 << (tile - 5 * own)
            return word + jnp.where(block == own, bit, 0)

        word_ref[...] = lax.fori_loop(0, count, step, jnp.zeros((count, rows), jnp.int32), unroll=8)

    return pl.pallas_call(
        kernel,
        out_shape=jax.ShapeDtypeStruct((count, rows), jnp.int32),
        cost_estimate=pl.CostEstimate(
            flops=16 * count * count * rows, bytes_accessed=8 * count * rows, transcendentals=0
        ),
    )(tiles_t)


def fetch(source, chunk, buffer, semaphores):
    copies = []
    for k in range(source.shape[0] // chunk):
        rows = pl.ds(k * chunk, chunk)
        copies.append(pltpu.make_async_copy(source.at[rows], buffer.at[rows], semaphores.at[k]))
        copies[-1].start()
    return copies


def logits_and_message(slots, halves, teacher_head, student_cols, words, own_word, per_shard):
    count = len(halves)
    half = halves[0].shape[0]
    rows = count * half
    block = half // 2
    cols = teacher_head.shape[1]
    lanes = cols // per_shard
    depth = 512
    t_steps, s_steps = teacher_head.shape[0] // depth, student_cols.shape[0] // depth

    def kernel(slot_ref, *refs):
        half_refs = refs[:count]
        (
            word_ref, own_word_ref, t_hbm, s_hbm, msg_ref, logit_ref,
            t_ref, s_ref, part_ref, all_ref, spare_ref, t_sem, s_sem,
        ) = refs[count:]
        copies = fetch(t_hbm, depth, t_ref, t_sem) + fetch(s_hbm, depth, s_ref, s_sem)

        for k in range(t_steps + s_steps):
            left = jnp.concatenate(
                [ref[:, k * depth : (k + 1) * depth] for ref in half_refs], axis=0
            )
            copies[k].wait()
            if k < t_steps:
                right, col = t_ref[k * depth : (k + 1) * depth, :], slice(0, cols)
            else:
                n = k - t_steps
                right, col = s_ref[n * depth : (n + 1) * depth, :], slice(cols, 2 * cols)
            term = jnp.dot(left, right, preferred_element_type=jnp.float32)
            if k in (0, t_steps):
                part_ref[:, col] = term
            else:
                part_ref[:, col] += term

        for n in range(16):
            third = lax.rem(slot_ref[0] + n // 4, 4)
            second = lax.rem(slot_ref[1] + (0, 3, 1, 2)[n % 4], 4)
            at = pl.multiple_of((third * 4 + second) * block, block)
            all_ref[pl.ds(at, block), :] = part_ref[n * block : (n + 1) * block, :]

        word = own_word_ref[...]
        t_log = all_ref[:, :cols].T
        s_log = all_ref[:, cols:].T
        logit_ref[...] = s_log
        t_top = jnp.max(t_log, axis=0, keepdims=True)
        named_before = jnp.zeros((1, rows), jnp.int32)
        t_total = jnp.zeros((1, rows), jnp.float32)
        t_rest = jnp.zeros((1, rows), jnp.float32)
        first = jnp.zeros((lanes, rows), jnp.float32)
        second = jnp.zeros((lanes, rows), jnp.float32)
        for t in range(per_shard):
            e = jnp.exp(t_log[t * lanes : (t + 1) * lanes] - t_top)
            part = jnp.sum(e, axis=0, keepdims=True)
            named = (word >> t) & 1
            t_total += part
            t_rest += jnp.where(named == 0, part, 0.0)
            first = jnp.where((named == 1) & (named_before == 0), e, first)
            second = jnp.where((named == 1) & (named_before == 1), e, second)
            named_before += named
        named_s, _ = expand_words(word_ref[...], per_shard)
        s_top = jnp.max(s_log, axis=0, keepdims=True)
        e = jnp.exp(s_log - s_top)
        s_total = jnp.sum(e, axis=0, keepdims=True)
        s_rest = jnp.sum(jnp.where(named_s, 0.0, e), axis=0, keepdims=True)
        line = lax.broadcasted_iota(jnp.int32, (8, rows), 0)
        stats = jnp.zeros((8, rows), jnp.float32)
        for at, value in enumerate((t_top, t_total, t_rest, s_top, s_total, s_rest)):
            stats = jnp.where(line == at, value, stats)
        for part in range(rows // 128):
            spare_ref[part, :lanes, :] = first[:, part * 128 : (part + 1) * 128]
            spare_ref[part, lanes:, :] = second[:, part * 128 : (part + 1) * 128]
        core = slot_ref[2]
        for x in range(4):
            for y in range(4):
                to = jnp.where(core == 0, x, y)
                at = 8 * jnp.where(core == 0, y, x)
                for slot in range(2):
                    lines = pl.ds(pl.multiple_of(slot * 32 + at, 8), 8)
                    for part in range(rows // 128):
                        msg_ref[to, lines, part * 128 : (part + 1) * 128] = spare_ref[
                            part, pl.ds(slot * lanes + y * 32 + x, 8, stride=4), :
                        ]
            msg_ref[x, 64:72, :] = stats

    whole = pl.BlockSpec(memory_space=pltpu.VMEM)
    remote = pl.BlockSpec(memory_space=pltpu.HBM)
    return pl.pallas_call(
        kernel,
        in_specs=[pl.BlockSpec(memory_space=pltpu.SMEM)] + [whole] * (count + 2) + [remote] * 2,
        out_specs=[whole, whole],
        out_shape=[
            jax.ShapeDtypeStruct((4, 72, rows), jnp.float32),
            jax.ShapeDtypeStruct((cols, rows), jnp.float32),
        ],
        scratch_shapes=[
            pltpu.VMEM(teacher_head.shape, jnp.bfloat16),
            pltpu.VMEM(student_cols.shape, jnp.bfloat16),
            pltpu.VMEM((rows, 2 * cols), jnp.float32),
            pltpu.VMEM((rows, 2 * cols), jnp.float32),
            pltpu.VMEM((rows // 128, 2 * lanes, 128), jnp.float32),
            pltpu.SemaphoreType.DMA((t_steps,)),
            pltpu.SemaphoreType.DMA((s_steps,)),
        ],
        compiler_params=pltpu.CompilerParams(vmem_limit_bytes=48 * 1024 * 1024),
    )(slots, *halves, words, own_word, teacher_head, student_cols)


def expand_words(words, per_shard):
    shards = words.shape[0]
    tile = lax.broadcasted_iota(jnp.int32, (shards * per_shard, 1), 0)
    within = tile - per_shard * ((tile * 205) >> 10)
    wide = spread_blocks(words.astype(jnp.bfloat16), per_shard).astype(jnp.int32)
    named = (wide >> within) & 1
    before = wide & ((1 << within) - 1)
    return named == 1, before == 0


def spread_blocks(value, per_shard):
    shards = value.shape[0]
    tile = lax.broadcasted_iota(jnp.int32, (shards * per_shard, shards), 0)
    start = per_shard * lax.broadcasted_iota(jnp.int32, (shards * per_shard, shards), 1)
    chosen = ((tile >= start) & (tile < start + per_shard)).astype(jnp.float32).astype(jnp.bfloat16)
    return jnp.dot(chosen, value, preferred_element_type=jnp.float32)


def regroup(arrived):
    sources, _, rows = arrived.shape

    def kernel(in_ref, out_ref):
        stats = [in_ref[j, 64:72, :] for j in range(sources)]

        def common(at):
            tops = [s[at : at + 1] for s in stats]
            top = functools.reduce(jnp.maximum, tops)
            weights = [jnp.exp(t - top) for t in tops]
            total = sum(w * s[at + 1 : at + 2] for w, s in zip(weights, stats))
            rest = sum(w * s[at + 2 : at + 3] for w, s in zip(weights, stats))
            return weights, (top, total, rest)

        weights, teacher = common(0)
        _, student = common(3)
        line = lax.broadcasted_iota(jnp.int32, (8, rows), 0)
        sums = jnp.zeros((8, rows), jnp.float32)
        for at, value in enumerate(teacher + student):
            sums = jnp.where(line == at, value, sums)
        block = jnp.zeros((32, 8, rows), jnp.float32)
        for j in range(sources):
            for slot in range(2):
                e = in_ref[j, slot * 32 : (slot + 1) * 32, :] * weights[j]
                block = jnp.where((line == 2 * j + slot)[None], e[:, None, :], block)
        out_ref[:, :8, :] = block
        out_ref[:, 8:, :] = jnp.broadcast_to(sums[None], (32, 8, rows))

    return pl.pallas_call(
        kernel,
        out_shape=jax.ShapeDtypeStruct((32, 16, rows), jnp.float32),
        compiler_params=pltpu.CompilerParams(vmem_limit_bytes=48 * 1024 * 1024),
    )(arrived)


def spread_sources(value, core, per_shard):
    sources = value.shape[0]
    tile = lax.broadcasted_iota(jnp.int32, (sources * per_shard, 1), 0)
    arrival = lax.broadcasted_iota(jnp.int32, (1, sources), 1)
    place, chip = arrival >> 5, arrival & 31
    shard = jnp.where(core == 0, chip * 4 + place, (place * 8 + (chip & 7)) * 4 + (chip >> 3))
    chosen = (((tile * 205) >> 10) == shard).astype(jnp.float32).astype(jnp.bfloat16)
    return jnp.dot(chosen, value, preferred_element_type=jnp.float32)


def gradient(slots, words, logit, arrived, order, student_cols, per_shard):
    cols, rows = logit.shape
    ds = student_cols.shape[0]
    width = 512

    def kernel(slot_ref, word_ref, logit_ref, msg_ref, order_ref, w_hbm, out_ref, w_ref, w_sem):
        copies = fetch(w_hbm, width, w_ref, w_sem)

        def sums(at):
            top_each = msg_ref[:, at, :]
            top = jnp.max(top_each, axis=0, keepdims=True)
            weight = jnp.exp(top_each - top)
            total = jnp.sum(weight * msg_ref[:, at + 1, :], axis=0, keepdims=True)
            rest = jnp.sum(weight * msg_ref[:, at + 2, :], axis=0, keepdims=True)
            return top, weight, total, rest / total

        _, t_weight, t_total, t_mass = sums(8)
        s_top, _, s_total, s_mass = sums(11)
        scale = t_weight / t_total

        def arrived_prob(slot):
            parts = [msg_ref[:, 2 * j + slot, :] * scale for j in range(4)]
            prob = jnp.concatenate(parts, axis=0).astype(jnp.bfloat16)
            return spread_sources(prob, slot_ref[2], per_shard)

        named, is_first = expand_words(word_ref[...], per_shard)
        teacher = jnp.where(is_first, arrived_prob(0), arrived_prob(1))
        prob = jnp.exp(logit_ref[...] - s_top) / s_total
        kl = (
            jnp.where(named, prob - teacher, prob * (1.0 - t_mass / s_mass)) * loss_scale
        ).astype(jnp.bfloat16)
        kl = lax.dot_general(
            order_ref[...], kl, (((1,), (1,)), ((), ())), preferred_element_type=jnp.float32
        ).astype(jnp.bfloat16)
        for k in range(ds // width):
            span = slice(k * width, (k + 1) * width)
            copies[k].wait()
            out_ref[:, span] = lax.dot_general(
                kl, w_ref[span, :], (((1,), (1,)), ((), ())), preferred_element_type=jnp.float32
            ).astype(jnp.bfloat16)

    whole = pl.BlockSpec(memory_space=pltpu.VMEM)
    return pl.pallas_call(
        kernel,
        in_specs=[pl.BlockSpec(memory_space=pltpu.SMEM)]
        + [whole] * 4
        + [pl.BlockSpec(memory_space=pltpu.HBM)],
        out_specs=whole,
        out_shape=jax.ShapeDtypeStruct((rows, ds), jnp.bfloat16),
        scratch_shapes=[
            pltpu.VMEM(student_cols.shape, jnp.bfloat16),
            pltpu.SemaphoreType.DMA((ds // width,)),
        ],
        compiler_params=pltpu.CompilerParams(vmem_limit_bytes=48 * 1024 * 1024),
    )(slots, words, logit, arrived, order, student_cols)


def per_device(teacher_hidden, teacher_head, student_hidden, student_head, tiles):
    shards = lax.axis_size(LINE)
    shard_index = lax.axis_index(LINE)
    core = lax.axis_index("mesh")
    ds, tiles_all, lane_count = student_head.shape
    student_cols = student_head.reshape(ds, tiles_all * lane_count)
    per_shard = tiles_all // shards
    picks = tiles.shape[1]

    both = jnp.concatenate((teacher_hidden, student_hidden), axis=1)
    mine = lax.dynamic_slice_in_dim(both, 2 * core, 2, 0)
    gathered = spread(mine, LINES_Z)
    by_chip = tiles.reshape(NY, NZ, NX, 2, 2, picks)
    by_chip = lax.dynamic_index_in_dim(by_chip, core, 3, keepdims=False)
    tiles_t = jnp.where(
        core == 0, by_chip.transpose(4, 2, 0, 1, 3), by_chip.transpose(4, 0, 2, 1, 3)
    ).reshape(picks, 2 * shards)
    words = tile_words(tiles_t)
    last, after, opposite = across(gathered, 1), across(gathered, -1), across(gathered, 2)
    own = (
        jnp.concatenate((gathered, last), axis=0),
        jnp.concatenate((after, opposite), axis=0),
    )
    below_first = along(own[0], 1)
    above_first = along(own[1], -1)
    below_second = along(own[1], 1)
    above_second = along(own[0], -1)
    below_first, above_first, words = lax.optimization_barrier((below_first, above_first, words))
    far = (along(below_first, 1), along(above_first, -1))
    halves = own + (above_second, above_first) + far + (below_first, below_second)
    own_word = lax.dynamic_slice_in_dim(words, shard_index, 1, 0)

    x, y = lax.axis_index("dp"), lax.axis_index("vocab") // NZ
    slots = jnp.stack((jnp.where(core == 0, x, y), jnp.where(core == 0, y, x), core))
    message, logit = logits_and_message(
        slots, halves, teacher_head, student_cols, words, own_word, per_shard
    )
    near = exchange(message, LINES_X[0] + LINES_Y[1])
    arrived = exchange(regroup(near), PLANES_YZ + PLANES_XZ)

    order = lax.dynamic_index_in_dim(
        jnp.asarray(row_orders(), jnp.bfloat16), core, 0, keepdims=False
    )
    partial = gradient(slots, words, logit, arrived, order, student_cols, per_shard)

    rows = partial.shape[0]
    near = exchange(partial, LINES_X[0] + LINES_Y[1])
    near = jnp.sum(near.reshape(NX, rows // NX, ds).astype(jnp.float32), axis=0)
    far = exchange(near.astype(jnp.bfloat16), PLANES_YZ + PLANES_XZ)
    summed = jnp.sum(far.reshape(NY * NZ, 2, ds).astype(jnp.float32), axis=0)
    return lax.ppermute(summed.astype(jnp.bfloat16), WHOLE, last_hop())


def solution(mesh):
    return jax.shard_map(
        per_device,
        mesh=mesh,
        in_specs=(
            P(("vocab", "dp"), None),
            P(None, ("vocab", "dp")),
            P(("vocab", "dp"), None),
            P(None, None, ("vocab", "dp")),
            P(),
        ),
        out_specs=P(("mesh", "vocab", "dp"), None),
        check_vma=False,
    )
```

```python
import functools

import jax
import jax.numpy as jnp
import numpy as np
from jax import lax
from jax.experimental import pallas as pl
from jax.experimental.pallas import tpu as pltpu
from jax.sharding import PartitionSpec as P

loss_scale = 1024.0
NX, NY, NZ = 4, 4, 8
LINE = ("vocab", "dp")
WHOLE = ("mesh", "vocab", "dp")
HALF = NX * NY * NZ


def device(m, x, y, z):
    return m * HALF + (y * NZ + z) * NX + x


LINES_Z = [
    [device(m, x, y, z) for z in range(NZ)]
    for m in range(2)
    for x in range(NX)
    for y in range(NY)
]
LINES_X = [
    [[device(m, x, y, z) for x in range(NX)] for y in range(NY) for z in range(NZ)]
    for m in range(2)
]
LINES_Y = [
    [[device(m, x, y, z) for y in range(NY)] for x in range(NX) for z in range(NZ)]
    for m in range(2)
]
PLANES_YZ = [
    [device(0, x, y, z) for y in range(NY) for z in range(NZ)] for x in range(NX)
]
PLANES_XZ = [
    [device(1, x, y, z) for x in range(NX) for z in range(NZ)] for y in range(NY)
]


def exchange(value, groups):
    return lax.all_to_all(value, WHOLE, 0, 0, tiled=True, axis_index_groups=groups)


def spread(value, groups):
    count = len(groups[0])
    rows, width = value.shape
    copies = jnp.broadcast_to(value[None], (count, rows, width)).reshape(count * rows, width)
    return exchange(copies, groups)


def step(value, axes, by):
    sizes = {"x": NX, "y": NY}
    pairs = []
    for m in range(2):
        for x in range(NX):
            for y in range(NY):
                for z in range(NZ):
                    to = {"x": x, "y": y}
                    to[axes[m]] = (to[axes[m]] + by) % sizes[axes[m]]
                    pairs.append((device(m, x, y, z), device(m, to["x"], to["y"], z)))
    return lax.ppermute(value, WHOLE, pairs)


def across(value, by):
    return step(value, ("y", "x"), by)


def along(value, by):
    return step(value, ("x", "y"), by)


def home(x, y, z):
    x1, x0 = x // 2, x % 2
    y1, y0 = y // 2, y % 2
    z2, z1, z0 = z // 4, (z // 2) % 2, z % 2
    return 2 * x0 + y1, 2 * y0 + z2, 4 * z1 + 2 * z0 + x1


def row_orders():
    orders = np.zeros((2, 2 * HALF, 2 * HALF), np.float32)
    for x in range(NX):
        for y in range(NY):
            for z in range(NZ):
                hx, hy, hz = home(x, y, z)
                for b in range(2):
                    orders[0, ((hx * NY + hy) * NZ + hz) * 2 + b, ((x * NY + y) * NZ + z) * 2 + b] = 1
                    orders[1, ((hy * NX + hx) * NZ + hz) * 2 + b, ((y * NX + x) * NZ + z) * 2 + b] = 1
    return orders


def last_hop():
    pairs = []
    for m in range(2):
        for x in range(NX):
            for y in range(NY):
                for z in range(NZ):
                    pairs.append(
                        (device(m, x, y, z), device(x % 2, 2 * (x // 2) + m, y, z))
                    )
    return pairs


def tile_words(tiles_t):
    count, rows = tiles_t.shape

    def kernel(tiles_ref, word_ref):
        block = lax.broadcasted_iota(jnp.int32, (count, rows), 0)

        def step(k, word):
            tile = tiles_ref[pl.ds(k, 1), :]
            own = (tile * 205) >> 10
            bit = 1 << (tile - 5 * own)
            return word + jnp.where(block == own, bit, 0)

        word_ref[...] = lax.fori_loop(0, count, step, jnp.zeros((count, rows), jnp.int32), unroll=8)

    return pl.pallas_call(
        kernel,
        out_shape=jax.ShapeDtypeStruct((count, rows), jnp.int32),
        cost_estimate=pl.CostEstimate(
            flops=16 * count * count * rows, bytes_accessed=8 * count * rows, transcendentals=0
        ),
    )(tiles_t)


def fetch(source, chunk, buffer, semaphores):
    copies = []
    for k in range(source.shape[0] // chunk):
        rows = pl.ds(k * chunk, chunk)
        copies.append(pltpu.make_async_copy(source.at[rows], buffer.at[rows], semaphores.at[k]))
        copies[-1].start()
    return copies


DEPTH = 512
EARLY_LIMIT = 32 * 1024 * 1024
GRADIENT_LIMIT = 48 * 1024 * 1024
LATE_LIMIT = 16 * 1024 * 1024


def add_logits(half_refs, t_ref, s_ref, out_ref, t_copies=(), s_copies=()):
    cols = t_ref.shape[1]
    at = 0
    for copies, ref, col in ((t_copies, t_ref, slice(0, cols)), (s_copies, s_ref, slice(cols, 2 * cols))):
        for k in range(ref.shape[0] // DEPTH):
            left = jnp.concatenate([half[:, at : at + DEPTH] for half in half_refs], axis=0)
            if copies:
                copies[k].wait()
            term = jnp.dot(
                left, ref[k * DEPTH : (k + 1) * DEPTH, :], preferred_element_type=jnp.float32
            )
            if k == 0:
                out_ref[:, col] = term
            else:
                out_ref[:, col] += term
            at += DEPTH


def logit_cost(rows, teacher_head, student_cols):
    elements = teacher_head.size + student_cols.size
    return pl.CostEstimate(
        flops=2 * rows * elements, bytes_accessed=2 * elements, transcendentals=0
    )


def early_logits(halves, teacher_head, student_cols):
    count = len(halves)
    rows = count * halves[0].shape[0]
    cols = teacher_head.shape[1]

    def kernel(*refs):
        t_hbm, s_hbm, out_ref, t_ref, s_ref, t_sem, s_sem = refs[count:]
        t_copies = fetch(t_hbm, DEPTH, t_ref, t_sem)
        s_copies = fetch(s_hbm, DEPTH, s_ref, s_sem)
        add_logits(refs[:count], t_ref, s_ref, out_ref, t_copies, s_copies)

    whole = pl.BlockSpec(memory_space=pltpu.VMEM)
    return pl.pallas_call(
        kernel,
        in_specs=[whole] * count + [pl.BlockSpec(memory_space=pltpu.HBM)] * 2,
        out_specs=[whole] * 3,
        out_shape=[
            jax.ShapeDtypeStruct((rows, 2 * cols), jnp.float32),
            jax.ShapeDtypeStruct(teacher_head.shape, teacher_head.dtype),
            jax.ShapeDtypeStruct(student_cols.shape, student_cols.dtype),
        ],
        scratch_shapes=[
            pltpu.SemaphoreType.DMA((teacher_head.shape[0] // DEPTH,)),
            pltpu.SemaphoreType.DMA((student_cols.shape[0] // DEPTH,)),
        ],
        cost_estimate=logit_cost(rows, teacher_head, student_cols),
        compiler_params=pltpu.CompilerParams(vmem_limit_bytes=EARLY_LIMIT),
    )(*halves, teacher_head, student_cols)


def logits_and_message(slots, early, halves, teacher_head, student_cols, words, own_word, per_shard):
    count = len(halves)
    half = halves[0].shape[0]
    rows = 2 * count * half
    block = half // 2
    cols = teacher_head.shape[1]
    lanes = cols // per_shard

    def kernel(slot_ref, early_ref, *refs):
        (
            word_ref, own_word_ref, t_ref, s_ref, msg_ref, logit_ref,
            late_ref, all_ref, spare_ref,
        ) = refs[count:]
        add_logits(refs[:count], t_ref, s_ref, late_ref)

        for source_ref, places in ((early_ref, (0, 1, 3, 6)), (late_ref, (2, 4, 5, 7))):
            for n, place in enumerate(places):
                for k in range(2):
                    third = lax.rem(slot_ref[0] + place // 2, 4)
                    second = lax.rem(slot_ref[1] + (0, 3, 1, 2)[2 * (place % 2) + k], 4)
                    at = pl.multiple_of((third * 4 + second) * block, block)
                    start = n * half + k * block
                    all_ref[pl.ds(at, block), :] = source_ref[start : start + block, :]

        word = own_word_ref[...]
        t_log = all_ref[:, :cols].T
        s_log = all_ref[:, cols:].T
        logit_ref[...] = s_log
        t_top = jnp.max(t_log, axis=0, keepdims=True)
        named_before = jnp.zeros((1, rows), jnp.int32)
        t_total = jnp.zeros((1, rows), jnp.float32)
        t_rest = jnp.zeros((1, rows), jnp.float32)
        first = jnp.zeros((lanes, rows), jnp.float32)
        second = jnp.zeros((lanes, rows), jnp.float32)
        for t in range(per_shard):
            e = jnp.exp(t_log[t * lanes : (t + 1) * lanes] - t_top)
            part = jnp.sum(e, axis=0, keepdims=True)
            named = (word >> t) & 1
            t_total += part
            t_rest += jnp.where(named == 0, part, 0.0)
            first = jnp.where((named == 1) & (named_before == 0), e, first)
            second = jnp.where((named == 1) & (named_before == 1), e, second)
            named_before += named
        named_s, _ = expand_words(word_ref[...], per_shard)
        s_top = jnp.max(s_log, axis=0, keepdims=True)
        e = jnp.exp(s_log - s_top)
        s_total = jnp.sum(e, axis=0, keepdims=True)
        s_rest = jnp.sum(jnp.where(named_s, 0.0, e), axis=0, keepdims=True)
        line = lax.broadcasted_iota(jnp.int32, (8, rows), 0)
        stats = jnp.zeros((8, rows), jnp.float32)
        for at, value in enumerate((t_top, t_total, t_rest, s_top, s_total, s_rest)):
            stats = jnp.where(line == at, value, stats)
        for part in range(rows // 128):
            spare_ref[part, :lanes, :] = first[:, part * 128 : (part + 1) * 128]
            spare_ref[part, lanes:, :] = second[:, part * 128 : (part + 1) * 128]
        core = slot_ref[2]
        for x in range(4):
            for y in range(4):
                to = jnp.where(core == 0, x, y)
                at = 8 * jnp.where(core == 0, y, x)
                for slot in range(2):
                    lines = pl.ds(pl.multiple_of(slot * 32 + at, 8), 8)
                    for part in range(rows // 128):
                        msg_ref[to, lines, part * 128 : (part + 1) * 128] = spare_ref[
                            part, pl.ds(slot * lanes + y * 32 + x, 8, stride=4), :
                        ]
            msg_ref[x, 64:72, :] = stats

    whole = pl.BlockSpec(memory_space=pltpu.VMEM)
    return pl.pallas_call(
        kernel,
        in_specs=[pl.BlockSpec(memory_space=pltpu.SMEM)] + [whole] * (count + 5),
        out_specs=[whole, whole],
        out_shape=[
            jax.ShapeDtypeStruct((4, 72, rows), jnp.float32),
            jax.ShapeDtypeStruct((cols, rows), jnp.float32),
        ],
        scratch_shapes=[
            pltpu.VMEM((rows // 2, 2 * cols), jnp.float32),
            pltpu.VMEM((rows, 2 * cols), jnp.float32),
            pltpu.VMEM((rows // 128, 2 * lanes, 128), jnp.float32),
        ],
        cost_estimate=logit_cost(rows // 2, teacher_head, student_cols),
        compiler_params=pltpu.CompilerParams(vmem_limit_bytes=LATE_LIMIT),
    )(slots, early, *halves, words, own_word, teacher_head, student_cols)


def expand_words(words, per_shard):
    shards = words.shape[0]
    tile = lax.broadcasted_iota(jnp.int32, (shards * per_shard, 1), 0)
    within = tile - per_shard * ((tile * 205) >> 10)
    wide = spread_blocks(words.astype(jnp.bfloat16), per_shard).astype(jnp.int32)
    named = (wide >> within) & 1
    before = wide & ((1 << within) - 1)
    return named == 1, before == 0


def spread_blocks(value, per_shard):
    shards = value.shape[0]
    tile = lax.broadcasted_iota(jnp.int32, (shards * per_shard, shards), 0)
    start = per_shard * lax.broadcasted_iota(jnp.int32, (shards * per_shard, shards), 1)
    chosen = ((tile >= start) & (tile < start + per_shard)).astype(jnp.float32).astype(jnp.bfloat16)
    return jnp.dot(chosen, value, preferred_element_type=jnp.float32)


def regroup(arrived):
    sources, _, rows = arrived.shape

    def kernel(in_ref, out_ref):
        stats = [in_ref[j, 64:72, :] for j in range(sources)]

        def common(at):
            tops = [s[at : at + 1] for s in stats]
            top = functools.reduce(jnp.maximum, tops)
            weights = [jnp.exp(t - top) for t in tops]
            total = sum(w * s[at + 1 : at + 2] for w, s in zip(weights, stats))
            rest = sum(w * s[at + 2 : at + 3] for w, s in zip(weights, stats))
            return weights, (top, total, rest)

        weights, teacher = common(0)
        _, student = common(3)
        line = lax.broadcasted_iota(jnp.int32, (8, rows), 0)
        sums = jnp.zeros((8, rows), jnp.float32)
        for at, value in enumerate(teacher + student):
            sums = jnp.where(line == at, value, sums)
        block = jnp.zeros((32, 8, rows), jnp.float32)
        for j in range(sources):
            for slot in range(2):
                e = in_ref[j, slot * 32 : (slot + 1) * 32, :] * weights[j]
                block = jnp.where((line == 2 * j + slot)[None], e[:, None, :], block)
        out_ref[:, :8, :] = block
        out_ref[:, 8:, :] = jnp.broadcast_to(sums[None], (32, 8, rows))

    return pl.pallas_call(
        kernel,
        out_shape=jax.ShapeDtypeStruct((32, 16, rows), jnp.float32),
        compiler_params=pltpu.CompilerParams(vmem_limit_bytes=LATE_LIMIT),
    )(arrived)


def spread_sources(value, core, per_shard):
    sources = value.shape[0]
    tile = lax.broadcasted_iota(jnp.int32, (sources * per_shard, 1), 0)
    arrival = lax.broadcasted_iota(jnp.int32, (1, sources), 1)
    place, chip = arrival >> 5, arrival & 31
    shard = jnp.where(core == 0, chip * 4 + place, (place * 8 + (chip & 7)) * 4 + (chip >> 3))
    chosen = (((tile * 205) >> 10) == shard).astype(jnp.float32).astype(jnp.bfloat16)
    return jnp.dot(chosen, value, preferred_element_type=jnp.float32)


def gradient(slots, words, logit, arrived, order, student_cols, per_shard):
    cols, rows = logit.shape
    ds = student_cols.shape[0]
    width = 512
    block = rows // 4

    def kernel(slot_ref, word_ref, logit_ref, msg_ref, order_ref, w_hbm, *refs):
        out_refs, (kl_ref, near_ref, w_ref, w_sem) = refs[:4], refs[4:]
        copies = fetch(w_hbm, width, w_ref, w_sem)

        def sums(at):
            top_each = msg_ref[:, at, :]
            top = jnp.max(top_each, axis=0, keepdims=True)
            weight = jnp.exp(top_each - top)
            total = jnp.sum(weight * msg_ref[:, at + 1, :], axis=0, keepdims=True)
            rest = jnp.sum(weight * msg_ref[:, at + 2, :], axis=0, keepdims=True)
            return top, weight, total, rest / total

        _, t_weight, t_total, t_mass = sums(8)
        s_top, _, s_total, s_mass = sums(11)
        scale = t_weight / t_total

        def arrived_prob(slot):
            parts = [msg_ref[:, 2 * j + slot, :] * scale for j in range(4)]
            prob = jnp.concatenate(parts, axis=0).astype(jnp.bfloat16)
            return spread_sources(prob, slot_ref[2], per_shard)

        named, is_first = expand_words(word_ref[...], per_shard)
        teacher = jnp.where(is_first, arrived_prob(0), arrived_prob(1))
        prob = jnp.exp(logit_ref[...] - s_top) / s_total
        kl = (
            jnp.where(named, prob - teacher, prob * (1.0 - t_mass / s_mass)) * loss_scale
        ).astype(jnp.bfloat16)
        kl_ref[...] = lax.dot_general(
            order_ref[...], kl, (((1,), (1,)), ((), ())), preferred_element_type=jnp.float32
        ).astype(jnp.bfloat16)
        for n in range(4):
            at = pl.multiple_of(lax.rem(slot_ref[0] + n, 4) * block, block)
            near_ref[n * block : (n + 1) * block, :] = kl_ref[pl.ds(at, block), :]
        for k in range(ds // width):
            span = slice(k * width, (k + 1) * width)
            copies[k].wait()
            term = lax.dot_general(
                near_ref[...],
                w_ref[span, :],
                (((1,), (1,)), ((), ())),
                preferred_element_type=jnp.float32,
            ).astype(jnp.bfloat16)
            for n in range(4):
                out_refs[n][:, span] = term[n * block : (n + 1) * block, :]

    whole = pl.BlockSpec(memory_space=pltpu.VMEM)
    return pl.pallas_call(
        kernel,
        in_specs=[pl.BlockSpec(memory_space=pltpu.SMEM)]
        + [whole] * 4
        + [pl.BlockSpec(memory_space=pltpu.HBM)],
        out_specs=[whole] * 4,
        out_shape=[jax.ShapeDtypeStruct((block, ds), jnp.bfloat16)] * 4,
        scratch_shapes=[
            pltpu.VMEM((rows, cols), jnp.bfloat16),
            pltpu.VMEM((rows, cols), jnp.bfloat16),
            pltpu.VMEM(student_cols.shape, jnp.bfloat16),
            pltpu.SemaphoreType.DMA((ds // width,)),
        ],
        compiler_params=pltpu.CompilerParams(vmem_limit_bytes=GRADIENT_LIMIT),
    )(slots, words, logit, arrived, order, student_cols)


def per_device(teacher_hidden, teacher_head, student_hidden, student_head, tiles):
    shards = lax.axis_size(LINE)
    shard_index = lax.axis_index(LINE)
    core = lax.axis_index("mesh")
    ds, tiles_all, lane_count = student_head.shape
    student_cols = student_head.reshape(ds, tiles_all * lane_count)
    per_shard = tiles_all // shards
    picks = tiles.shape[1]

    both = jnp.concatenate((teacher_hidden, student_hidden), axis=1)
    mine = lax.dynamic_slice_in_dim(both, 2 * core, 2, 0)
    gathered = spread(mine, LINES_Z)
    by_chip = tiles.reshape(NY, NZ, NX, 2, 2, picks)
    by_chip = lax.dynamic_index_in_dim(by_chip, core, 3, keepdims=False)
    tiles_t = jnp.where(
        core == 0, by_chip.transpose(4, 2, 0, 1, 3), by_chip.transpose(4, 0, 2, 1, 3)
    ).reshape(picks, 2 * shards)
    words = tile_words(tiles_t)
    last, after, opposite = across(gathered, 1), across(gathered, -1), across(gathered, 2)
    opposite, words = lax.optimization_barrier((opposite, words))
    own = (
        jnp.concatenate((gathered, last), axis=0),
        jnp.concatenate((after, opposite), axis=0),
    )
    below_first = along(own[0], 1)
    above_first = along(own[1], -1)
    below_second = along(own[1], 1)
    above_second = along(own[0], -1)
    far = (along(below_first, 1), along(above_first, -1))
    early, teacher_near, student_near = early_logits(own + (above_first, below_first), teacher_head, student_cols)
    late = (above_second,) + far + (below_second,)
    own_word = lax.dynamic_slice_in_dim(words, shard_index, 1, 0)

    x, y = lax.axis_index("dp"), lax.axis_index("vocab") // NZ
    slots = jnp.stack((jnp.where(core == 0, x, y), jnp.where(core == 0, y, x), core))
    message, logit = logits_and_message(
        slots, early, late, teacher_near, student_near, words, own_word, per_shard
    )
    near = exchange(message, LINES_X[0] + LINES_Y[1])
    arrived = exchange(regroup(near), PLANES_YZ + PLANES_XZ)

    order = lax.dynamic_index_in_dim(
        jnp.asarray(row_orders(), jnp.bfloat16), core, 0, keepdims=False
    )
    kept, after_chip, opposite_chip, last_chip = gradient(
        slots, words, logit, arrived, order, student_cols, per_shard
    )
    terms = (kept, along(opposite_chip, 2), along(after_chip, 1), along(last_chip, -1))
    near = sum(term.astype(jnp.float32) for term in terms)
    far = exchange(near.astype(jnp.bfloat16), PLANES_YZ + PLANES_XZ)
    summed = jnp.sum(far.reshape(NY * NZ, 2, ds).astype(jnp.float32), axis=0)
    return lax.ppermute(summed.astype(jnp.bfloat16), WHOLE, last_hop())


def solution(mesh):
    return jax.shard_map(
        per_device,
        mesh=mesh,
        in_specs=(
            P(("vocab", "dp"), None),
            P(None, ("vocab", "dp")),
            P(("vocab", "dp"), None),
            P(None, None, ("vocab", "dp")),
            P(),
        ),
        out_specs=P(("mesh", "vocab", "dp"), None),
        check_vma=False,
    )
```

```python
import functools

import jax
import jax.numpy as jnp
import numpy as np
from jax import lax
from jax.experimental import pallas as pl
from jax.experimental.pallas import tpu as pltpu
from jax.sharding import PartitionSpec as P

loss_scale = 1024.0
NX, NY, NZ = 4, 4, 8
LINE = ("vocab", "dp")
WHOLE = ("mesh", "vocab", "dp")
HALF = NX * NY * NZ


def device(m, x, y, z):
    return m * HALF + (y * NZ + z) * NX + x


LINES_Z = [
    [device(m, x, y, z) for z in range(NZ)]
    for m in range(2)
    for x in range(NX)
    for y in range(NY)
]
LINES_X = [
    [[device(m, x, y, z) for x in range(NX)] for y in range(NY) for z in range(NZ)]
    for m in range(2)
]
LINES_Y = [
    [[device(m, x, y, z) for y in range(NY)] for x in range(NX) for z in range(NZ)]
    for m in range(2)
]
PLANES_YZ = [
    [device(0, x, y, z) for y in range(NY) for z in range(NZ)] for x in range(NX)
]
PLANES_XZ = [
    [device(1, x, y, z) for x in range(NX) for z in range(NZ)] for y in range(NY)
]


def exchange(value, groups):
    return lax.all_to_all(value, WHOLE, 0, 0, tiled=True, axis_index_groups=groups)


def spread(value, groups):
    count = len(groups[0])
    rows, width = value.shape
    copies = jnp.broadcast_to(value[None], (count, rows, width)).reshape(count * rows, width)
    return exchange(copies, groups)


def step(value, axes, by):
    sizes = {"x": NX, "y": NY}
    pairs = []
    for m in range(2):
        for x in range(NX):
            for y in range(NY):
                for z in range(NZ):
                    to = {"x": x, "y": y}
                    to[axes[m]] = (to[axes[m]] + by) % sizes[axes[m]]
                    pairs.append((device(m, x, y, z), device(m, to["x"], to["y"], z)))
    return lax.ppermute(value, WHOLE, pairs)


def across(value, by):
    return step(value, ("y", "x"), by)


def along(value, by):
    return step(value, ("x", "y"), by)


def home(x, y, z):
    x1, x0 = x // 2, x % 2
    y1, y0 = y // 2, y % 2
    z2, z1, z0 = z // 4, (z // 2) % 2, z % 2
    return 2 * x0 + y1, 2 * y0 + z2, 4 * z1 + 2 * z0 + x1


def row_orders():
    orders = np.zeros((2, 2 * HALF, 2 * HALF), np.float32)
    for x in range(NX):
        for y in range(NY):
            for z in range(NZ):
                hx, hy, hz = home(x, y, z)
                for b in range(2):
                    orders[0, ((hx * NY + hy) * NZ + hz) * 2 + b, ((x * NY + y) * NZ + z) * 2 + b] = 1
                    orders[1, ((hy * NX + hx) * NZ + hz) * 2 + b, ((y * NX + x) * NZ + z) * 2 + b] = 1
    return orders


def last_hop():
    pairs = []
    for m in range(2):
        for x in range(NX):
            for y in range(NY):
                for z in range(NZ):
                    pairs.append(
                        (device(m, x, y, z), device(x % 2, 2 * (x // 2) + m, y, z))
                    )
    return pairs


def tile_words(tiles_t):
    count, rows = tiles_t.shape

    def kernel(tiles_ref, word_ref):
        block = lax.broadcasted_iota(jnp.int32, (count, rows), 0)

        def step(k, word):
            tile = tiles_ref[pl.ds(k, 1), :]
            own = (tile * 205) >> 10
            bit = 1 << (tile - 5 * own)
            return word + jnp.where(block == own, bit, 0)

        word_ref[...] = lax.fori_loop(0, count, step, jnp.zeros((count, rows), jnp.int32), unroll=8)

    return pl.pallas_call(
        kernel,
        out_shape=jax.ShapeDtypeStruct((count, rows), jnp.int32),
        cost_estimate=pl.CostEstimate(
            flops=16 * count * count * rows, bytes_accessed=8 * count * rows, transcendentals=0
        ),
    )(tiles_t)


def fetch(source, chunk, buffer, semaphores):
    copies = []
    for k in range(source.shape[0] // chunk):
        rows = pl.ds(k * chunk, chunk)
        copies.append(pltpu.make_async_copy(source.at[rows], buffer.at[rows], semaphores.at[k]))
        copies[-1].start()
    return copies


DEPTH = 512
EARLY_LIMIT = 32 * 1024 * 1024
GRADIENT_LIMIT = 48 * 1024 * 1024
LATE_LIMIT = 16 * 1024 * 1024


def add_logits(half_refs, t_ref, s_ref, out_ref, t_copies=(), s_copies=()):
    cols = t_ref.shape[1]
    at = 0
    for copies, ref, col in ((t_copies, t_ref, slice(0, cols)), (s_copies, s_ref, slice(cols, 2 * cols))):
        for k in range(ref.shape[0] // DEPTH):
            left = jnp.concatenate([half[:, at : at + DEPTH] for half in half_refs], axis=0)
            if copies:
                copies[k].wait()
            term = jnp.dot(
                left, ref[k * DEPTH : (k + 1) * DEPTH, :], preferred_element_type=jnp.float32
            )
            if k == 0:
                out_ref[:, col] = term
            else:
                out_ref[:, col] += term
            at += DEPTH


def logit_cost(rows, teacher_head, student_cols):
    elements = teacher_head.size + student_cols.size
    return pl.CostEstimate(
        flops=2 * rows * elements, bytes_accessed=2 * elements, transcendentals=0
    )


def early_logits(halves, teacher_head, student_cols):
    count = len(halves)
    rows = count * halves[0].shape[0]
    cols = teacher_head.shape[1]

    def kernel(*refs):
        t_hbm, s_hbm, out_ref, t_ref, s_ref, t_sem, s_sem = refs[count:]
        t_copies = fetch(t_hbm, DEPTH, t_ref, t_sem)
        s_copies = fetch(s_hbm, DEPTH, s_ref, s_sem)
        add_logits(refs[:count], t_ref, s_ref, out_ref, t_copies, s_copies)

    whole = pl.BlockSpec(memory_space=pltpu.VMEM)
    return pl.pallas_call(
        kernel,
        in_specs=[whole] * count + [pl.BlockSpec(memory_space=pltpu.HBM)] * 2,
        out_specs=[whole] * 3,
        out_shape=[
            jax.ShapeDtypeStruct((rows, 2 * cols), jnp.float32),
            jax.ShapeDtypeStruct(teacher_head.shape, teacher_head.dtype),
            jax.ShapeDtypeStruct(student_cols.shape, student_cols.dtype),
        ],
        scratch_shapes=[
            pltpu.SemaphoreType.DMA((teacher_head.shape[0] // DEPTH,)),
            pltpu.SemaphoreType.DMA((student_cols.shape[0] // DEPTH,)),
        ],
        cost_estimate=logit_cost(rows, teacher_head, student_cols),
        compiler_params=pltpu.CompilerParams(vmem_limit_bytes=EARLY_LIMIT),
    )(*halves, teacher_head, student_cols)


def logits_and_message(slots, early, halves, teacher_head, student_cols, words, own_word, per_shard):
    count = len(halves)
    half = halves[0].shape[0]
    rows = early.shape[0] + count * half
    block = half // 2
    cols = teacher_head.shape[1]
    lanes = cols // per_shard

    def kernel(slot_ref, early_ref, *refs):
        (
            word_ref, own_word_ref, t_ref, s_ref, *msg_refs, logit_ref,
            late_ref, all_ref, spare_ref,
        ) = refs[count:]
        add_logits(refs[:count], t_ref, s_ref, late_ref)

        for source_ref, places in ((early_ref, (0, 1, 3, 6)), (late_ref, (2, 4, 5, 7))):
            for n, place in enumerate(places):
                for k in range(2):
                    third = lax.rem(slot_ref[0] + place // 2, 4)
                    second = lax.rem(slot_ref[1] + (0, 3, 1, 2)[2 * (place % 2) + k], 4)
                    at = pl.multiple_of((third * 4 + second) * block, block)
                    start = n * half + k * block
                    all_ref[pl.ds(at, block), :] = source_ref[start : start + block, :]

        word = own_word_ref[...]
        t_log = all_ref[:, :cols].T
        s_log = all_ref[:, cols:].T
        logit_ref[...] = s_log
        t_top = jnp.max(t_log, axis=0, keepdims=True)
        named_before = jnp.zeros((1, rows), jnp.int32)
        t_total = jnp.zeros((1, rows), jnp.float32)
        t_rest = jnp.zeros((1, rows), jnp.float32)
        first = jnp.zeros((lanes, rows), jnp.float32)
        second = jnp.zeros((lanes, rows), jnp.float32)
        for t in range(per_shard):
            e = jnp.exp(t_log[t * lanes : (t + 1) * lanes] - t_top)
            part = jnp.sum(e, axis=0, keepdims=True)
            named = (word >> t) & 1
            t_total += part
            t_rest += jnp.where(named == 0, part, 0.0)
            first = jnp.where((named == 1) & (named_before == 0), e, first)
            second = jnp.where((named == 1) & (named_before == 1), e, second)
            named_before += named
        named_s, _ = expand_words(word_ref[...], per_shard)
        s_top = jnp.max(s_log, axis=0, keepdims=True)
        e = jnp.exp(s_log - s_top)
        s_total = jnp.sum(e, axis=0, keepdims=True)
        s_rest = jnp.sum(jnp.where(named_s, 0.0, e), axis=0, keepdims=True)
        line = lax.broadcasted_iota(jnp.int32, (8, rows), 0)
        stats = jnp.zeros((8, rows), jnp.float32)
        for at, value in enumerate((t_top, t_total, t_rest, s_top, s_total, s_rest)):
            stats = jnp.where(line == at, value, stats)
        for part in range(rows // 128):
            spare_ref[part, :lanes, :] = first[:, part * 128 : (part + 1) * 128]
            spare_ref[part, lanes:, :] = second[:, part * 128 : (part + 1) * 128]
        for n in range(4):
            to = lax.rem(slot_ref[0] + n, 4)
            for r in range(4):
                x = jnp.where(slot_ref[2] == 0, to, r)
                y = jnp.where(slot_ref[2] == 0, r, to)
                for slot in range(2):
                    for part in range(rows // 128):
                        msg_refs[n][
                            slot * 32 + 8 * r : slot * 32 + 8 * r + 8, part * 128 : (part + 1) * 128
                        ] = spare_ref[part, pl.ds(slot * lanes + y * 32 + x, 8, stride=4), :]
            msg_refs[n][64:72, :] = stats

    whole = pl.BlockSpec(memory_space=pltpu.VMEM)
    return pl.pallas_call(
        kernel,
        in_specs=[pl.BlockSpec(memory_space=pltpu.SMEM)] + [whole] * (count + 5),
        out_specs=[whole] * 5,
        out_shape=[jax.ShapeDtypeStruct((72, rows), jnp.float32)] * 4
        + [jax.ShapeDtypeStruct((cols, rows), jnp.float32)],
        scratch_shapes=[
            pltpu.VMEM((count * half, 2 * cols), jnp.float32),
            pltpu.VMEM((rows, 2 * cols), jnp.float32),
            pltpu.VMEM((rows // 128, 2 * lanes, 128), jnp.float32),
        ],
        cost_estimate=logit_cost(count * half, teacher_head, student_cols),
        compiler_params=pltpu.CompilerParams(vmem_limit_bytes=LATE_LIMIT),
    )(slots, early, *halves, words, own_word, teacher_head, student_cols)


def expand_words(words, per_shard):
    shards = words.shape[0]
    tile = lax.broadcasted_iota(jnp.int32, (shards * per_shard, 1), 0)
    within = tile - per_shard * ((tile * 205) >> 10)
    wide = spread_blocks(words.astype(jnp.bfloat16), per_shard).astype(jnp.int32)
    named = (wide >> within) & 1
    before = wide & ((1 << within) - 1)
    return named == 1, before == 0


def spread_blocks(value, per_shard):
    shards = value.shape[0]
    tile = lax.broadcasted_iota(jnp.int32, (shards * per_shard, shards), 0)
    start = per_shard * lax.broadcasted_iota(jnp.int32, (shards * per_shard, shards), 1)
    chosen = ((tile >= start) & (tile < start + per_shard)).astype(jnp.float32).astype(jnp.bfloat16)
    return jnp.dot(chosen, value, preferred_element_type=jnp.float32)


def regroup(arrived):
    sources = len(arrived)
    rows = arrived[0].shape[1]

    def kernel(*refs):
        in_refs, out_ref = refs[:sources], refs[sources]
        stats = [ref[64:72, :] for ref in in_refs]

        def common(at):
            tops = [s[at : at + 1] for s in stats]
            top = functools.reduce(jnp.maximum, tops)
            weights = [jnp.exp(t - top) for t in tops]
            total = sum(w * s[at + 1 : at + 2] for w, s in zip(weights, stats))
            rest = sum(w * s[at + 2 : at + 3] for w, s in zip(weights, stats))
            return weights, (top, total, rest)

        weights, teacher = common(0)
        _, student = common(3)
        line = lax.broadcasted_iota(jnp.int32, (8, rows), 0)
        sums = jnp.zeros((8, rows), jnp.float32)
        for at, value in enumerate(teacher + student):
            sums = jnp.where(line == at, value, sums)
        block = jnp.zeros((32, 8, rows), jnp.float32)
        for j in range(sources):
            for slot in range(2):
                e = in_refs[j][slot * 32 : (slot + 1) * 32, :] * weights[j]
                block = jnp.where((line == 2 * j + slot)[None], e[:, None, :], block)
        out_ref[:, :8, :] = block
        out_ref[:, 8:, :] = jnp.broadcast_to(sums[None], (32, 8, rows))

    return pl.pallas_call(
        kernel,
        out_shape=jax.ShapeDtypeStruct((32, 16, rows), jnp.float32),
        compiler_params=pltpu.CompilerParams(vmem_limit_bytes=LATE_LIMIT),
    )(*arrived)


def spread_sources(value, slot_ref, per_shard):
    sources = value.shape[0]
    tile = lax.broadcasted_iota(jnp.int32, (sources * per_shard, 1), 0)
    arrival = lax.broadcasted_iota(jnp.int32, (1, sources), 1)
    place, chip = (slot_ref[0] + 4 - (arrival >> 5)) & 3, arrival & 31
    shard = jnp.where(slot_ref[2] == 0, chip * 4 + place, (place * 8 + (chip & 7)) * 4 + (chip >> 3))
    chosen = (((tile * 205) >> 10) == shard).astype(jnp.float32).astype(jnp.bfloat16)
    return jnp.dot(chosen, value, preferred_element_type=jnp.float32)


def gradient(slots, words, logit, arrived, order, student_cols, per_shard):
    cols, rows = logit.shape
    ds = student_cols.shape[0]
    width = 512
    block = rows // 4

    def kernel(slot_ref, word_ref, logit_ref, msg_ref, order_ref, w_hbm, *refs):
        out_refs, (kl_ref, near_ref, w_ref, w_sem) = refs[:4], refs[4:]
        copies = fetch(w_hbm, width, w_ref, w_sem)

        def sums(at):
            top_each = msg_ref[:, at, :]
            top = jnp.max(top_each, axis=0, keepdims=True)
            weight = jnp.exp(top_each - top)
            total = jnp.sum(weight * msg_ref[:, at + 1, :], axis=0, keepdims=True)
            rest = jnp.sum(weight * msg_ref[:, at + 2, :], axis=0, keepdims=True)
            return top, weight, total, rest / total

        _, t_weight, t_total, t_mass = sums(8)
        s_top, _, s_total, s_mass = sums(11)
        scale = t_weight / t_total

        def arrived_prob(slot):
            parts = [msg_ref[:, 2 * j + slot, :] * scale for j in range(4)]
            prob = jnp.concatenate(parts, axis=0).astype(jnp.bfloat16)
            return spread_sources(prob, slot_ref, per_shard)

        named, is_first = expand_words(word_ref[...], per_shard)
        teacher = jnp.where(is_first, arrived_prob(0), arrived_prob(1))
        prob = jnp.exp(logit_ref[...] - s_top) * (1.0 / s_total)
        kl = (
            jnp.where(named, prob - teacher, prob * (1.0 - t_mass / s_mass)) * loss_scale
        ).astype(jnp.bfloat16)
        kl_ref[...] = lax.dot_general(
            order_ref[...], kl, (((1,), (1,)), ((), ())), preferred_element_type=jnp.float32
        ).astype(jnp.bfloat16)
        for n in range(4):
            at = pl.multiple_of(lax.rem(slot_ref[0] + n, 4) * block, block)
            near_ref[n * block : (n + 1) * block, :] = kl_ref[pl.ds(at, block), :]
        for k in range(ds // width):
            span = slice(k * width, (k + 1) * width)
            copies[k].wait()
            term = lax.dot_general(
                near_ref[...],
                w_ref[span, :],
                (((1,), (1,)), ((), ())),
                preferred_element_type=jnp.float32,
            ).astype(jnp.bfloat16)
            for n in range(4):
                out_refs[n][:, span] = term[n * block : (n + 1) * block, :]

    whole = pl.BlockSpec(memory_space=pltpu.VMEM)
    return pl.pallas_call(
        kernel,
        in_specs=[pl.BlockSpec(memory_space=pltpu.SMEM)]
        + [whole] * 4
        + [pl.BlockSpec(memory_space=pltpu.HBM)],
        out_specs=[whole] * 4,
        out_shape=[jax.ShapeDtypeStruct((block, ds), jnp.bfloat16)] * 4,
        scratch_shapes=[
            pltpu.VMEM((rows, cols), jnp.bfloat16),
            pltpu.VMEM((rows, cols), jnp.bfloat16),
            pltpu.VMEM(student_cols.shape, jnp.bfloat16),
            pltpu.SemaphoreType.DMA((ds // width,)),
        ],
        compiler_params=pltpu.CompilerParams(vmem_limit_bytes=GRADIENT_LIMIT),
    )(slots, words, logit, arrived, order, student_cols)


def per_device(teacher_hidden, teacher_head, student_hidden, student_head, tiles):
    shards = lax.axis_size(LINE)
    shard_index = lax.axis_index(LINE)
    core = lax.axis_index("mesh")
    ds, tiles_all, lane_count = student_head.shape
    student_cols = student_head.reshape(ds, tiles_all * lane_count)
    per_shard = tiles_all // shards
    picks = tiles.shape[1]

    both = jnp.concatenate((teacher_hidden, student_hidden), axis=1)
    mine = lax.dynamic_slice_in_dim(both, 2 * core, 2, 0)
    gathered = spread(mine, LINES_Z)
    by_chip = tiles.reshape(NY, NZ, NX, 2, 2, picks)
    by_chip = lax.dynamic_index_in_dim(by_chip, core, 3, keepdims=False)
    tiles_t = jnp.where(
        core == 0, by_chip.transpose(4, 2, 0, 1, 3), by_chip.transpose(4, 0, 2, 1, 3)
    ).reshape(picks, 2 * shards)
    words = tile_words(tiles_t)
    last, after, opposite = across(gathered, 1), across(gathered, -1), across(gathered, 2)
    opposite, words = lax.optimization_barrier((opposite, words))
    own = (
        jnp.concatenate((gathered, last), axis=0),
        jnp.concatenate((after, opposite), axis=0),
    )
    below_first = along(own[0], 1)
    above_first = along(own[1], -1)
    below_second = along(own[1], 1)
    above_second = along(own[0], -1)
    far = (along(below_first, 1), along(above_first, -1))
    early, teacher_near, student_near = early_logits(
        own + (above_first, below_first), teacher_head, student_cols
    )
    late = (above_second,) + far + (below_second,)
    own_word = lax.dynamic_slice_in_dim(words, shard_index, 1, 0)

    x, y = lax.axis_index("dp"), lax.axis_index("vocab") // NZ
    slots = jnp.stack((jnp.where(core == 0, x, y), jnp.where(core == 0, y, x), core))
    *message, logit = logits_and_message(
        slots, early, late, teacher_near, student_near, words, own_word, per_shard
    )
    near = (
        message[0], along(message[1], 1), along(message[2], 2), along(message[3], -1),
    )
    arrived = exchange(regroup(near), PLANES_YZ + PLANES_XZ)

    order = lax.dynamic_index_in_dim(
        jnp.asarray(row_orders(), jnp.bfloat16), core, 0, keepdims=False
    )
    kept, after_chip, opposite_chip, last_chip = gradient(
        slots, words, logit, arrived, order, student_cols, per_shard
    )
    terms = (kept, along(opposite_chip, 2), along(after_chip, 1), along(last_chip, -1))
    near = sum(term.astype(jnp.float32) for term in terms)
    far = exchange(near.astype(jnp.bfloat16), PLANES_YZ + PLANES_XZ)
    summed = jnp.sum(far.reshape(NY * NZ, 2, ds).astype(jnp.float32), axis=0)
    return lax.ppermute(summed.astype(jnp.bfloat16), WHOLE, last_hop())


def solution(mesh):
    return jax.shard_map(
        per_device,
        mesh=mesh,
        in_specs=(
            P(("vocab", "dp"), None),
            P(None, ("vocab", "dp")),
            P(("vocab", "dp"), None),
            P(None, None, ("vocab", "dp")),
            P(),
        ),
        out_specs=P(("mesh", "vocab", "dp"), None),
        check_vma=False,
    )
```

```python
import functools

import jax
import jax.numpy as jnp
import numpy as np
from jax import lax
from jax.experimental import pallas as pl
from jax.experimental.pallas import tpu as pltpu
from jax.sharding import PartitionSpec as P

loss_scale = 1024.0
NX, NY, NZ = 4, 4, 8
LINE = ("vocab", "dp")
WHOLE = ("mesh", "vocab", "dp")
HALF = NX * NY * NZ


def device(m, x, y, z):
    return m * HALF + (y * NZ + z) * NX + x


LINES_Z = [
    [device(m, x, y, z) for z in range(NZ)]
    for m in range(2)
    for x in range(NX)
    for y in range(NY)
]
LINES_X = [
    [[device(m, x, y, z) for x in range(NX)] for y in range(NY) for z in range(NZ)]
    for m in range(2)
]
LINES_Y = [
    [[device(m, x, y, z) for y in range(NY)] for x in range(NX) for z in range(NZ)]
    for m in range(2)
]
PLANES_YZ = [
    [device(0, x, y, z) for y in range(NY) for z in range(NZ)] for x in range(NX)
]
PLANES_XZ = [
    [device(1, x, y, z) for x in range(NX) for z in range(NZ)] for y in range(NY)
]


def exchange(value, groups):
    return lax.all_to_all(value, WHOLE, 0, 0, tiled=True, axis_index_groups=groups)


def spread(value, groups):
    count = len(groups[0])
    rows, width = value.shape
    copies = jnp.broadcast_to(value[None], (count, rows, width)).reshape(count * rows, width)
    return exchange(copies, groups)


def step(value, axes, by):
    sizes = {"x": NX, "y": NY}
    pairs = []
    for m in range(2):
        for x in range(NX):
            for y in range(NY):
                for z in range(NZ):
                    to = {"x": x, "y": y}
                    to[axes[m]] = (to[axes[m]] + by) % sizes[axes[m]]
                    pairs.append((device(m, x, y, z), device(m, to["x"], to["y"], z)))
    return lax.ppermute(value, WHOLE, pairs)


def across(value, by):
    return step(value, ("y", "x"), by)


def along(value, by):
    return step(value, ("x", "y"), by)


def home(x, y, z):
    x1, x0 = x // 2, x % 2
    y1, y0 = y // 2, y % 2
    z2, z1, z0 = z // 4, (z // 2) % 2, z % 2
    return 2 * x0 + y1, 2 * y0 + z2, 4 * z1 + 2 * z0 + x1


def row_orders():
    orders = np.zeros((2, 2 * HALF, 2 * HALF), np.float32)
    for x in range(NX):
        for y in range(NY):
            for z in range(NZ):
                hx, hy, hz = home(x, y, z)
                for b in range(2):
                    orders[0, ((hx * NY + hy) * NZ + hz) * 2 + b, ((x * NY + y) * NZ + z) * 2 + b] = 1
                    orders[1, ((hy * NX + hx) * NZ + hz) * 2 + b, ((y * NX + x) * NZ + z) * 2 + b] = 1
    return orders


def last_hop():
    pairs = []
    for m in range(2):
        for x in range(NX):
            for y in range(NY):
                for z in range(NZ):
                    pairs.append(
                        (device(m, x, y, z), device(x % 2, 2 * (x // 2) + m, y, z))
                    )
    return pairs


def tile_words(tiles_t):
    count, rows = tiles_t.shape

    def kernel(tiles_ref, word_ref):
        block = lax.broadcasted_iota(jnp.int32, (count, rows), 0)

        def step(k, word):
            tile = tiles_ref[pl.ds(k, 1), :]
            own = (tile * 205) >> 10
            bit = 1 << (tile - 5 * own)
            return word + jnp.where(block == own, bit, 0)

        word_ref[...] = lax.fori_loop(0, count, step, jnp.zeros((count, rows), jnp.int32), unroll=8)

    return pl.pallas_call(
        kernel,
        out_shape=jax.ShapeDtypeStruct((count, rows), jnp.int32),
        cost_estimate=pl.CostEstimate(
            flops=16 * count * count * rows, bytes_accessed=8 * count * rows, transcendentals=0
        ),
    )(tiles_t)


def fetch(source, chunk, buffer, semaphores):
    copies = []
    for k in range(source.shape[0] // chunk):
        rows = pl.ds(k * chunk, chunk)
        copies.append(pltpu.make_async_copy(source.at[rows], buffer.at[rows], semaphores.at[k]))
        copies[-1].start()
    return copies


DEPTH = 512
EARLY_LIMIT = 40 * 1024 * 1024
GRADIENT_LIMIT = 48 * 1024 * 1024
LATE_LIMIT = 16 * 1024 * 1024


def add_logits(half_refs, heads, out_ref, copies=None):
    at = 0
    for col, refs in heads:
        start = at
        for ref in refs:
            for k in range(ref.shape[0] // DEPTH):
                left = jnp.concatenate([half[:, at : at + DEPTH] for half in half_refs], axis=0)
                if copies is not None:
                    copies[at // DEPTH].wait()
                term = jnp.dot(
                    left, ref[k * DEPTH : (k + 1) * DEPTH, :], preferred_element_type=jnp.float32
                )
                if at == start:
                    out_ref[:, col] = term
                else:
                    out_ref[:, col] += term
                at += DEPTH


def logit_cost(rows, elements):
    return pl.CostEstimate(
        flops=2 * rows * elements, bytes_accessed=2 * elements, transcendentals=0
    )


def early_logits(halves, teacher_head, student_cols):
    count = len(halves)
    rows = count * halves[0].shape[0]
    cols = teacher_head.shape[1]

    half = teacher_head.shape[0] // 2

    def kernel(*refs):
        t_hbm, s_hbm, out_ref, t_low, t_high, s_ref, low_sem, high_sem, s_sem = refs[count:]
        copies = (
            fetch(t_hbm.at[pl.ds(0, half)], DEPTH, t_low, low_sem)
            + fetch(t_hbm.at[pl.ds(half, half)], DEPTH, t_high, high_sem)
            + fetch(s_hbm, DEPTH, s_ref, s_sem)
        )
        heads = ((slice(0, cols), (t_low, t_high)), (slice(cols, 2 * cols), (s_ref,)))
        add_logits(refs[:count], heads, out_ref, copies)

    whole = pl.BlockSpec(memory_space=pltpu.VMEM)
    low = jax.ShapeDtypeStruct((half, cols), teacher_head.dtype)
    return pl.pallas_call(
        kernel,
        in_specs=[whole] * count + [pl.BlockSpec(memory_space=pltpu.HBM)] * 2,
        out_specs=[whole] * 4,
        out_shape=[
            jax.ShapeDtypeStruct((rows, 2 * cols), jnp.float32),
            low,
            low,
            jax.ShapeDtypeStruct(student_cols.shape, student_cols.dtype),
        ],
        scratch_shapes=[
            pltpu.SemaphoreType.DMA((half // DEPTH,)),
            pltpu.SemaphoreType.DMA((half // DEPTH,)),
            pltpu.SemaphoreType.DMA((student_cols.shape[0] // DEPTH,)),
        ],
        cost_estimate=logit_cost(rows, teacher_head.size + student_cols.size),
        compiler_params=pltpu.CompilerParams(vmem_limit_bytes=EARLY_LIMIT),
    )(*halves, teacher_head, student_cols)


def logits_and_message(slots, early, halves, heads, words, own_word, per_shard):
    count = len(halves)
    half = halves[0].shape[0]
    rows = early.shape[0] + count * half
    block = half // 2
    cols = heads[0].shape[1]
    lanes = cols // per_shard
    elements = sum(head.size for head in heads)

    def kernel(slot_ref, early_ref, *refs):
        (
            word_ref, own_word_ref, t_low, t_high, s_ref, *msg_refs, logit_ref,
            late_ref, all_ref, spare_ref,
        ) = refs[count:]
        near = ((slice(0, cols), (t_low, t_high)), (slice(cols, 2 * cols), (s_ref,)))
        add_logits(refs[:count], near, late_ref)

        for source_ref, places in ((early_ref, (0, 1, 3, 6)), (late_ref, (2, 4, 5, 7))):
            for n, place in enumerate(places):
                for k in range(2):
                    third = lax.rem(slot_ref[0] + place // 2, 4)
                    second = lax.rem(slot_ref[1] + (0, 3, 1, 2)[2 * (place % 2) + k], 4)
                    at = pl.multiple_of((third * 4 + second) * block, block)
                    start = n * half + k * block
                    all_ref[pl.ds(at, block), :] = source_ref[start : start + block, :]

        word = own_word_ref[...]
        t_log = all_ref[:, :cols].T
        s_log = all_ref[:, cols:].T
        logit_ref[...] = s_log
        t_top = jnp.max(t_log, axis=0, keepdims=True)
        named_before = jnp.zeros((1, rows), jnp.int32)
        t_total = jnp.zeros((1, rows), jnp.float32)
        t_rest = jnp.zeros((1, rows), jnp.float32)
        first = jnp.zeros((lanes, rows), jnp.float32)
        second = jnp.zeros((lanes, rows), jnp.float32)
        for t in range(per_shard):
            e = jnp.exp(t_log[t * lanes : (t + 1) * lanes] - t_top)
            part = jnp.sum(e, axis=0, keepdims=True)
            named = (word >> t) & 1
            t_total += part
            t_rest += jnp.where(named == 0, part, 0.0)
            first = jnp.where((named == 1) & (named_before == 0), e, first)
            second = jnp.where((named == 1) & (named_before == 1), e, second)
            named_before += named
        named_s, _ = expand_words(word_ref[...], per_shard)
        s_top = jnp.max(s_log, axis=0, keepdims=True)
        e = jnp.exp(s_log - s_top)
        s_total = jnp.sum(e, axis=0, keepdims=True)
        s_rest = jnp.sum(jnp.where(named_s, 0.0, e), axis=0, keepdims=True)
        line = lax.broadcasted_iota(jnp.int32, (8, rows), 0)
        stats = jnp.zeros((8, rows), jnp.float32)
        for at, value in enumerate((t_top, t_total, t_rest, s_top, s_total, s_rest)):
            stats = jnp.where(line == at, value, stats)
        for part in range(rows // 128):
            spare_ref[part, :lanes, :] = first[:, part * 128 : (part + 1) * 128]
            spare_ref[part, lanes:, :] = second[:, part * 128 : (part + 1) * 128]
        for n in range(4):
            to = lax.rem(slot_ref[0] + n, 4)
            for r in range(4):
                x = jnp.where(slot_ref[2] == 0, to, r)
                y = jnp.where(slot_ref[2] == 0, r, to)
                for slot in range(2):
                    for part in range(rows // 128):
                        msg_refs[n][
                            slot * 32 + 8 * r : slot * 32 + 8 * r + 8, part * 128 : (part + 1) * 128
                        ] = spare_ref[part, pl.ds(slot * lanes + y * 32 + x, 8, stride=4), :]
            msg_refs[n][64:72, :] = stats

    whole = pl.BlockSpec(memory_space=pltpu.VMEM)
    return pl.pallas_call(
        kernel,
        in_specs=[pl.BlockSpec(memory_space=pltpu.SMEM)] + [whole] * (count + 6),
        out_specs=[whole] * 5,
        out_shape=[jax.ShapeDtypeStruct((72, rows), jnp.float32)] * 4
        + [jax.ShapeDtypeStruct((cols, rows), jnp.float32)],
        scratch_shapes=[
            pltpu.VMEM((count * half, 2 * cols), jnp.float32),
            pltpu.VMEM((rows, 2 * cols), jnp.float32),
            pltpu.VMEM((rows // 128, 2 * lanes, 128), jnp.float32),
        ],
        cost_estimate=logit_cost(count * half, elements),
        compiler_params=pltpu.CompilerParams(vmem_limit_bytes=LATE_LIMIT),
    )(slots, early, *halves, words, own_word, *heads)


def expand_words(words, per_shard):
    shards = words.shape[0]
    tile = lax.broadcasted_iota(jnp.int32, (shards * per_shard, 1), 0)
    within = tile - per_shard * ((tile * 205) >> 10)
    wide = spread_blocks(words.astype(jnp.bfloat16), per_shard).astype(jnp.int32)
    named = (wide >> within) & 1
    before = wide & ((1 << within) - 1)
    return named == 1, before == 0


def spread_blocks(value, per_shard):
    shards = value.shape[0]
    tile = lax.broadcasted_iota(jnp.int32, (shards * per_shard, shards), 0)
    start = per_shard * lax.broadcasted_iota(jnp.int32, (shards * per_shard, shards), 1)
    chosen = ((tile >= start) & (tile < start + per_shard)).astype(jnp.float32).astype(jnp.bfloat16)
    return jnp.dot(chosen, value, preferred_element_type=jnp.float32)


def regroup(arrived):
    sources = len(arrived)
    rows = arrived[0].shape[1]

    def kernel(*refs):
        in_refs, out_ref = refs[:sources], refs[sources]
        stats = [ref[64:72, :] for ref in in_refs]

        def common(at):
            tops = [s[at : at + 1] for s in stats]
            top = functools.reduce(jnp.maximum, tops)
            weights = [jnp.exp(t - top) for t in tops]
            total = sum(w * s[at + 1 : at + 2] for w, s in zip(weights, stats))
            rest = sum(w * s[at + 2 : at + 3] for w, s in zip(weights, stats))
            return weights, (top, total, rest)

        weights, teacher = common(0)
        _, student = common(3)
        line = lax.broadcasted_iota(jnp.int32, (8, rows), 0)
        sums = jnp.zeros((8, rows), jnp.float32)
        for at, value in enumerate(teacher + student):
            sums = jnp.where(line == at, value, sums)
        block = jnp.zeros((32, 8, rows), jnp.float32)
        for j in range(sources):
            for slot in range(2):
                e = in_refs[j][slot * 32 : (slot + 1) * 32, :] * weights[j]
                block = jnp.where((line == 2 * j + slot)[None], e[:, None, :], block)
        out_ref[:, :8, :] = block
        out_ref[:, 8:, :] = jnp.broadcast_to(sums[None], (32, 8, rows))

    return pl.pallas_call(
        kernel,
        out_shape=jax.ShapeDtypeStruct((32, 16, rows), jnp.float32),
        compiler_params=pltpu.CompilerParams(vmem_limit_bytes=LATE_LIMIT),
    )(*arrived)


def spread_sources(value, slot_ref, per_shard):
    sources = value.shape[0]
    tile = lax.broadcasted_iota(jnp.int32, (sources * per_shard, 1), 0)
    arrival = lax.broadcasted_iota(jnp.int32, (1, sources), 1)
    place, chip = (slot_ref[0] + 4 - (arrival >> 5)) & 3, arrival & 31
    shard = jnp.where(slot_ref[2] == 0, chip * 4 + place, (place * 8 + (chip & 7)) * 4 + (chip >> 3))
    chosen = (((tile * 205) >> 10) == shard).astype(jnp.float32).astype(jnp.bfloat16)
    return jnp.dot(chosen, value, preferred_element_type=jnp.float32)


def gradient(slots, words, logit, arrived, order, student_cols, per_shard):
    cols, rows = logit.shape
    ds = student_cols.shape[0]
    width = 512
    block = rows // 4

    def kernel(slot_ref, word_ref, logit_ref, msg_ref, order_ref, w_hbm, *refs):
        out_refs, (kl_ref, near_ref, w_ref, w_sem) = refs[:4], refs[4:]
        copies = fetch(w_hbm, width, w_ref, w_sem)

        def sums(at):
            top_each = msg_ref[:, at, :]
            top = jnp.max(top_each, axis=0, keepdims=True)
            weight = jnp.exp(top_each - top)
            total = jnp.sum(weight * msg_ref[:, at + 1, :], axis=0, keepdims=True)
            rest = jnp.sum(weight * msg_ref[:, at + 2, :], axis=0, keepdims=True)
            return top, weight, total, rest / total

        _, t_weight, t_total, t_mass = sums(8)
        s_top, _, s_total, s_mass = sums(11)
        scale = t_weight / t_total

        def arrived_prob(slot):
            parts = [msg_ref[:, 2 * j + slot, :] * scale for j in range(4)]
            prob = jnp.concatenate(parts, axis=0).astype(jnp.bfloat16)
            return spread_sources(prob, slot_ref, per_shard)

        named, is_first = expand_words(word_ref[...], per_shard)
        teacher = jnp.where(is_first, arrived_prob(0), arrived_prob(1))
        prob = jnp.exp(logit_ref[...] - s_top) * (1.0 / s_total)
        kl = (
            jnp.where(named, prob - teacher, prob * (1.0 - t_mass / s_mass)) * loss_scale
        ).astype(jnp.bfloat16)
        kl_ref[...] = lax.dot_general(
            order_ref[...], kl, (((1,), (1,)), ((), ())), preferred_element_type=jnp.float32
        ).astype(jnp.bfloat16)
        for n in range(4):
            at = pl.multiple_of(lax.rem(slot_ref[0] + n, 4) * block, block)
            near_ref[n * block : (n + 1) * block, :] = kl_ref[pl.ds(at, block), :]
        for k in range(ds // width):
            span = slice(k * width, (k + 1) * width)
            copies[k].wait()
            term = lax.dot_general(
                near_ref[...],
                w_ref[span, :],
                (((1,), (1,)), ((), ())),
                preferred_element_type=jnp.float32,
            ).astype(jnp.bfloat16)
            for n in range(4):
                out_refs[n][:, span] = term[n * block : (n + 1) * block, :]

    whole = pl.BlockSpec(memory_space=pltpu.VMEM)
    return pl.pallas_call(
        kernel,
        in_specs=[pl.BlockSpec(memory_space=pltpu.SMEM)]
        + [whole] * 4
        + [pl.BlockSpec(memory_space=pltpu.HBM)],
        out_specs=[whole] * 4,
        out_shape=[jax.ShapeDtypeStruct((block, ds), jnp.bfloat16)] * 4,
        scratch_shapes=[
            pltpu.VMEM((rows, cols), jnp.bfloat16),
            pltpu.VMEM((rows, cols), jnp.bfloat16),
            pltpu.VMEM(student_cols.shape, jnp.bfloat16),
            pltpu.SemaphoreType.DMA((ds // width,)),
        ],
        compiler_params=pltpu.CompilerParams(vmem_limit_bytes=GRADIENT_LIMIT),
    )(slots, words, logit, arrived, order, student_cols)


def per_device(teacher_hidden, teacher_head, student_hidden, student_head, tiles):
    shards = lax.axis_size(LINE)
    shard_index = lax.axis_index(LINE)
    core = lax.axis_index("mesh")
    ds, tiles_all, lane_count = student_head.shape
    student_cols = student_head.reshape(ds, tiles_all * lane_count)
    per_shard = tiles_all // shards
    picks = tiles.shape[1]

    both = jnp.concatenate((teacher_hidden, student_hidden), axis=1)
    mine = lax.dynamic_slice_in_dim(both, 2 * core, 2, 0)
    gathered = spread(mine, LINES_Z)
    by_chip = tiles.reshape(NY, NZ, NX, 2, 2, picks)
    by_chip = lax.dynamic_index_in_dim(by_chip, core, 3, keepdims=False)
    tiles_t = jnp.where(
        core == 0, by_chip.transpose(4, 2, 0, 1, 3), by_chip.transpose(4, 0, 2, 1, 3)
    ).reshape(picks, 2 * shards)
    words = tile_words(tiles_t)
    last, after, opposite = across(gathered, 1), across(gathered, -1), across(gathered, 2)
    opposite, words = lax.optimization_barrier((opposite, words))
    own = (
        jnp.concatenate((gathered, last), axis=0),
        jnp.concatenate((after, opposite), axis=0),
    )
    below_first = along(own[0], 1)
    above_first = along(own[1], -1)
    below_second = along(own[1], 1)
    above_second = along(own[0], -1)
    far = (along(below_first, 1), along(above_first, -1))
    early, *near_heads = early_logits(
        own + (above_first, below_first), teacher_head, student_cols
    )
    late = (above_second,) + far + (below_second,)
    own_word = lax.dynamic_slice_in_dim(words, shard_index, 1, 0)

    x, y = lax.axis_index("dp"), lax.axis_index("vocab") // NZ
    slots = jnp.stack((jnp.where(core == 0, x, y), jnp.where(core == 0, y, x), core))
    *message, logit = logits_and_message(
        slots, early, late, near_heads, words, own_word, per_shard
    )
    near = (
        message[0], along(message[1], 1), along(message[2], 2), along(message[3], -1),
    )
    arrived = exchange(regroup(near), PLANES_YZ + PLANES_XZ)

    order = lax.dynamic_index_in_dim(
        jnp.asarray(row_orders(), jnp.bfloat16), core, 0, keepdims=False
    )
    kept, after_chip, opposite_chip, last_chip = gradient(
        slots, words, logit, arrived, order, student_cols, per_shard
    )
    terms = (kept, along(opposite_chip, 2), along(after_chip, 1), along(last_chip, -1))
    near = sum(term.astype(jnp.float32) for term in terms)
    far = exchange(near.astype(jnp.bfloat16), PLANES_YZ + PLANES_XZ)
    summed = jnp.sum(far.reshape(NY * NZ, 2, ds).astype(jnp.float32), axis=0)
    return lax.ppermute(summed.astype(jnp.bfloat16), WHOLE, last_hop())


def solution(mesh):
    return jax.shard_map(
        per_device,
        mesh=mesh,
        in_specs=(
            P(("vocab", "dp"), None),
            P(None, ("vocab", "dp")),
            P(("vocab", "dp"), None),
            P(None, None, ("vocab", "dp")),
            P(),
        ),
        out_specs=P(("mesh", "vocab", "dp"), None),
        check_vma=False,
    )
```

```python
import functools

import jax
import jax.numpy as jnp
import numpy as np
from jax import lax
from jax.experimental import pallas as pl
from jax.experimental.pallas import tpu as pltpu
from jax.sharding import PartitionSpec as P

loss_scale = 1024.0
NX, NY, NZ = 4, 4, 8
LINE = ("vocab", "dp")
WHOLE = ("mesh", "vocab", "dp")
HALF = NX * NY * NZ


def device(m, x, y, z):
    return m * HALF + (y * NZ + z) * NX + x


LINES_Z = [
    [device(m, x, y, z) for z in range(NZ)]
    for m in range(2)
    for x in range(NX)
    for y in range(NY)
]
LINES_X = [
    [[device(m, x, y, z) for x in range(NX)] for y in range(NY) for z in range(NZ)]
    for m in range(2)
]
LINES_Y = [
    [[device(m, x, y, z) for y in range(NY)] for x in range(NX) for z in range(NZ)]
    for m in range(2)
]
PLANES_YZ = [
    [device(0, x, y, z) for y in range(NY) for z in range(NZ)] for x in range(NX)
]
PLANES_XZ = [
    [device(1, x, y, z) for x in range(NX) for z in range(NZ)] for y in range(NY)
]


def exchange(value, groups):
    return lax.all_to_all(value, WHOLE, 0, 0, tiled=True, axis_index_groups=groups)


def spread(value, groups):
    count = len(groups[0])
    rows, width = value.shape
    copies = jnp.broadcast_to(value[None], (count, rows, width)).reshape(count * rows, width)
    return exchange(copies, groups)


def step(value, axes, by):
    sizes = {"x": NX, "y": NY}
    pairs = []
    for m in range(2):
        for x in range(NX):
            for y in range(NY):
                for z in range(NZ):
                    to = {"x": x, "y": y}
                    to[axes[m]] = (to[axes[m]] + by) % sizes[axes[m]]
                    pairs.append((device(m, x, y, z), device(m, to["x"], to["y"], z)))
    return lax.ppermute(value, WHOLE, pairs)


def across(value, by):
    return step(value, ("y", "x"), by)


def along(value, by):
    return step(value, ("x", "y"), by)


def home(x, y, z):
    x1, x0 = x // 2, x % 2
    y1, y0 = y // 2, y % 2
    z2, z1, z0 = z // 4, (z // 2) % 2, z % 2
    return 2 * x0 + y1, 2 * y0 + z2, 4 * z1 + 2 * z0 + x1


def row_orders():
    orders = np.zeros((2, 2 * HALF, 2 * HALF), np.float32)
    for x in range(NX):
        for y in range(NY):
            for z in range(NZ):
                hx, hy, hz = home(x, y, z)
                for b in range(2):
                    orders[0, ((hx * NY + hy) * NZ + hz) * 2 + b, ((x * NY + y) * NZ + z) * 2 + b] = 1
                    orders[1, ((hy * NX + hx) * NZ + hz) * 2 + b, ((y * NX + x) * NZ + z) * 2 + b] = 1
    return orders


def last_hop():
    pairs = []
    for m in range(2):
        for x in range(NX):
            for y in range(NY):
                for z in range(NZ):
                    pairs.append(
                        (device(m, x, y, z), device(x % 2, 2 * (x // 2) + m, y, z))
                    )
    return pairs


def tile_words(tiles_t):
    count, rows = tiles_t.shape

    def kernel(tiles_ref, word_ref):
        block = lax.broadcasted_iota(jnp.int32, (count, rows), 0)

        def step(k, word):
            tile = tiles_ref[pl.ds(k, 1), :]
            own = (tile * 205) >> 10
            bit = 1 << (tile - 5 * own)
            return word + jnp.where(block == own, bit, 0)

        word_ref[...] = lax.fori_loop(0, count, step, jnp.zeros((count, rows), jnp.int32), unroll=8)

    return pl.pallas_call(
        kernel,
        out_shape=jax.ShapeDtypeStruct((count, rows), jnp.int32),
        cost_estimate=pl.CostEstimate(
            flops=16 * count * count * rows, bytes_accessed=8 * count * rows, transcendentals=0
        ),
    )(tiles_t)


def fetch(source, chunk, buffer, semaphores):
    copies = []
    for k in range(source.shape[0] // chunk):
        rows = pl.ds(k * chunk, chunk)
        copies.append(pltpu.make_async_copy(source.at[rows], buffer.at[rows], semaphores.at[k]))
        copies[-1].start()
    return copies


DEPTH = 512
EARLY_LIMIT = 40 * 1024 * 1024
GRADIENT_LIMIT = 48 * 1024 * 1024
LATE_LIMIT = 16 * 1024 * 1024


def add_logits(half_refs, heads, out_ref, copies=None):
    at = 0
    for col, refs in heads:
        start = at
        for ref in refs:
            for k in range(ref.shape[0] // DEPTH):
                left = jnp.concatenate([half[:, at : at + DEPTH] for half in half_refs], axis=0)
                if copies is not None:
                    copies[at // DEPTH].wait()
                term = jnp.dot(
                    left, ref[k * DEPTH : (k + 1) * DEPTH, :], preferred_element_type=jnp.float32
                )
                if at == start:
                    out_ref[:, col] = term
                else:
                    out_ref[:, col] += term
                at += DEPTH


def logit_cost(rows, elements):
    return pl.CostEstimate(
        flops=2 * rows * elements, bytes_accessed=2 * elements, transcendentals=0
    )


def early_logits(halves, teacher_head, student_cols):
    count = len(halves)
    rows = count * halves[0].shape[0]
    cols = teacher_head.shape[1]

    half = teacher_head.shape[0] // 2

    def kernel(*refs):
        t_hbm, s_hbm, out_ref, t_low, t_high, s_ref, low_sem, high_sem, s_sem = refs[count:]
        copies = (
            fetch(t_hbm.at[pl.ds(0, half)], DEPTH, t_low, low_sem)
            + fetch(t_hbm.at[pl.ds(half, half)], DEPTH, t_high, high_sem)
            + fetch(s_hbm, DEPTH, s_ref, s_sem)
        )
        heads = ((slice(0, cols), (t_low, t_high)), (slice(cols, 2 * cols), (s_ref,)))
        add_logits(refs[:count], heads, out_ref, copies)

    whole = pl.BlockSpec(memory_space=pltpu.VMEM)
    low = jax.ShapeDtypeStruct((half, cols), teacher_head.dtype)
    return pl.pallas_call(
        kernel,
        in_specs=[whole] * count + [pl.BlockSpec(memory_space=pltpu.HBM)] * 2,
        out_specs=[whole] * 4,
        out_shape=[
            jax.ShapeDtypeStruct((rows, 2 * cols), jnp.float32),
            low,
            low,
            jax.ShapeDtypeStruct(student_cols.shape, student_cols.dtype),
        ],
        scratch_shapes=[
            pltpu.SemaphoreType.DMA((half // DEPTH,)),
            pltpu.SemaphoreType.DMA((half // DEPTH,)),
            pltpu.SemaphoreType.DMA((student_cols.shape[0] // DEPTH,)),
        ],
        cost_estimate=logit_cost(rows, teacher_head.size + student_cols.size),
        compiler_params=pltpu.CompilerParams(vmem_limit_bytes=EARLY_LIMIT),
    )(*halves, teacher_head, student_cols)


def logits_and_message(slots, early, halves, heads, words, own_word, per_shard):
    count = len(halves)
    half = halves[0].shape[0]
    rows = early.shape[0] + count * half
    block = half // 2
    cols = heads[0].shape[1]
    lanes = cols // per_shard
    elements = sum(head.size for head in heads)

    def kernel(slot_ref, early_ref, *refs):
        (
            word_ref, own_word_ref, t_low, t_high, s_ref, *msg_refs, logit_ref,
            late_ref, all_ref, spare_ref,
        ) = refs[count:]
        near = ((slice(0, cols), (t_low, t_high)), (slice(cols, 2 * cols), (s_ref,)))
        add_logits(refs[:count], near, late_ref)

        for source_ref, places in ((early_ref, (0, 1, 3, 6)), (late_ref, (2, 4, 5, 7))):
            for n, place in enumerate(places):
                for k in range(2):
                    third = lax.rem(slot_ref[0] + place // 2, 4)
                    second = lax.rem(slot_ref[1] + (0, 3, 1, 2)[2 * (place % 2) + k], 4)
                    at = pl.multiple_of((third * 4 + second) * block, block)
                    start = n * half + k * block
                    all_ref[pl.ds(at, block), :] = source_ref[start : start + block, :]

        word = own_word_ref[...]
        t_log = all_ref[:, :cols].T
        s_log = all_ref[:, cols:].T
        logit_ref[...] = s_log
        t_top = jnp.max(t_log, axis=0, keepdims=True)
        named_before = jnp.zeros((1, rows), jnp.int32)
        t_total = jnp.zeros((1, rows), jnp.float32)
        t_rest = jnp.zeros((1, rows), jnp.float32)
        first = jnp.zeros((lanes, rows), jnp.float32)
        second = jnp.zeros((lanes, rows), jnp.float32)
        for t in range(per_shard):
            e = jnp.exp(t_log[t * lanes : (t + 1) * lanes] - t_top)
            part = jnp.sum(e, axis=0, keepdims=True)
            named = (word >> t) & 1
            t_total += part
            t_rest += jnp.where(named == 0, part, 0.0)
            first = jnp.where((named == 1) & (named_before == 0), e, first)
            second = jnp.where((named == 1) & (named_before == 1), e, second)
            named_before += named
        named_s, _ = expand_words(word_ref[...], per_shard)
        s_top = jnp.max(s_log, axis=0, keepdims=True)
        e = jnp.exp(s_log - s_top)
        s_total = jnp.sum(e, axis=0, keepdims=True)
        s_rest = jnp.sum(jnp.where(named_s, 0.0, e), axis=0, keepdims=True)
        line = lax.broadcasted_iota(jnp.int32, (8, rows), 0)
        stats = jnp.zeros((8, rows), jnp.float32)
        for at, value in enumerate((t_top, t_total, t_rest, s_top, s_total, s_rest)):
            stats = jnp.where(line == at, value, stats)
        for part in range(rows // 128):
            spare_ref[part, :lanes, :] = first[:, part * 128 : (part + 1) * 128]
            spare_ref[part, lanes:, :] = second[:, part * 128 : (part + 1) * 128]
        for n in range(4):
            to = lax.rem(slot_ref[0] + n, 4)
            for r in range(4):
                x = jnp.where(slot_ref[2] == 0, to, r)
                y = jnp.where(slot_ref[2] == 0, r, to)
                for slot in range(2):
                    for part in range(rows // 128):
                        msg_refs[n][
                            slot * 32 + 8 * r : slot * 32 + 8 * r + 8, part * 128 : (part + 1) * 128
                        ] = spare_ref[part, pl.ds(slot * lanes + y * 32 + x, 8, stride=4), :]
            msg_refs[n][64:72, :] = stats

    whole = pl.BlockSpec(memory_space=pltpu.VMEM)
    return pl.pallas_call(
        kernel,
        in_specs=[pl.BlockSpec(memory_space=pltpu.SMEM)] + [whole] * (count + 6),
        out_specs=[whole] * 5,
        out_shape=[jax.ShapeDtypeStruct((72, rows), jnp.float32)] * 4
        + [jax.ShapeDtypeStruct((cols, rows), jnp.float32)],
        scratch_shapes=[
            pltpu.VMEM((count * half, 2 * cols), jnp.float32),
            pltpu.VMEM((rows, 2 * cols), jnp.float32),
            pltpu.VMEM((rows // 128, 2 * lanes, 128), jnp.float32),
        ],
        cost_estimate=logit_cost(count * half, elements),
        compiler_params=pltpu.CompilerParams(vmem_limit_bytes=LATE_LIMIT),
    )(slots, early, *halves, words, own_word, *heads)


def expand_words(words, per_shard):
    shards = words.shape[0]
    tile = lax.broadcasted_iota(jnp.int32, (shards * per_shard, 1), 0)
    within = tile - per_shard * ((tile * 205) >> 10)
    wide = spread_blocks(words.astype(jnp.bfloat16), per_shard).astype(jnp.int32)
    named = (wide >> within) & 1
    before = wide & ((1 << within) - 1)
    return named == 1, before == 0


def spread_blocks(value, per_shard):
    shards = value.shape[0]
    tile = lax.broadcasted_iota(jnp.int32, (shards * per_shard, shards), 0)
    start = per_shard * lax.broadcasted_iota(jnp.int32, (shards * per_shard, shards), 1)
    chosen = ((tile >= start) & (tile < start + per_shard)).astype(jnp.float32).astype(jnp.bfloat16)
    return jnp.dot(chosen, value, preferred_element_type=jnp.float32)


def regroup(arrived):
    sources = len(arrived)
    rows = arrived[0].shape[1]

    def kernel(*refs):
        in_refs, out_ref = refs[:sources], refs[sources]
        stats = [ref[64:72, :] for ref in in_refs]

        def common(at):
            tops = [s[at : at + 1] for s in stats]
            top = functools.reduce(jnp.maximum, tops)
            weights = [jnp.exp(t - top) for t in tops]
            total = sum(w * s[at + 1 : at + 2] for w, s in zip(weights, stats))
            rest = sum(w * s[at + 2 : at + 3] for w, s in zip(weights, stats))
            return weights, (top, total, rest)

        weights, teacher = common(0)
        _, student = common(3)
        line = lax.broadcasted_iota(jnp.int32, (8, rows), 0)
        sums = jnp.zeros((8, rows), jnp.float32)
        for at, value in enumerate(teacher + student):
            sums = jnp.where(line == at, value, sums)
        block = jnp.zeros((32, 8, rows), jnp.float32)
        for j in range(sources):
            for slot in range(2):
                e = in_refs[j][slot * 32 : (slot + 1) * 32, :] * weights[j]
                block = jnp.where((line == 2 * j + slot)[None], e[:, None, :], block)
        out_ref[:, :8, :] = block
        out_ref[:, 8:, :] = jnp.broadcast_to(sums[None], (32, 8, rows))

    return pl.pallas_call(
        kernel,
        out_shape=jax.ShapeDtypeStruct((32, 16, rows), jnp.float32),
        compiler_params=pltpu.CompilerParams(vmem_limit_bytes=LATE_LIMIT),
    )(*arrived)


def spread_sources(value, slot_ref, per_shard):
    sources = value.shape[0]
    tile = lax.broadcasted_iota(jnp.int32, (sources * per_shard, 1), 0)
    arrival = lax.broadcasted_iota(jnp.int32, (1, sources), 1)
    place, chip = (slot_ref[0] + 4 - (arrival >> 5)) & 3, arrival & 31
    shard = jnp.where(slot_ref[2] == 0, chip * 4 + place, (place * 8 + (chip & 7)) * 4 + (chip >> 3))
    chosen = (((tile * 205) >> 10) == shard).astype(jnp.float32).astype(jnp.bfloat16)
    return jnp.dot(chosen, value, preferred_element_type=jnp.float32)


def gradient(slots, words, logit, arrived, order, student_cols, per_shard):
    cols, rows = logit.shape
    ds = student_cols.shape[0]
    width = 512
    block = rows // 4

    def kernel(slot_ref, word_ref, logit_ref, msg_ref, order_ref, w_hbm, *refs):
        out_refs, (kl_ref, near_ref, w_ref, w_sem) = refs[:4], refs[4:]
        copies = fetch(w_hbm, width, w_ref, w_sem)

        def sums(at):
            top_each = msg_ref[:, at, :]
            top = jnp.max(top_each, axis=0, keepdims=True)
            weight = jnp.exp(top_each - top)
            total = jnp.sum(weight * msg_ref[:, at + 1, :], axis=0, keepdims=True)
            rest = jnp.sum(weight * msg_ref[:, at + 2, :], axis=0, keepdims=True)
            return top, weight, total, rest / total

        _, t_weight, t_total, t_mass = sums(8)
        s_top, _, s_total, s_mass = sums(11)
        scale = t_weight / t_total

        def arrived_prob(slot):
            parts = [msg_ref[:, 2 * j + slot, :] * scale for j in range(4)]
            prob = jnp.concatenate(parts, axis=0).astype(jnp.bfloat16)
            return spread_sources(prob, slot_ref, per_shard)

        named, is_first = expand_words(word_ref[...], per_shard)
        teacher = jnp.where(is_first, arrived_prob(0), arrived_prob(1))
        prob = jnp.exp(logit_ref[...] - s_top) * (1.0 / s_total)
        kl = (
            jnp.where(named, prob - teacher, prob * (1.0 - t_mass / s_mass)) * loss_scale
        ).astype(jnp.bfloat16)
        kl_ref[...] = lax.dot_general(
            order_ref[...], kl, (((1,), (1,)), ((), ())), preferred_element_type=jnp.float32
        ).astype(jnp.bfloat16)
        for n in range(4):
            at = pl.multiple_of(lax.rem(slot_ref[0] + n, 4) * block, block)
            near_ref[n * block : (n + 1) * block, :] = kl_ref[pl.ds(at, block), :]
        for k in range(ds // width):
            span = slice(k * width, (k + 1) * width)
            copies[k].wait()
            term = lax.dot_general(
                near_ref[...],
                w_ref[span, :],
                (((1,), (1,)), ((), ())),
                preferred_element_type=jnp.float32,
            ).astype(jnp.bfloat16)
            for n in range(4):
                out_refs[n][:, span] = term[n * block : (n + 1) * block, :]

    whole = pl.BlockSpec(memory_space=pltpu.VMEM)
    return pl.pallas_call(
        kernel,
        in_specs=[pl.BlockSpec(memory_space=pltpu.SMEM)]
        + [whole] * 4
        + [pl.BlockSpec(memory_space=pltpu.HBM)],
        out_specs=[whole] * 4,
        out_shape=[jax.ShapeDtypeStruct((block, ds), jnp.bfloat16)] * 4,
        scratch_shapes=[
            pltpu.VMEM((rows, cols), jnp.bfloat16),
            pltpu.VMEM((rows, cols), jnp.bfloat16),
            pltpu.VMEM(student_cols.shape, jnp.bfloat16),
            pltpu.SemaphoreType.DMA((ds // width,)),
        ],
        compiler_params=pltpu.CompilerParams(vmem_limit_bytes=GRADIENT_LIMIT),
    )(slots, words, logit, arrived, order, student_cols)


def per_device(teacher_hidden, teacher_head, student_hidden, student_head, tiles):
    shards = lax.axis_size(LINE)
    shard_index = lax.axis_index(LINE)
    core = lax.axis_index("mesh")
    ds, tiles_all, lane_count = student_head.shape
    student_cols = student_head.reshape(ds, tiles_all * lane_count)
    per_shard = tiles_all // shards
    picks = tiles.shape[1]

    both = jnp.concatenate((teacher_hidden, student_hidden), axis=1)
    mine = lax.dynamic_slice_in_dim(both, 2 * core, 2, 0)
    gathered = spread(mine, LINES_Z)
    by_chip = tiles.reshape(NY, NZ, NX, 2, 2, picks)
    by_chip = lax.dynamic_index_in_dim(by_chip, core, 3, keepdims=False)
    tiles_t = jnp.where(
        core == 0, by_chip.transpose(4, 2, 0, 1, 3), by_chip.transpose(4, 0, 2, 1, 3)
    ).reshape(picks, 2 * shards)
    words = tile_words(tiles_t)
    last, after, opposite = across(gathered, 1), across(gathered, -1), across(gathered, 2)
    opposite, words = lax.optimization_barrier((opposite, words))
    own = (
        jnp.concatenate((gathered, last), axis=0),
        jnp.concatenate((after, opposite), axis=0),
    )
    below_first, above_second = along(own[0], 1), along(own[0], -1)
    below_first, above_second, second = lax.optimization_barrier(
        (below_first, above_second, own[1])
    )
    own = (own[0], second)
    above_first = along(own[1], -1)
    below_second = along(own[1], 1)
    far = (along(below_first, 1), along(above_first, -1))
    early, *near_heads = early_logits(
        own + (above_first, below_first), teacher_head, student_cols
    )
    late = (above_second,) + far + (below_second,)
    own_word = lax.dynamic_slice_in_dim(words, shard_index, 1, 0)

    x, y = lax.axis_index("dp"), lax.axis_index("vocab") // NZ
    slots = jnp.stack((jnp.where(core == 0, x, y), jnp.where(core == 0, y, x), core))
    *message, logit = logits_and_message(
        slots, early, late, near_heads, words, own_word, per_shard
    )
    near = (
        message[0], along(message[1], 1), along(message[2], 2), along(message[3], -1),
    )
    arrived = exchange(regroup(near), PLANES_YZ + PLANES_XZ)

    order = lax.dynamic_index_in_dim(
        jnp.asarray(row_orders(), jnp.bfloat16), core, 0, keepdims=False
    )
    kept, after_chip, opposite_chip, last_chip = gradient(
        slots, words, logit, arrived, order, student_cols, per_shard
    )
    terms = (kept, along(opposite_chip, 2), along(after_chip, 1), along(last_chip, -1))
    near = sum(term.astype(jnp.float32) for term in terms)
    far = exchange(near.astype(jnp.bfloat16), PLANES_YZ + PLANES_XZ)
    summed = jnp.sum(far.reshape(NY * NZ, 2, ds).astype(jnp.float32), axis=0)
    return lax.ppermute(summed.astype(jnp.bfloat16), WHOLE, last_hop())


def solution(mesh):
    return jax.shard_map(
        per_device,
        mesh=mesh,
        in_specs=(
            P(("vocab", "dp"), None),
            P(None, ("vocab", "dp")),
            P(("vocab", "dp"), None),
            P(None, None, ("vocab", "dp")),
            P(),
        ),
        out_specs=P(("mesh", "vocab", "dp"), None),
        check_vma=False,
    )
```

```python
import functools

import jax
import jax.numpy as jnp
import numpy as np
from jax import lax
from jax.experimental import pallas as pl
from jax.experimental.pallas import tpu as pltpu
from jax.sharding import PartitionSpec as P

loss_scale = 1024.0
NX, NY, NZ = 4, 4, 8
LINE = ("vocab", "dp")
WHOLE = ("mesh", "vocab", "dp")
HALF = NX * NY * NZ


def device(m, x, y, z):
    return m * HALF + (y * NZ + z) * NX + x


LINES_Z = [
    [device(m, x, y, z) for z in range(NZ)]
    for m in range(2)
    for x in range(NX)
    for y in range(NY)
]
LINES_X = [
    [[device(m, x, y, z) for x in range(NX)] for y in range(NY) for z in range(NZ)]
    for m in range(2)
]
LINES_Y = [
    [[device(m, x, y, z) for y in range(NY)] for x in range(NX) for z in range(NZ)]
    for m in range(2)
]
PLANES_YZ = [
    [device(0, x, y, z) for y in range(NY) for z in range(NZ)] for x in range(NX)
]
PLANES_XZ = [
    [device(1, x, y, z) for x in range(NX) for z in range(NZ)] for y in range(NY)
]


def exchange(value, groups):
    return lax.all_to_all(value, WHOLE, 0, 0, tiled=True, axis_index_groups=groups)


def spread(value, groups):
    count = len(groups[0])
    rows, width = value.shape
    copies = jnp.broadcast_to(value[None], (count, rows, width)).reshape(count * rows, width)
    return exchange(copies, groups)


def step(value, axes, by):
    sizes = {"x": NX, "y": NY}
    pairs = []
    for m in range(2):
        for x in range(NX):
            for y in range(NY):
                for z in range(NZ):
                    to = {"x": x, "y": y}
                    to[axes[m]] = (to[axes[m]] + by) % sizes[axes[m]]
                    pairs.append((device(m, x, y, z), device(m, to["x"], to["y"], z)))
    return lax.ppermute(value, WHOLE, pairs)


def across(value, by):
    return step(value, ("y", "x"), by)


def along(value, by):
    return step(value, ("x", "y"), by)


def home(x, y, z):
    x1, x0 = x // 2, x % 2
    y1, y0 = y // 2, y % 2
    z2, z1, z0 = z // 4, (z // 2) % 2, z % 2
    return 2 * x0 + y1, 2 * y0 + z2, 4 * z1 + 2 * z0 + x1


def row_orders():
    orders = np.zeros((2, 2 * HALF, 2 * HALF), np.float32)
    for x in range(NX):
        for y in range(NY):
            for z in range(NZ):
                hx, hy, hz = home(x, y, z)
                for b in range(2):
                    orders[0, ((hx * NY + hy) * NZ + hz) * 2 + b, ((x * NY + y) * NZ + z) * 2 + b] = 1
                    orders[1, ((hy * NX + hx) * NZ + hz) * 2 + b, ((y * NX + x) * NZ + z) * 2 + b] = 1
    return orders


def last_hop():
    pairs = []
    for m in range(2):
        for x in range(NX):
            for y in range(NY):
                for z in range(NZ):
                    pairs.append(
                        (device(m, x, y, z), device(x % 2, 2 * (x // 2) + m, y, z))
                    )
    return pairs


def tile_words(tiles_t):
    count, rows = tiles_t.shape

    def kernel(tiles_ref, word_ref):
        block = lax.broadcasted_iota(jnp.int32, (count, rows), 0)

        def step(k, word):
            tile = tiles_ref[pl.ds(k, 1), :]
            own = (tile * 205) >> 10
            bit = 1 << (tile - 5 * own)
            return word + jnp.where(block == own, bit, 0)

        word_ref[...] = lax.fori_loop(0, count, step, jnp.zeros((count, rows), jnp.int32), unroll=8)

    return pl.pallas_call(
        kernel,
        out_shape=jax.ShapeDtypeStruct((count, rows), jnp.int32),
        cost_estimate=pl.CostEstimate(
            flops=16 * count * count * rows, bytes_accessed=8 * count * rows, transcendentals=0
        ),
    )(tiles_t)


def fetch(source, chunk, buffer, semaphores):
    copies = []
    for k in range(source.shape[0] // chunk):
        rows = pl.ds(k * chunk, chunk)
        copies.append(pltpu.make_async_copy(source.at[rows], buffer.at[rows], semaphores.at[k]))
        copies[-1].start()
    return copies


DEPTH = 512
EARLY_LIMIT = 40 * 1024 * 1024
NEAR_LIMIT = 48 * 1024 * 1024
LATE_LIMIT = 16 * 1024 * 1024


def add_logits(half_refs, heads, out_ref, copies=None):
    at = 0
    for col, refs in heads:
        start = at
        for ref in refs:
            for k in range(ref.shape[0] // DEPTH):
                left = jnp.concatenate([half[:, at : at + DEPTH] for half in half_refs], axis=0)
                if copies is not None:
                    copies[at // DEPTH].wait()
                term = jnp.dot(
                    left, ref[k * DEPTH : (k + 1) * DEPTH, :], preferred_element_type=jnp.float32
                )
                if at == start:
                    out_ref[:, col] = term
                else:
                    out_ref[:, col] += term
                at += DEPTH


def logit_cost(rows, elements):
    return pl.CostEstimate(
        flops=2 * rows * elements, bytes_accessed=2 * elements, transcendentals=0
    )


def early_logits(halves, teacher_head, student_cols):
    count = len(halves)
    rows = count * halves[0].shape[0]
    cols = teacher_head.shape[1]

    half = teacher_head.shape[0] // 2

    def kernel(*refs):
        t_hbm, s_hbm, out_ref, t_low, t_high, s_ref, low_sem, high_sem, s_sem = refs[count:]
        copies = (
            fetch(t_hbm.at[pl.ds(0, half)], DEPTH, t_low, low_sem)
            + fetch(t_hbm.at[pl.ds(half, half)], DEPTH, t_high, high_sem)
            + fetch(s_hbm, DEPTH, s_ref, s_sem)
        )
        heads = ((slice(0, cols), (t_low, t_high)), (slice(cols, 2 * cols), (s_ref,)))
        add_logits(refs[:count], heads, out_ref, copies)

    whole = pl.BlockSpec(memory_space=pltpu.VMEM)
    low = jax.ShapeDtypeStruct((half, cols), teacher_head.dtype)
    return pl.pallas_call(
        kernel,
        in_specs=[whole] * count + [pl.BlockSpec(memory_space=pltpu.HBM)] * 2,
        out_specs=[whole] * 4,
        out_shape=[
            jax.ShapeDtypeStruct((rows, 2 * cols), jnp.float32),
            low,
            low,
            jax.ShapeDtypeStruct(student_cols.shape, student_cols.dtype),
        ],
        scratch_shapes=[
            pltpu.SemaphoreType.DMA((half // DEPTH,)),
            pltpu.SemaphoreType.DMA((half // DEPTH,)),
            pltpu.SemaphoreType.DMA((student_cols.shape[0] // DEPTH,)),
        ],
        cost_estimate=logit_cost(rows, teacher_head.size + student_cols.size),
        compiler_params=pltpu.CompilerParams(vmem_limit_bytes=EARLY_LIMIT),
    )(*halves, teacher_head, student_cols)


def logits_and_message(slots, early, halves, heads, words, own_word, per_shard):
    count = len(halves)
    half = halves[0].shape[0]
    rows = early.shape[0] + count * half
    block = half // 2
    cols = heads[0].shape[1]
    lanes = cols // per_shard
    elements = sum(head.size for head in heads)

    def kernel(slot_ref, early_ref, *refs):
        (
            word_ref, own_word_ref, t_low, t_high, s_ref, *msg_refs, logit_ref,
            late_ref, all_ref, spare_ref,
        ) = refs[count:]
        near = ((slice(0, cols), (t_low, t_high)), (slice(cols, 2 * cols), (s_ref,)))
        add_logits(refs[:count], near, late_ref)

        for source_ref, places in ((early_ref, (0, 1, 3, 6)), (late_ref, (2, 4, 5, 7))):
            for n, place in enumerate(places):
                for k in range(2):
                    third = lax.rem(slot_ref[0] + place // 2, 4)
                    second = lax.rem(slot_ref[1] + (0, 3, 1, 2)[2 * (place % 2) + k], 4)
                    at = pl.multiple_of((third * 4 + second) * block, block)
                    start = n * half + k * block
                    all_ref[pl.ds(at, block), :] = source_ref[start : start + block, :]

        word = own_word_ref[...]
        t_log = all_ref[:, :cols].T
        s_log = all_ref[:, cols:].T
        logit_ref[...] = s_log
        t_top = jnp.max(t_log, axis=0, keepdims=True)
        named_before = jnp.zeros((1, rows), jnp.int32)
        t_total = jnp.zeros((1, rows), jnp.float32)
        t_rest = jnp.zeros((1, rows), jnp.float32)
        first = jnp.zeros((lanes, rows), jnp.float32)
        second = jnp.zeros((lanes, rows), jnp.float32)
        for t in range(per_shard):
            e = jnp.exp(t_log[t * lanes : (t + 1) * lanes] - t_top)
            part = jnp.sum(e, axis=0, keepdims=True)
            named = (word >> t) & 1
            t_total += part
            t_rest += jnp.where(named == 0, part, 0.0)
            first = jnp.where((named == 1) & (named_before == 0), e, first)
            second = jnp.where((named == 1) & (named_before == 1), e, second)
            named_before += named
        named_s, _ = expand_words(word_ref[...], per_shard)
        s_top = jnp.max(s_log, axis=0, keepdims=True)
        e = jnp.exp(s_log - s_top)
        s_total = jnp.sum(e, axis=0, keepdims=True)
        s_rest = jnp.sum(jnp.where(named_s, 0.0, e), axis=0, keepdims=True)
        line = lax.broadcasted_iota(jnp.int32, (8, rows), 0)
        stats = jnp.zeros((8, rows), jnp.float32)
        for at, value in enumerate((t_top, t_total, t_rest, s_top, s_total, s_rest)):
            stats = jnp.where(line == at, value, stats)
        for part in range(rows // 128):
            spare_ref[part, :lanes, :] = first[:, part * 128 : (part + 1) * 128]
            spare_ref[part, lanes:, :] = second[:, part * 128 : (part + 1) * 128]
        for n in range(4):
            to = lax.rem(slot_ref[0] + n, 4)
            for r in range(4):
                x = jnp.where(slot_ref[2] == 0, to, r)
                y = jnp.where(slot_ref[2] == 0, r, to)
                for slot in range(2):
                    for part in range(rows // 128):
                        msg_refs[n][
                            slot * 32 + 8 * r : slot * 32 + 8 * r + 8, part * 128 : (part + 1) * 128
                        ] = spare_ref[part, pl.ds(slot * lanes + y * 32 + x, 8, stride=4), :]
            msg_refs[n][64:72, :] = stats

    whole = pl.BlockSpec(memory_space=pltpu.VMEM)
    return pl.pallas_call(
        kernel,
        in_specs=[pl.BlockSpec(memory_space=pltpu.SMEM)] + [whole] * (count + 6),
        out_specs=[whole] * 5,
        out_shape=[jax.ShapeDtypeStruct((72, rows), jnp.float32)] * 4
        + [jax.ShapeDtypeStruct((cols, rows), jnp.float32)],
        scratch_shapes=[
            pltpu.VMEM((count * half, 2 * cols), jnp.float32),
            pltpu.VMEM((rows, 2 * cols), jnp.float32),
            pltpu.VMEM((rows // 128, 2 * lanes, 128), jnp.float32),
        ],
        cost_estimate=logit_cost(count * half, elements),
        compiler_params=pltpu.CompilerParams(vmem_limit_bytes=LATE_LIMIT),
    )(slots, early, *halves, words, own_word, *heads)


def expand_words(words, per_shard):
    shards = words.shape[0]
    tile = lax.broadcasted_iota(jnp.int32, (shards * per_shard, 1), 0)
    within = tile - per_shard * ((tile * 205) >> 10)
    wide = spread_blocks(words.astype(jnp.bfloat16), per_shard).astype(jnp.int32)
    named = (wide >> within) & 1
    before = wide & ((1 << within) - 1)
    return named == 1, before == 0


def spread_blocks(value, per_shard):
    shards = value.shape[0]
    tile = lax.broadcasted_iota(jnp.int32, (shards * per_shard, shards), 0)
    start = per_shard * lax.broadcasted_iota(jnp.int32, (shards * per_shard, shards), 1)
    chosen = ((tile >= start) & (tile < start + per_shard)).astype(jnp.float32).astype(jnp.bfloat16)
    return jnp.dot(chosen, value, preferred_element_type=jnp.float32)


def regroup(arrived):
    sources = len(arrived)
    rows = arrived[0].shape[1]

    def kernel(*refs):
        in_refs, out_ref = refs[:sources], refs[sources]
        stats = [ref[64:72, :] for ref in in_refs]

        def common(at):
            tops = [s[at : at + 1] for s in stats]
            top = functools.reduce(jnp.maximum, tops)
            weights = [jnp.exp(t - top) for t in tops]
            total = sum(w * s[at + 1 : at + 2] for w, s in zip(weights, stats))
            rest = sum(w * s[at + 2 : at + 3] for w, s in zip(weights, stats))
            return weights, (top, total, rest)

        weights, teacher = common(0)
        _, student = common(3)
        line = lax.broadcasted_iota(jnp.int32, (8, rows), 0)
        sums = jnp.zeros((8, rows), jnp.float32)
        for at, value in enumerate(teacher + student):
            sums = jnp.where(line == at, value, sums)
        block = jnp.zeros((32, 8, rows), jnp.float32)
        for j in range(sources):
            for slot in range(2):
                e = in_refs[j][slot * 32 : (slot + 1) * 32, :] * weights[j]
                block = jnp.where((line == 2 * j + slot)[None], e[:, None, :], block)
        out_ref[:, :8, :] = block
        out_ref[:, 8:, :] = jnp.broadcast_to(sums[None], (32, 8, rows))

    return pl.pallas_call(
        kernel,
        out_shape=jax.ShapeDtypeStruct((32, 16, rows), jnp.float32),
        compiler_params=pltpu.CompilerParams(vmem_limit_bytes=LATE_LIMIT),
    )(*arrived)


def spread_sources(value, slot_ref, per_shard):
    sources = value.shape[0]
    tile = lax.broadcasted_iota(jnp.int32, (sources * per_shard, 1), 0)
    arrival = lax.broadcasted_iota(jnp.int32, (1, sources), 1)
    place, chip = (slot_ref[0] + 4 - (arrival >> 5)) & 3, arrival & 31
    shard = jnp.where(slot_ref[2] == 0, chip * 4 + place, (place * 8 + (chip & 7)) * 4 + (chip >> 3))
    chosen = (((tile * 205) >> 10) == shard).astype(jnp.float32).astype(jnp.bfloat16)
    return jnp.dot(chosen, value, preferred_element_type=jnp.float32)


def bring_near(head, pieces):
    def kernel(head_hbm, *refs):
        near_refs, sem = refs[:pieces], refs[pieces]
        copies = [
            pltpu.make_async_copy(head_hbm.at[pl.ds(k * DEPTH, DEPTH)], near_refs[k], sem.at[k])
            for k in range(pieces)
        ]
        for copy in copies:
            copy.start()
        for copy in copies:
            copy.wait()

    return pl.pallas_call(
        kernel,
        in_specs=[pl.BlockSpec(memory_space=pltpu.HBM)],
        out_specs=[pl.BlockSpec(memory_space=pltpu.VMEM)] * pieces,
        out_shape=[jax.ShapeDtypeStruct((DEPTH, head.shape[1]), head.dtype)] * pieces,
        scratch_shapes=[pltpu.SemaphoreType.DMA((pieces,))],
        cost_estimate=pl.CostEstimate(
            flops=2 * head.size * 512, bytes_accessed=2 * head.size, transcendentals=0
        ),
        compiler_params=pltpu.CompilerParams(vmem_limit_bytes=NEAR_LIMIT),
    )(head)


def gradient(slots, words, logit, arrived, order, pieces, student_cols, per_shard):
    cols, rows = logit.shape
    ds = student_cols.shape[0]
    count, width = len(pieces), pieces[0].shape[0]
    rest = ds - count * width
    block = rows // 4

    def kernel(slot_ref, word_ref, logit_ref, msg_ref, order_ref, *refs):
        near_w, w_hbm, out_refs = refs[:count], refs[count], refs[count + 1 : count + 5]
        kl_ref, near_ref, w_ref, w_sem = refs[count + 5 :]
        copies = fetch(w_hbm.at[pl.ds(count * width, rest)], width, w_ref, w_sem)

        def sums(at):
            top_each = msg_ref[:, at, :]
            top = jnp.max(top_each, axis=0, keepdims=True)
            weight = jnp.exp(top_each - top)
            total = jnp.sum(weight * msg_ref[:, at + 1, :], axis=0, keepdims=True)
            rest = jnp.sum(weight * msg_ref[:, at + 2, :], axis=0, keepdims=True)
            return top, weight, total, rest / total

        _, t_weight, t_total, t_mass = sums(8)
        s_top, _, s_total, s_mass = sums(11)
        scale = t_weight / t_total

        def arrived_prob(slot):
            parts = [msg_ref[:, 2 * j + slot, :] * scale for j in range(4)]
            prob = jnp.concatenate(parts, axis=0).astype(jnp.bfloat16)
            return spread_sources(prob, slot_ref, per_shard)

        named, is_first = expand_words(word_ref[...], per_shard)
        teacher = jnp.where(is_first, arrived_prob(0), arrived_prob(1))
        prob = jnp.exp(logit_ref[...] - s_top) * (1.0 / s_total)
        kl = (
            jnp.where(named, prob - teacher, prob * (1.0 - t_mass / s_mass)) * loss_scale
        ).astype(jnp.bfloat16)
        kl_ref[...] = lax.dot_general(
            order_ref[...], kl, (((1,), (1,)), ((), ())), preferred_element_type=jnp.float32
        ).astype(jnp.bfloat16)
        for n in range(4):
            at = pl.multiple_of(lax.rem(slot_ref[0] + n, 4) * block, block)
            near_ref[n * block : (n + 1) * block, :] = kl_ref[pl.ds(at, block), :]
        for k in range(ds // width):
            span = slice(k * width, (k + 1) * width)
            if k < count:
                piece = near_w[k][...]
            else:
                copies[k - count].wait()
                piece = w_ref[(k - count) * width : (k - count + 1) * width, :]
            term = lax.dot_general(
                near_ref[...],
                piece,
                (((1,), (1,)), ((), ())),
                preferred_element_type=jnp.float32,
            ).astype(jnp.bfloat16)
            for n in range(4):
                out_refs[n][:, span] = term[n * block : (n + 1) * block, :]

    whole = pl.BlockSpec(memory_space=pltpu.VMEM)
    return pl.pallas_call(
        kernel,
        in_specs=[pl.BlockSpec(memory_space=pltpu.SMEM)]
        + [whole] * (4 + count)
        + [pl.BlockSpec(memory_space=pltpu.HBM)],
        out_specs=[whole] * 4,
        out_shape=[jax.ShapeDtypeStruct((block, ds), jnp.bfloat16)] * 4,
        scratch_shapes=[
            pltpu.VMEM((rows, cols), jnp.bfloat16),
            pltpu.VMEM((rows, cols), jnp.bfloat16),
            pltpu.VMEM((rest, cols), jnp.bfloat16),
            pltpu.SemaphoreType.DMA((rest // width,)),
        ],
        compiler_params=pltpu.CompilerParams(vmem_limit_bytes=NEAR_LIMIT),
    )(slots, words, logit, arrived, order, *pieces, student_cols)


def per_device(teacher_hidden, teacher_head, student_hidden, student_head, tiles):
    shards = lax.axis_size(LINE)
    shard_index = lax.axis_index(LINE)
    core = lax.axis_index("mesh")
    ds, tiles_all, lane_count = student_head.shape
    student_cols = student_head.reshape(ds, tiles_all * lane_count)
    per_shard = tiles_all // shards
    picks = tiles.shape[1]

    both = jnp.concatenate((teacher_hidden, student_hidden), axis=1)
    mine = lax.dynamic_slice_in_dim(both, 2 * core, 2, 0)
    gathered = spread(mine, LINES_Z)
    by_chip = tiles.reshape(NY, NZ, NX, 2, 2, picks)
    by_chip = lax.dynamic_index_in_dim(by_chip, core, 3, keepdims=False)
    tiles_t = jnp.where(
        core == 0, by_chip.transpose(4, 2, 0, 1, 3), by_chip.transpose(4, 0, 2, 1, 3)
    ).reshape(picks, 2 * shards)
    words = tile_words(tiles_t)
    last, after, opposite = across(gathered, 1), across(gathered, -1), across(gathered, 2)
    opposite, words = lax.optimization_barrier((opposite, words))
    own = (
        jnp.concatenate((gathered, last), axis=0),
        jnp.concatenate((after, opposite), axis=0),
    )
    below_first = along(own[0], 1)
    above_first = along(own[1], -1)
    below_second = along(own[1], 1)
    above_second = along(own[0], -1)
    far = (along(below_first, 1), along(above_first, -1))
    early, *near_heads = early_logits(
        own + (above_first, below_first), teacher_head, student_cols
    )
    late = (above_second,) + far + (below_second,)
    own_word = lax.dynamic_slice_in_dim(words, shard_index, 1, 0)

    x, y = lax.axis_index("dp"), lax.axis_index("vocab") // NZ
    slots = jnp.stack((jnp.where(core == 0, x, y), jnp.where(core == 0, y, x), core))
    *message, logit = logits_and_message(
        slots, early, late, near_heads, words, own_word, per_shard
    )
    near = (
        message[0], along(message[1], 1), along(message[2], 2), along(message[3], -1),
    )
    joined, student_far = lax.optimization_barrier((regroup(near), student_cols))
    arrived = exchange(joined, PLANES_YZ + PLANES_XZ)
    student_near = bring_near(student_far, 2)

    order = lax.dynamic_index_in_dim(
        jnp.asarray(row_orders(), jnp.bfloat16), core, 0, keepdims=False
    )
    kept, after_chip, opposite_chip, last_chip = gradient(
        slots, words, logit, arrived, order, student_near, student_cols, per_shard
    )
    terms = (kept, along(opposite_chip, 2), along(after_chip, 1), along(last_chip, -1))
    near = sum(term.astype(jnp.float32) for term in terms)
    far = exchange(near.astype(jnp.bfloat16), PLANES_YZ + PLANES_XZ)
    summed = jnp.sum(far.reshape(NY * NZ, 2, ds).astype(jnp.float32), axis=0)
    return lax.ppermute(summed.astype(jnp.bfloat16), WHOLE, last_hop())


def solution(mesh):
    return jax.shard_map(
        per_device,
        mesh=mesh,
        in_specs=(
            P(("vocab", "dp"), None),
            P(None, ("vocab", "dp")),
            P(("vocab", "dp"), None),
            P(None, None, ("vocab", "dp")),
            P(),
        ),
        out_specs=P(("mesh", "vocab", "dp"), None),
        check_vma=False,
    )
```

```python
import functools

import jax
import jax.numpy as jnp
import numpy as np
from jax import lax
from jax.experimental import pallas as pl
from jax.experimental.pallas import tpu as pltpu
from jax.sharding import PartitionSpec as P

loss_scale = 1024.0
NX, NY, NZ = 4, 4, 8
LINE = ("vocab", "dp")
WHOLE = ("mesh", "vocab", "dp")
HALF = NX * NY * NZ


def device(m, x, y, z):
    return m * HALF + (y * NZ + z) * NX + x


LINES_Z = [
    [device(m, x, y, z) for z in range(NZ)]
    for m in range(2)
    for x in range(NX)
    for y in range(NY)
]
LINES_X = [
    [[device(m, x, y, z) for x in range(NX)] for y in range(NY) for z in range(NZ)]
    for m in range(2)
]
LINES_Y = [
    [[device(m, x, y, z) for y in range(NY)] for x in range(NX) for z in range(NZ)]
    for m in range(2)
]
PLANES_YZ = [
    [device(0, x, y, z) for y in range(NY) for z in range(NZ)] for x in range(NX)
]
PLANES_XZ = [
    [device(1, x, y, z) for x in range(NX) for z in range(NZ)] for y in range(NY)
]


def exchange(value, groups):
    return lax.all_to_all(value, WHOLE, 0, 0, tiled=True, axis_index_groups=groups)


def row_copies(core, teacher_hidden, student_hidden):
    dt, ds = teacher_hidden.shape[1], student_hidden.shape[1]

    def kernel(core_ref, t_ref, s_ref, out_ref):
        for ref, span in ((t_ref, slice(0, dt)), (s_ref, slice(dt, dt + ds))):
            rows = ref[...].astype(jnp.float32)
            rows = jnp.where(core_ref[0] == 0, rows[:2], rows[2:]).astype(jnp.bfloat16)
            for k in range(NZ):
                out_ref[k, :, span] = rows

    whole = pl.BlockSpec(memory_space=pltpu.VMEM)
    return pl.pallas_call(
        kernel,
        in_specs=[pl.BlockSpec(memory_space=pltpu.SMEM), whole, whole],
        out_specs=whole,
        out_shape=jax.ShapeDtypeStruct((NZ, 2, dt + ds), jnp.bfloat16),
    )(core, teacher_hidden, student_hidden)


def step(value, axes, by):
    sizes = {"x": NX, "y": NY}
    pairs = []
    for m in range(2):
        for x in range(NX):
            for y in range(NY):
                for z in range(NZ):
                    to = {"x": x, "y": y}
                    to[axes[m]] = (to[axes[m]] + by) % sizes[axes[m]]
                    pairs.append((device(m, x, y, z), device(m, to["x"], to["y"], z)))
    return lax.ppermute(value, WHOLE, pairs)


def across(value, by):
    return step(value, ("y", "x"), by)


def along(value, by):
    return step(value, ("x", "y"), by)


def home(x, y, z):
    x1, x0 = x // 2, x % 2
    y1, y0 = y // 2, y % 2
    z2, z1, z0 = z // 4, (z // 2) % 2, z % 2
    return 2 * x0 + y1, 2 * y0 + z2, 4 * z1 + 2 * z0 + x1


def row_orders():
    orders = np.zeros((2, 2 * HALF, 2 * HALF), np.float32)
    for x in range(NX):
        for y in range(NY):
            for z in range(NZ):
                hx, hy, hz = home(x, y, z)
                for b in range(2):
                    orders[0, ((hx * NY + hy) * NZ + hz) * 2 + b, ((x * NY + y) * NZ + z) * 2 + b] = 1
                    orders[1, ((hy * NX + hx) * NZ + hz) * 2 + b, ((y * NX + x) * NZ + z) * 2 + b] = 1
    return orders


def last_hop():
    pairs = []
    for m in range(2):
        for x in range(NX):
            for y in range(NY):
                for z in range(NZ):
                    pairs.append(
                        (device(m, x, y, z), device(x % 2, 2 * (x // 2) + m, y, z))
                    )
    return pairs


def tile_words(tiles_t):
    count, rows = tiles_t.shape

    def kernel(tiles_ref, word_ref):
        block = lax.broadcasted_iota(jnp.int32, (count, rows), 0)

        def step(k, word):
            tile = tiles_ref[pl.ds(k, 1), :]
            own = (tile * 205) >> 10
            bit = 1 << (tile - 5 * own)
            return word + jnp.where(block == own, bit, 0)

        word_ref[...] = lax.fori_loop(0, count, step, jnp.zeros((count, rows), jnp.int32), unroll=8)

    return pl.pallas_call(
        kernel,
        out_shape=jax.ShapeDtypeStruct((count, rows), jnp.int32),
        cost_estimate=pl.CostEstimate(
            flops=16 * count * count * rows, bytes_accessed=8 * count * rows, transcendentals=0
        ),
    )(tiles_t)


def fetch(source, chunk, buffer, semaphores):
    copies = []
    for k in range(source.shape[0] // chunk):
        rows = pl.ds(k * chunk, chunk)
        copies.append(pltpu.make_async_copy(source.at[rows], buffer.at[rows], semaphores.at[k]))
        copies[-1].start()
    return copies


DEPTH = 512
EARLY_LIMIT = 40 * 1024 * 1024
NEAR_LIMIT = 48 * 1024 * 1024
LATE_LIMIT = 16 * 1024 * 1024


def add_logits(half_refs, heads, out_ref, copies=None):
    at = 0
    for col, refs in heads:
        start = at
        for ref in refs:
            for k in range(ref.shape[0] // DEPTH):
                left = jnp.concatenate([half[:, at : at + DEPTH] for half in half_refs], axis=0)
                if copies is not None:
                    copies[at // DEPTH].wait()
                term = jnp.dot(
                    left, ref[k * DEPTH : (k + 1) * DEPTH, :], preferred_element_type=jnp.float32
                )
                if at == start:
                    out_ref[:, col] = term
                else:
                    out_ref[:, col] += term
                at += DEPTH


def logit_cost(rows, elements):
    return pl.CostEstimate(
        flops=2 * rows * elements, bytes_accessed=2 * elements, transcendentals=0
    )


def early_logits(halves, teacher_head, student_cols):
    count = len(halves)
    rows = count * halves[0].shape[0]
    cols = teacher_head.shape[1]

    half = teacher_head.shape[0] // 2

    def kernel(*refs):
        t_hbm, s_hbm, out_ref, t_low, t_high, s_ref, low_sem, high_sem, s_sem = refs[count:]
        copies = (
            fetch(t_hbm.at[pl.ds(0, half)], DEPTH, t_low, low_sem)
            + fetch(t_hbm.at[pl.ds(half, half)], DEPTH, t_high, high_sem)
            + fetch(s_hbm, DEPTH, s_ref, s_sem)
        )
        heads = ((slice(0, cols), (t_low, t_high)), (slice(cols, 2 * cols), (s_ref,)))
        add_logits(refs[:count], heads, out_ref, copies)

    whole = pl.BlockSpec(memory_space=pltpu.VMEM)
    low = jax.ShapeDtypeStruct((half, cols), teacher_head.dtype)
    return pl.pallas_call(
        kernel,
        in_specs=[whole] * count + [pl.BlockSpec(memory_space=pltpu.HBM)] * 2,
        out_specs=[whole] * 4,
        out_shape=[
            jax.ShapeDtypeStruct((rows, 2 * cols), jnp.float32),
            low,
            low,
            jax.ShapeDtypeStruct(student_cols.shape, student_cols.dtype),
        ],
        scratch_shapes=[
            pltpu.SemaphoreType.DMA((half // DEPTH,)),
            pltpu.SemaphoreType.DMA((half // DEPTH,)),
            pltpu.SemaphoreType.DMA((student_cols.shape[0] // DEPTH,)),
        ],
        cost_estimate=logit_cost(rows, teacher_head.size + student_cols.size),
        compiler_params=pltpu.CompilerParams(vmem_limit_bytes=EARLY_LIMIT),
    )(*halves, teacher_head, student_cols)


def logits_and_message(slots, early, halves, heads, words, own_word, per_shard):
    count = len(halves)
    half = halves[0].shape[0]
    rows = early.shape[0] + count * half
    block = half // 2
    cols = heads[0].shape[1]
    lanes = cols // per_shard
    elements = sum(head.size for head in heads)

    def kernel(slot_ref, early_ref, *refs):
        (
            word_ref, own_word_ref, t_low, t_high, s_ref, *msg_refs, logit_ref,
            late_ref, all_ref, spare_ref,
        ) = refs[count:]
        near = ((slice(0, cols), (t_low, t_high)), (slice(cols, 2 * cols), (s_ref,)))
        add_logits(refs[:count], near, late_ref)

        for source_ref, places in ((early_ref, (0, 1, 3, 6)), (late_ref, (2, 4, 5, 7))):
            for n, place in enumerate(places):
                for k in range(2):
                    third = lax.rem(slot_ref[0] + place // 2, 4)
                    second = lax.rem(slot_ref[1] + (0, 3, 1, 2)[2 * (place % 2) + k], 4)
                    at = pl.multiple_of((third * 4 + second) * block, block)
                    start = n * half + k * block
                    all_ref[pl.ds(at, block), :] = source_ref[start : start + block, :]

        word = own_word_ref[...]
        t_log = all_ref[:, :cols].T
        s_log = all_ref[:, cols:].T
        logit_ref[...] = s_log
        t_top = jnp.max(t_log, axis=0, keepdims=True)
        named_before = jnp.zeros((1, rows), jnp.int32)
        t_total = jnp.zeros((1, rows), jnp.float32)
        t_rest = jnp.zeros((1, rows), jnp.float32)
        first = jnp.zeros((lanes, rows), jnp.float32)
        second = jnp.zeros((lanes, rows), jnp.float32)
        for t in range(per_shard):
            e = jnp.exp(t_log[t * lanes : (t + 1) * lanes] - t_top)
            part = jnp.sum(e, axis=0, keepdims=True)
            named = (word >> t) & 1
            t_total += part
            t_rest += jnp.where(named == 0, part, 0.0)
            first = jnp.where((named == 1) & (named_before == 0), e, first)
            second = jnp.where((named == 1) & (named_before == 1), e, second)
            named_before += named
        named_s, _ = expand_words(word_ref[...], per_shard)
        s_top = jnp.max(s_log, axis=0, keepdims=True)
        e = jnp.exp(s_log - s_top)
        s_total = jnp.sum(e, axis=0, keepdims=True)
        s_rest = jnp.sum(jnp.where(named_s, 0.0, e), axis=0, keepdims=True)
        line = lax.broadcasted_iota(jnp.int32, (8, rows), 0)
        stats = jnp.zeros((8, rows), jnp.float32)
        for at, value in enumerate((t_top, t_total, t_rest, s_top, s_total, s_rest)):
            stats = jnp.where(line == at, value, stats)
        for part in range(rows // 128):
            spare_ref[part, :lanes, :] = first[:, part * 128 : (part + 1) * 128]
            spare_ref[part, lanes:, :] = second[:, part * 128 : (part + 1) * 128]
        for n in range(4):
            to = lax.rem(slot_ref[0] + n, 4)
            for r in range(4):
                x = jnp.where(slot_ref[2] == 0, to, r)
                y = jnp.where(slot_ref[2] == 0, r, to)
                for slot in range(2):
                    for part in range(rows // 128):
                        msg_refs[n][
                            slot * 32 + 8 * r : slot * 32 + 8 * r + 8, part * 128 : (part + 1) * 128
                        ] = spare_ref[part, pl.ds(slot * lanes + y * 32 + x, 8, stride=4), :]
            msg_refs[n][64:72, :] = stats

    whole = pl.BlockSpec(memory_space=pltpu.VMEM)
    return pl.pallas_call(
        kernel,
        in_specs=[pl.BlockSpec(memory_space=pltpu.SMEM)] + [whole] * (count + 6),
        out_specs=[whole] * 5,
        out_shape=[jax.ShapeDtypeStruct((72, rows), jnp.float32)] * 4
        + [jax.ShapeDtypeStruct((cols, rows), jnp.float32)],
        scratch_shapes=[
            pltpu.VMEM((count * half, 2 * cols), jnp.float32),
            pltpu.VMEM((rows, 2 * cols), jnp.float32),
            pltpu.VMEM((rows // 128, 2 * lanes, 128), jnp.float32),
        ],
        cost_estimate=logit_cost(count * half, elements),
        compiler_params=pltpu.CompilerParams(vmem_limit_bytes=LATE_LIMIT),
    )(slots, early, *halves, words, own_word, *heads)


def expand_words(words, per_shard):
    shards = words.shape[0]
    tile = lax.broadcasted_iota(jnp.int32, (shards * per_shard, 1), 0)
    within = tile - per_shard * ((tile * 205) >> 10)
    wide = spread_blocks(words.astype(jnp.bfloat16), per_shard).astype(jnp.int32)
    named = (wide >> within) & 1
    before = wide & ((1 << within) - 1)
    return named == 1, before == 0


def spread_blocks(value, per_shard):
    shards = value.shape[0]
    tile = lax.broadcasted_iota(jnp.int32, (shards * per_shard, shards), 0)
    start = per_shard * lax.broadcasted_iota(jnp.int32, (shards * per_shard, shards), 1)
    chosen = ((tile >= start) & (tile < start + per_shard)).astype(jnp.float32).astype(jnp.bfloat16)
    return jnp.dot(chosen, value, preferred_element_type=jnp.float32)


def regroup(arrived):
    sources = len(arrived)
    rows = arrived[0].shape[1]

    def kernel(*refs):
        in_refs, out_ref = refs[:sources], refs[sources]
        stats = [ref[64:72, :] for ref in in_refs]

        def common(at):
            tops = [s[at : at + 1] for s in stats]
            top = functools.reduce(jnp.maximum, tops)
            weights = [jnp.exp(t - top) for t in tops]
            total = sum(w * s[at + 1 : at + 2] for w, s in zip(weights, stats))
            rest = sum(w * s[at + 2 : at + 3] for w, s in zip(weights, stats))
            return weights, (top, total, rest)

        weights, teacher = common(0)
        _, student = common(3)
        line = lax.broadcasted_iota(jnp.int32, (8, rows), 0)
        sums = jnp.zeros((8, rows), jnp.float32)
        for at, value in enumerate(teacher + student):
            sums = jnp.where(line == at, value, sums)
        block = jnp.zeros((32, 8, rows), jnp.float32)
        for j in range(sources):
            for slot in range(2):
                e = in_refs[j][slot * 32 : (slot + 1) * 32, :] * weights[j]
                block = jnp.where((line == 2 * j + slot)[None], e[:, None, :], block)
        out_ref[:, :8, :] = block
        out_ref[:, 8:, :] = jnp.broadcast_to(sums[None], (32, 8, rows))

    return pl.pallas_call(
        kernel,
        out_shape=jax.ShapeDtypeStruct((32, 16, rows), jnp.float32),
        compiler_params=pltpu.CompilerParams(vmem_limit_bytes=LATE_LIMIT),
    )(*arrived)


def spread_sources(value, slot_ref, per_shard):
    sources = value.shape[0]
    tile = lax.broadcasted_iota(jnp.int32, (sources * per_shard, 1), 0)
    arrival = lax.broadcasted_iota(jnp.int32, (1, sources), 1)
    place, chip = (slot_ref[0] + 4 - (arrival >> 5)) & 3, arrival & 31
    shard = jnp.where(slot_ref[2] == 0, chip * 4 + place, (place * 8 + (chip & 7)) * 4 + (chip >> 3))
    chosen = (((tile * 205) >> 10) == shard).astype(jnp.float32).astype(jnp.bfloat16)
    return jnp.dot(chosen, value, preferred_element_type=jnp.float32)


def bring_near(head, pieces):
    def kernel(head_hbm, *refs):
        near_refs, sem = refs[:pieces], refs[pieces]
        copies = [
            pltpu.make_async_copy(head_hbm.at[pl.ds(k * DEPTH, DEPTH)], near_refs[k], sem.at[k])
            for k in range(pieces)
        ]
        for copy in copies:
            copy.start()
        for copy in copies:
            copy.wait()

    return pl.pallas_call(
        kernel,
        in_specs=[pl.BlockSpec(memory_space=pltpu.HBM)],
        out_specs=[pl.BlockSpec(memory_space=pltpu.VMEM)] * pieces,
        out_shape=[jax.ShapeDtypeStruct((DEPTH, head.shape[1]), head.dtype)] * pieces,
        scratch_shapes=[pltpu.SemaphoreType.DMA((pieces,))],
        cost_estimate=pl.CostEstimate(
            flops=2 * head.size * 512, bytes_accessed=2 * head.size, transcendentals=0
        ),
        compiler_params=pltpu.CompilerParams(vmem_limit_bytes=NEAR_LIMIT),
    )(head)


def gradient(slots, words, logit, arrived, order, pieces, student_cols, per_shard):
    cols, rows = logit.shape
    ds = student_cols.shape[0]
    count, width = len(pieces), pieces[0].shape[0]
    rest = ds - count * width
    block = rows // 4

    def kernel(slot_ref, word_ref, logit_ref, msg_ref, order_ref, *refs):
        near_w, w_hbm, out_refs = refs[:count], refs[count], refs[count + 1 : count + 5]
        kl_ref, near_ref, w_ref, w_sem = refs[count + 5 :]
        copies = fetch(w_hbm.at[pl.ds(count * width, rest)], width, w_ref, w_sem)

        def sums(at):
            top_each = msg_ref[:, at, :]
            top = jnp.max(top_each, axis=0, keepdims=True)
            weight = jnp.exp(top_each - top)
            total = jnp.sum(weight * msg_ref[:, at + 1, :], axis=0, keepdims=True)
            rest = jnp.sum(weight * msg_ref[:, at + 2, :], axis=0, keepdims=True)
            return top, weight, total, rest / total

        _, t_weight, t_total, t_mass = sums(8)
        s_top, _, s_total, s_mass = sums(11)
        scale = t_weight / t_total

        def arrived_prob(slot):
            parts = [msg_ref[:, 2 * j + slot, :] * scale for j in range(4)]
            prob = jnp.concatenate(parts, axis=0).astype(jnp.bfloat16)
            return spread_sources(prob, slot_ref, per_shard)

        named, is_first = expand_words(word_ref[...], per_shard)
        teacher = jnp.where(is_first, arrived_prob(0), arrived_prob(1))
        prob = jnp.exp(logit_ref[...] - s_top) * (1.0 / s_total)
        kl = (
            jnp.where(named, prob - teacher, prob * (1.0 - t_mass / s_mass)) * loss_scale
        ).astype(jnp.bfloat16)
        kl_ref[...] = lax.dot_general(
            order_ref[...], kl, (((1,), (1,)), ((), ())), preferred_element_type=jnp.float32
        ).astype(jnp.bfloat16)
        for n in range(4):
            at = pl.multiple_of(lax.rem(slot_ref[0] + n, 4) * block, block)
            near_ref[n * block : (n + 1) * block, :] = kl_ref[pl.ds(at, block), :]
        for k in range(ds // width):
            span = slice(k * width, (k + 1) * width)
            if k < count:
                piece = near_w[k][...]
            else:
                copies[k - count].wait()
                piece = w_ref[(k - count) * width : (k - count + 1) * width, :]
            term = lax.dot_general(
                near_ref[...],
                piece,
                (((1,), (1,)), ((), ())),
                preferred_element_type=jnp.float32,
            ).astype(jnp.bfloat16)
            for n in range(4):
                out_refs[n][:, span] = term[n * block : (n + 1) * block, :]

    whole = pl.BlockSpec(memory_space=pltpu.VMEM)
    return pl.pallas_call(
        kernel,
        in_specs=[pl.BlockSpec(memory_space=pltpu.SMEM)]
        + [whole] * (4 + count)
        + [pl.BlockSpec(memory_space=pltpu.HBM)],
        out_specs=[whole] * 4,
        out_shape=[jax.ShapeDtypeStruct((block, ds), jnp.bfloat16)] * 4,
        scratch_shapes=[
            pltpu.VMEM((rows, cols), jnp.bfloat16),
            pltpu.VMEM((rows, cols), jnp.bfloat16),
            pltpu.VMEM((rest, cols), jnp.bfloat16),
            pltpu.SemaphoreType.DMA((rest // width,)),
        ],
        compiler_params=pltpu.CompilerParams(vmem_limit_bytes=NEAR_LIMIT),
    )(slots, words, logit, arrived, order, *pieces, student_cols)


def per_device(teacher_hidden, teacher_head, student_hidden, student_head, tiles):
    shards = lax.axis_size(LINE)
    shard_index = lax.axis_index(LINE)
    core = lax.axis_index("mesh")
    ds, tiles_all, lane_count = student_head.shape
    student_cols = student_head.reshape(ds, tiles_all * lane_count)
    per_shard = tiles_all // shards
    picks = tiles.shape[1]

    copies = row_copies(core.reshape(1), teacher_hidden, student_hidden)
    gathered = exchange(copies.reshape(2 * NZ, copies.shape[2]), LINES_Z)

    by_chip = tiles.reshape(NY, NZ, NX, 2, 2, picks)
    by_chip = lax.dynamic_index_in_dim(by_chip, core, 3, keepdims=False)
    tiles_t = jnp.where(
        core == 0, by_chip.transpose(4, 2, 0, 1, 3), by_chip.transpose(4, 0, 2, 1, 3)
    ).reshape(picks, 2 * shards)
    words = tile_words(tiles_t)
    last, after, opposite = across(gathered, 1), across(gathered, -1), across(gathered, 2)
    opposite, words = lax.optimization_barrier((opposite, words))
    own = (
        jnp.concatenate((gathered, last), axis=0),
        jnp.concatenate((after, opposite), axis=0),
    )
    below_first = along(own[0], 1)
    above_first = along(own[1], -1)
    below_second = along(own[1], 1)
    above_second = along(own[0], -1)
    far = (along(below_first, 1), along(above_first, -1))
    early, *near_heads = early_logits(
        own + (above_first, below_first), teacher_head, student_cols
    )
    late = (above_second,) + far + (below_second,)
    own_word = lax.dynamic_slice_in_dim(words, shard_index, 1, 0)

    x, y = lax.axis_index("dp"), lax.axis_index("vocab") // NZ
    slots = jnp.stack((jnp.where(core == 0, x, y), jnp.where(core == 0, y, x), core))
    *message, logit = logits_and_message(
        slots, early, late, near_heads, words, own_word, per_shard
    )
    near = (
        message[0], along(message[1], 1), along(message[2], 2), along(message[3], -1),
    )
    joined, student_far = lax.optimization_barrier((regroup(near), student_cols))
    arrived = exchange(joined, PLANES_YZ + PLANES_XZ)
    student_near = bring_near(student_far, 2)

    order = lax.dynamic_index_in_dim(
        jnp.asarray(row_orders(), jnp.bfloat16), core, 0, keepdims=False
    )
    kept, after_chip, opposite_chip, last_chip = gradient(
        slots, words, logit, arrived, order, student_near, student_cols, per_shard
    )
    terms = (kept, along(opposite_chip, 2), along(after_chip, 1), along(last_chip, -1))
    near = sum(term.astype(jnp.float32) for term in terms)
    far = exchange(near.astype(jnp.bfloat16), PLANES_YZ + PLANES_XZ)
    summed = jnp.sum(far.reshape(NY * NZ, 2, ds).astype(jnp.float32), axis=0)
    return lax.ppermute(summed.astype(jnp.bfloat16), WHOLE, last_hop())


def solution(mesh):
    return jax.shard_map(
        per_device,
        mesh=mesh,
        in_specs=(
            P(("vocab", "dp"), None),
            P(None, ("vocab", "dp")),
            P(("vocab", "dp"), None),
            P(None, None, ("vocab", "dp")),
            P(),
        ),
        out_specs=P(("mesh", "vocab", "dp"), None),
        check_vma=False,
    )
```

```python
import functools

import jax
import jax.numpy as jnp
import numpy as np
from jax import lax
from jax.experimental import pallas as pl
from jax.experimental.pallas import tpu as pltpu
from jax.sharding import PartitionSpec as P

loss_scale = 1024.0
NX, NY, NZ = 4, 4, 8
LINE = ("vocab", "dp")
WHOLE = ("mesh", "vocab", "dp")
HALF = NX * NY * NZ


def device(m, x, y, z):
    return m * HALF + (y * NZ + z) * NX + x


LINES_Z = [
    [device(m, x, y, z) for z in range(NZ)]
    for m in range(2)
    for x in range(NX)
    for y in range(NY)
]
LINES_X = [
    [[device(m, x, y, z) for x in range(NX)] for y in range(NY) for z in range(NZ)]
    for m in range(2)
]
LINES_Y = [
    [[device(m, x, y, z) for y in range(NY)] for x in range(NX) for z in range(NZ)]
    for m in range(2)
]
PLANES_YZ = [
    [device(0, x, y, z) for y in range(NY) for z in range(NZ)] for x in range(NX)
]
PLANES_XZ = [
    [device(1, x, y, z) for x in range(NX) for z in range(NZ)] for y in range(NY)
]


def exchange(value, groups):
    return lax.all_to_all(value, WHOLE, 0, 0, tiled=True, axis_index_groups=groups)


def row_copies(core, teacher_hidden, student_hidden):
    dt, ds = teacher_hidden.shape[1], student_hidden.shape[1]

    def kernel(core_ref, t_ref, s_ref, out_ref):
        for ref, span in ((t_ref, slice(0, dt)), (s_ref, slice(dt, dt + ds))):
            rows = ref[...].astype(jnp.float32)
            rows = jnp.where(core_ref[0] == 0, rows[:2], rows[2:]).astype(jnp.bfloat16)
            for k in range(NZ):
                out_ref[k, :, span] = rows

    whole = pl.BlockSpec(memory_space=pltpu.VMEM)
    return pl.pallas_call(
        kernel,
        in_specs=[pl.BlockSpec(memory_space=pltpu.SMEM), whole, whole],
        out_specs=whole,
        out_shape=jax.ShapeDtypeStruct((NZ, 2, dt + ds), jnp.bfloat16),
    )(core, teacher_hidden, student_hidden)


def step(value, axes, by):
    sizes = {"x": NX, "y": NY}
    pairs = []
    for m in range(2):
        for x in range(NX):
            for y in range(NY):
                for z in range(NZ):
                    to = {"x": x, "y": y}
                    to[axes[m]] = (to[axes[m]] + by) % sizes[axes[m]]
                    pairs.append((device(m, x, y, z), device(m, to["x"], to["y"], z)))
    return lax.ppermute(value, WHOLE, pairs)


def across(value, by):
    return step(value, ("y", "x"), by)


def along(value, by):
    return step(value, ("x", "y"), by)


def home(x, y, z):
    x1, x0 = x // 2, x % 2
    y1, y0 = y // 2, y % 2
    z2, z1, z0 = z // 4, (z // 2) % 2, z % 2
    return 2 * x0 + y1, 2 * y0 + z2, 4 * z1 + 2 * z0 + x1


def row_orders():
    orders = np.zeros((2, 2 * HALF, 2 * HALF), np.float32)
    for x in range(NX):
        for y in range(NY):
            for z in range(NZ):
                hx, hy, hz = home(x, y, z)
                for b in range(2):
                    orders[0, ((hx * NY + hy) * NZ + hz) * 2 + b, ((x * NY + y) * NZ + z) * 2 + b] = 1
                    orders[1, ((hy * NX + hx) * NZ + hz) * 2 + b, ((y * NX + x) * NZ + z) * 2 + b] = 1
    return orders


def last_hop():
    pairs = []
    for m in range(2):
        for x in range(NX):
            for y in range(NY):
                for z in range(NZ):
                    pairs.append(
                        (device(m, x, y, z), device(x % 2, 2 * (x // 2) + m, y, z))
                    )
    return pairs


def tile_words(tiles_t):
    count, rows = tiles_t.shape

    def kernel(tiles_ref, word_ref):
        block = lax.broadcasted_iota(jnp.int32, (count, rows), 0)

        def step(k, word):
            tile = tiles_ref[pl.ds(k, 1), :]
            own = (tile * 205) >> 10
            bit = 1 << (tile - 5 * own)
            return word + jnp.where(block == own, bit, 0)

        word_ref[...] = lax.fori_loop(0, count, step, jnp.zeros((count, rows), jnp.int32), unroll=8)

    return pl.pallas_call(
        kernel,
        out_shape=jax.ShapeDtypeStruct((count, rows), jnp.int32),
        cost_estimate=pl.CostEstimate(
            flops=16 * count * count * rows, bytes_accessed=8 * count * rows, transcendentals=0
        ),
    )(tiles_t)


def fetch(source, chunk, buffer, semaphores):
    copies = []
    for k in range(source.shape[0] // chunk):
        rows = pl.ds(k * chunk, chunk)
        copies.append(pltpu.make_async_copy(source.at[rows], buffer.at[rows], semaphores.at[k]))
        copies[-1].start()
    return copies


DEPTH = 512
EARLY_LIMIT = 40 * 1024 * 1024
NEAR_LIMIT = 48 * 1024 * 1024
LATE_LIMIT = 16 * 1024 * 1024


def add_logits(half_refs, heads, out_ref, copies=None):
    at = 0
    for col, refs in heads:
        start = at
        for ref in refs:
            for k in range(ref.shape[0] // DEPTH):
                left = jnp.concatenate([half[:, at : at + DEPTH] for half in half_refs], axis=0)
                if copies is not None:
                    copies[at // DEPTH].wait()
                term = jnp.dot(
                    left, ref[k * DEPTH : (k + 1) * DEPTH, :], preferred_element_type=jnp.float32
                )
                if at == start:
                    out_ref[:, col] = term
                else:
                    out_ref[:, col] += term
                at += DEPTH


def logit_cost(rows, elements):
    return pl.CostEstimate(
        flops=2 * rows * elements, bytes_accessed=2 * elements, transcendentals=0
    )


def early_logits(halves, teacher_head, student_cols):
    count = len(halves)
    rows = count * halves[0].shape[0]
    cols = teacher_head.shape[1]

    half = teacher_head.shape[0] // 2

    def kernel(*refs):
        t_hbm, s_hbm, out_ref, t_low, t_high, s_ref, low_sem, high_sem, s_sem = refs[count:]
        copies = (
            fetch(t_hbm.at[pl.ds(0, half)], DEPTH, t_low, low_sem)
            + fetch(t_hbm.at[pl.ds(half, half)], DEPTH, t_high, high_sem)
            + fetch(s_hbm, DEPTH, s_ref, s_sem)
        )
        heads = ((slice(0, cols), (t_low, t_high)), (slice(cols, 2 * cols), (s_ref,)))
        add_logits(refs[:count], heads, out_ref, copies)

    whole = pl.BlockSpec(memory_space=pltpu.VMEM)
    low = jax.ShapeDtypeStruct((half, cols), teacher_head.dtype)
    return pl.pallas_call(
        kernel,
        in_specs=[whole] * count + [pl.BlockSpec(memory_space=pltpu.HBM)] * 2,
        out_specs=[whole] * 4,
        out_shape=[
            jax.ShapeDtypeStruct((rows, 2 * cols), jnp.float32),
            low,
            low,
            jax.ShapeDtypeStruct(student_cols.shape, student_cols.dtype),
        ],
        scratch_shapes=[
            pltpu.SemaphoreType.DMA((half // DEPTH,)),
            pltpu.SemaphoreType.DMA((half // DEPTH,)),
            pltpu.SemaphoreType.DMA((student_cols.shape[0] // DEPTH,)),
        ],
        cost_estimate=logit_cost(rows, teacher_head.size + student_cols.size),
        compiler_params=pltpu.CompilerParams(vmem_limit_bytes=EARLY_LIMIT),
    )(*halves, teacher_head, student_cols)


def logits_and_message(slots, early, halves, heads, words, own_word, per_shard):
    count = len(halves)
    half = halves[0].shape[0]
    rows = early.shape[0] + count * half
    block = half // 2
    cols = heads[0].shape[1]
    lanes = cols // per_shard
    elements = sum(head.size for head in heads)

    def kernel(slot_ref, early_ref, *refs):
        (
            word_ref, own_word_ref, t_low, t_high, s_ref, *msg_refs, logit_ref,
            late_ref, all_ref, spare_ref,
        ) = refs[count:]
        near = ((slice(0, cols), (t_low, t_high)), (slice(cols, 2 * cols), (s_ref,)))
        add_logits(refs[:count], near, late_ref)

        for source_ref, places in ((early_ref, (0, 1, 3, 6)), (late_ref, (2, 4, 5, 7))):
            for n, place in enumerate(places):
                for k in range(2):
                    third = lax.rem(slot_ref[0] + place // 2, 4)
                    second = lax.rem(slot_ref[1] + (0, 3, 1, 2)[2 * (place % 2) + k], 4)
                    at = pl.multiple_of((third * 4 + second) * block, block)
                    start = n * half + k * block
                    all_ref[pl.ds(at, block), :] = source_ref[start : start + block, :]

        word = own_word_ref[...]
        t_log = all_ref[:, :cols].T
        s_log = all_ref[:, cols:].T
        logit_ref[...] = s_log
        t_top = jnp.max(t_log, axis=0, keepdims=True)
        named_before = jnp.zeros((1, rows), jnp.int32)
        t_total = jnp.zeros((1, rows), jnp.float32)
        t_rest = jnp.zeros((1, rows), jnp.float32)
        first = jnp.zeros((lanes, rows), jnp.float32)
        second = jnp.zeros((lanes, rows), jnp.float32)
        for t in range(per_shard):
            e = jnp.exp(t_log[t * lanes : (t + 1) * lanes] - t_top)
            part = jnp.sum(e, axis=0, keepdims=True)
            named = (word >> t) & 1
            t_total += part
            t_rest += jnp.where(named == 0, part, 0.0)
            first = jnp.where((named == 1) & (named_before == 0), e, first)
            second = jnp.where((named == 1) & (named_before == 1), e, second)
            named_before += named
        named_s, _ = expand_words(word_ref[...], per_shard)
        s_top = jnp.max(s_log, axis=0, keepdims=True)
        e = jnp.exp(s_log - s_top)
        s_total = jnp.sum(e, axis=0, keepdims=True)
        s_rest = jnp.sum(jnp.where(named_s, 0.0, e), axis=0, keepdims=True)
        line = lax.broadcasted_iota(jnp.int32, (8, rows), 0)
        stats = jnp.zeros((8, rows), jnp.float32)
        for at, value in enumerate((t_top, t_total, t_rest, s_top, s_total, s_rest)):
            stats = jnp.where(line == at, value, stats)
        for part in range(rows // 128):
            spare_ref[part, :lanes, :] = first[:, part * 128 : (part + 1) * 128]
            spare_ref[part, lanes:, :] = second[:, part * 128 : (part + 1) * 128]
        for n in range(4):
            to = lax.rem(slot_ref[0] + n, 4)
            for r in range(4):
                x = jnp.where(slot_ref[2] == 0, to, r)
                y = jnp.where(slot_ref[2] == 0, r, to)
                for slot in range(2):
                    for part in range(rows // 128):
                        msg_refs[n][
                            slot * 32 + 8 * r : slot * 32 + 8 * r + 8, part * 128 : (part + 1) * 128
                        ] = spare_ref[part, pl.ds(slot * lanes + y * 32 + x, 8, stride=4), :]
            msg_refs[n][64:72, :] = stats

    whole = pl.BlockSpec(memory_space=pltpu.VMEM)
    return pl.pallas_call(
        kernel,
        in_specs=[pl.BlockSpec(memory_space=pltpu.SMEM)] + [whole] * (count + 6),
        out_specs=[whole] * 5,
        out_shape=[jax.ShapeDtypeStruct((72, rows), jnp.float32)] * 4
        + [jax.ShapeDtypeStruct((cols, rows), jnp.float32)],
        scratch_shapes=[
            pltpu.VMEM((count * half, 2 * cols), jnp.float32),
            pltpu.VMEM((rows, 2 * cols), jnp.float32),
            pltpu.VMEM((rows // 128, 2 * lanes, 128), jnp.float32),
        ],
        cost_estimate=logit_cost(count * half, elements),
        compiler_params=pltpu.CompilerParams(vmem_limit_bytes=LATE_LIMIT),
    )(slots, early, *halves, words, own_word, *heads)


def expand_words(words, per_shard):
    shards = words.shape[0]
    tile = lax.broadcasted_iota(jnp.int32, (shards * per_shard, 1), 0)
    within = tile - per_shard * ((tile * 205) >> 10)
    wide = spread_blocks(words.astype(jnp.bfloat16), per_shard).astype(jnp.int32)
    named = (wide >> within) & 1
    before = wide & ((1 << within) - 1)
    return named == 1, before == 0


def spread_blocks(value, per_shard):
    shards = value.shape[0]
    tile = lax.broadcasted_iota(jnp.int32, (shards * per_shard, shards), 0)
    start = per_shard * lax.broadcasted_iota(jnp.int32, (shards * per_shard, shards), 1)
    chosen = ((tile >= start) & (tile < start + per_shard)).astype(jnp.float32).astype(jnp.bfloat16)
    return jnp.dot(chosen, value, preferred_element_type=jnp.float32)


def regroup(arrived):
    sources = len(arrived)
    rows = arrived[0].shape[1]

    def kernel(*refs):
        in_refs, out_ref = refs[:sources], refs[sources]
        stats = [ref[64:72, :] for ref in in_refs]

        def common(at):
            tops = [s[at : at + 1] for s in stats]
            top = functools.reduce(jnp.maximum, tops)
            weights = [jnp.exp(t - top) for t in tops]
            total = sum(w * s[at + 1 : at + 2] for w, s in zip(weights, stats))
            rest = sum(w * s[at + 2 : at + 3] for w, s in zip(weights, stats))
            return weights, (top, total, rest)

        weights, teacher = common(0)
        _, student = common(3)
        line = lax.broadcasted_iota(jnp.int32, (8, rows), 0)
        sums = jnp.zeros((8, rows), jnp.float32)
        for at, value in enumerate(teacher + student):
            sums = jnp.where(line == at, value, sums)
        block = jnp.zeros((32, 8, rows), jnp.float32)
        for j in range(sources):
            for slot in range(2):
                e = in_refs[j][slot * 32 : (slot + 1) * 32, :] * weights[j]
                block = jnp.where((line == 2 * j + slot)[None], e[:, None, :], block)
        out_ref[:, :8, :] = block
        out_ref[:, 8:, :] = jnp.broadcast_to(sums[None], (32, 8, rows))

    return pl.pallas_call(
        kernel,
        out_shape=jax.ShapeDtypeStruct((32, 16, rows), jnp.float32),
        compiler_params=pltpu.CompilerParams(vmem_limit_bytes=LATE_LIMIT),
    )(*arrived)


def spread_sources(value, slot_ref, per_shard):
    sources = value.shape[0]
    tile = lax.broadcasted_iota(jnp.int32, (sources * per_shard, 1), 0)
    arrival = lax.broadcasted_iota(jnp.int32, (1, sources), 1)
    place, chip = (slot_ref[0] + 4 - (arrival >> 5)) & 3, arrival & 31
    shard = jnp.where(slot_ref[2] == 0, chip * 4 + place, (place * 8 + (chip & 7)) * 4 + (chip >> 3))
    chosen = (((tile * 205) >> 10) == shard).astype(jnp.float32).astype(jnp.bfloat16)
    return jnp.dot(chosen, value, preferred_element_type=jnp.float32)


def bring_near(head, pieces):
    def kernel(head_hbm, *refs):
        near_refs, sem = refs[:pieces], refs[pieces]
        copies = [
            pltpu.make_async_copy(head_hbm.at[pl.ds(k * DEPTH, DEPTH)], near_refs[k], sem.at[k])
            for k in range(pieces)
        ]
        for copy in copies:
            copy.start()
        for copy in copies:
            copy.wait()

    return pl.pallas_call(
        kernel,
        in_specs=[pl.BlockSpec(memory_space=pltpu.HBM)],
        out_specs=[pl.BlockSpec(memory_space=pltpu.VMEM)] * pieces,
        out_shape=[jax.ShapeDtypeStruct((DEPTH, head.shape[1]), head.dtype)] * pieces,
        scratch_shapes=[pltpu.SemaphoreType.DMA((pieces,))],
        cost_estimate=pl.CostEstimate(
            flops=2 * head.size * 512, bytes_accessed=2 * head.size, transcendentals=0
        ),
        compiler_params=pltpu.CompilerParams(vmem_limit_bytes=NEAR_LIMIT),
    )(head)


def gradient(slots, words, logit, arrived, order, pieces, student_cols, per_shard):
    cols, rows = logit.shape
    ds = student_cols.shape[0]
    count, width = len(pieces), pieces[0].shape[0]
    rest = ds - count * width
    block = rows // 4

    def kernel(slot_ref, word_ref, logit_ref, msg_ref, order_ref, *refs):
        near_w, w_hbm, out_refs = refs[:count], refs[count], refs[count + 1 : count + 5]
        kl_ref, near_ref, w_ref, w_sem = refs[count + 5 :]
        copies = fetch(w_hbm.at[pl.ds(count * width, rest)], width, w_ref, w_sem)

        def sums(at):
            top_each = msg_ref[:, at, :]
            top = jnp.max(top_each, axis=0, keepdims=True)
            weight = jnp.exp(top_each - top)
            total = jnp.sum(weight * msg_ref[:, at + 1, :], axis=0, keepdims=True)
            rest = jnp.sum(weight * msg_ref[:, at + 2, :], axis=0, keepdims=True)
            return top, weight, total, rest / total

        _, t_weight, t_total, t_mass = sums(8)
        s_top, _, s_total, s_mass = sums(11)
        scale = t_weight / t_total

        def arrived_prob(slot):
            parts = [msg_ref[:, 2 * j + slot, :] * scale for j in range(4)]
            prob = jnp.concatenate(parts, axis=0).astype(jnp.bfloat16)
            return spread_sources(prob, slot_ref, per_shard)

        named, is_first = expand_words(word_ref[...], per_shard)
        teacher = jnp.where(is_first, arrived_prob(0), arrived_prob(1))
        prob = jnp.exp(logit_ref[...] - s_top) * (1.0 / s_total)
        kl = (
            jnp.where(named, prob - teacher, prob * (1.0 - t_mass / s_mass)) * loss_scale
        ).astype(jnp.bfloat16)
        kl_ref[...] = lax.dot_general(
            order_ref[...], kl, (((1,), (1,)), ((), ())), preferred_element_type=jnp.float32
        ).astype(jnp.bfloat16)
        for n in range(4):
            at = pl.multiple_of(lax.rem(slot_ref[0] + n, 4) * block, block)
            near_ref[n * block : (n + 1) * block, :] = kl_ref[pl.ds(at, block), :]
        for k in range(ds // width):
            span = slice(k * width, (k + 1) * width)
            if k < count:
                piece = near_w[k][...]
            else:
                copies[k - count].wait()
                piece = w_ref[(k - count) * width : (k - count + 1) * width, :]
            term = lax.dot_general(
                near_ref[...],
                piece,
                (((1,), (1,)), ((), ())),
                preferred_element_type=jnp.float32,
            ).astype(jnp.bfloat16)
            for n in range(4):
                out_refs[n][:, span] = term[n * block : (n + 1) * block, :]

    whole = pl.BlockSpec(memory_space=pltpu.VMEM)
    return pl.pallas_call(
        kernel,
        in_specs=[pl.BlockSpec(memory_space=pltpu.SMEM)]
        + [whole] * (4 + count)
        + [pl.BlockSpec(memory_space=pltpu.HBM)],
        out_specs=[whole] * 4,
        out_shape=[jax.ShapeDtypeStruct((block, ds), jnp.bfloat16)] * 4,
        scratch_shapes=[
            pltpu.VMEM((rows, cols), jnp.bfloat16),
            pltpu.VMEM((rows, cols), jnp.bfloat16),
            pltpu.VMEM((rest, cols), jnp.bfloat16),
            pltpu.SemaphoreType.DMA((rest // width,)),
        ],
        compiler_params=pltpu.CompilerParams(vmem_limit_bytes=NEAR_LIMIT),
    )(slots, words, logit, arrived, order, *pieces, student_cols)


def per_device(teacher_hidden, teacher_head, student_hidden, student_head, tiles):
    shards = lax.axis_size(LINE)
    shard_index = lax.axis_index(LINE)
    core = lax.axis_index("mesh")
    ds, tiles_all, lane_count = student_head.shape
    student_cols = student_head.reshape(ds, tiles_all * lane_count)
    per_shard = tiles_all // shards
    picks = tiles.shape[1]

    copies = row_copies(core.reshape(1), teacher_hidden, student_hidden)
    gathered = exchange(copies.reshape(2 * NZ, copies.shape[2]), LINES_Z)

    by_chip = tiles.reshape(NY, NZ, NX, 2, 2, picks)
    by_chip = lax.dynamic_index_in_dim(by_chip, core, 3, keepdims=False)
    tiles_t = jnp.where(
        core == 0, by_chip.transpose(4, 2, 0, 1, 3), by_chip.transpose(4, 0, 2, 1, 3)
    ).reshape(picks, 2 * shards)
    words = tile_words(tiles_t)
    last, after, opposite = across(gathered, 1), across(gathered, -1), across(gathered, 2)
    gathered, words = lax.optimization_barrier((gathered, words))
    own = (
        jnp.concatenate((gathered, last), axis=0),
        jnp.concatenate((after, opposite), axis=0),
    )
    below_first = along(own[0], 1)
    above_first = along(own[1], -1)
    below_second = along(own[1], 1)
    above_second = along(own[0], -1)
    far = (along(below_first, 1), along(above_first, -1))
    early, *near_heads = early_logits(
        own + (above_first, below_first), teacher_head, student_cols
    )
    late = (above_second,) + far + (below_second,)
    own_word = lax.dynamic_slice_in_dim(words, shard_index, 1, 0)

    x, y = lax.axis_index("dp"), lax.axis_index("vocab") // NZ
    slots = jnp.stack((jnp.where(core == 0, x, y), jnp.where(core == 0, y, x), core))
    *message, logit = logits_and_message(
        slots, early, late, near_heads, words, own_word, per_shard
    )
    near = (
        message[0], along(message[1], 1), along(message[2], 2), along(message[3], -1),
    )
    joined, student_far = lax.optimization_barrier((regroup(near), student_cols))
    arrived = exchange(joined, PLANES_YZ + PLANES_XZ)
    student_near = bring_near(student_far, 2)

    order = lax.dynamic_index_in_dim(
        jnp.asarray(row_orders(), jnp.bfloat16), core, 0, keepdims=False
    )
    kept, after_chip, opposite_chip, last_chip = gradient(
        slots, words, logit, arrived, order, student_near, student_cols, per_shard
    )
    terms = (kept, along(opposite_chip, 2), along(after_chip, 1), along(last_chip, -1))
    near = sum(term.astype(jnp.float32) for term in terms)
    far = exchange(near.astype(jnp.bfloat16), PLANES_YZ + PLANES_XZ)
    summed = jnp.sum(far.reshape(NY * NZ, 2, ds).astype(jnp.float32), axis=0)
    return lax.ppermute(summed.astype(jnp.bfloat16), WHOLE, last_hop())


def solution(mesh):
    return jax.shard_map(
        per_device,
        mesh=mesh,
        in_specs=(
            P(("vocab", "dp"), None),
            P(None, ("vocab", "dp")),
            P(("vocab", "dp"), None),
            P(None, None, ("vocab", "dp")),
            P(),
        ),
        out_specs=P(("mesh", "vocab", "dp"), None),
        check_vma=False,
    )
```
